128 devices in a mesh: lat: 8 (over y_hi, x), lon: 16 (over y_lo, z, core).
Axes of the slice: x: 4, y: 4 (y_hi: 2, y_lo: 2; y = y_hi * 2 + y_lo), z: 4, core: 2. Of those that a mesh axis runs over, the one named last changes fastest.
Arguments:
- field: bfloat16 [8, 96, 384, 192], P(None, 'lat', 'lon'), may hold values from -6 to 6
- a_norm_one: float32 [192], replicated, may hold values from 0.1 to 1.9
- a_project: bfloat16 [192, 576], replicated, may hold values from -0.4375 to 0.4375
- a_bias: float32 [6, 144, 144], replicated, may hold values from -4 to 240
- a_output: bfloat16 [192, 192], replicated, may hold values from -0.4375 to 0.4375
- a_norm_two: float32 [192], replicated, may hold values from 0.1 to 1.9
- a_raise: bfloat16 [192, 768], replicated, may hold values from -0.4375 to 0.4375
- a_lower: bfloat16 [768, 192], replicated, may hold values from -0.21875 to 0.21875
- merge_norm_gain: float32 [768], replicated, may hold values from 0.1 to 1.9
- merge_weight: bfloat16 [768, 384], replicated, may hold values from -0.21875 to 0.21875
- b_norm_one: float32 [384], replicated, may hold values from 0.1 to 1.9
- b_project: bfloat16 [384, 1152], replicated, may hold values from -0.3125 to 0.3125
- b_bias: float32 [12, 144, 144], replicated, may hold values from -4 to 240
- b_output: bfloat16 [384, 384], replicated, may hold values from -0.3125 to 0.3125
- b_norm_two: float32 [384], replicated, may hold values from 0.1 to 1.9
- b_raise: bfloat16 [384, 1536], replicated, may hold values from -0.3125 to 0.3125
- b_lower: bfloat16 [1536, 384], replicated, may hold values from -0.15625 to 0.15625
- up_first: bfloat16 [384, 768], replicated, may hold values from -0.3125 to 0.3125
- up_norm: float32 [192], replicated, may hold values from 0.1 to 1.9
- up_second: bfloat16 [192, 192], replicated, may hold values from -0.4375 to 0.4375
Outputs:
- fine: bfloat16 [8, 96, 384, 192], P(None, 'lat', 'lon')
The draws below stay inside these ranges and needn't reach their ends.
All inputs are finite; a program needn't handle non-finite values.
Results may differ from the reference program's by a relative error of at most 0.023.
Values may be sent and summed in bfloat16 or wider, within the bound.
No kernel may reach another device: no remote copies, remote signals or barrier semaphores. Data moves between devices by JAX's collectives and lax.ppermute only.
A program may use at most 192 MiB of HBM per device.

```python
import math
import jax
import jax.numpy as jnp
from jax import lax

P_SIZE = 8
C = 192
WIN_P = 2
WIN_LAT = 6
WIN_LON = 12
WIN = 144
C2 = 384
HEADS = 6
HEADS2 = 12
FF = 768
FF2 = 1536
LAT = 96
LON = 384


def draw_a_bias(key, part):
    key = jax.random.fold_in(key, 11)
    return jax.random.truncated_normal(key, -4.0, 4.0, (HEADS, WIN, WIN), jnp.float32)


def draw_b_bias(key, part):
    key = jax.random.fold_in(key, 12)
    return jax.random.truncated_normal(key, -4.0, 4.0, (HEADS2, WIN, WIN), jnp.float32)


def level_of(key, shape, pieces, smallest, largest):
    level = 1.0
    for dim, blocks in pieces:
        draws = jax.random.uniform(jax.random.fold_in(jax.random.fold_in(key, 6), dim), (blocks,), jnp.float32, smallest / len(pieces), largest / len(pieces))
        level = level * jnp.repeat(jnp.exp(draws), shape[dim] // blocks).reshape((-1,) + (1,) * (len(shape) - 1 - dim))
    return level


def gaussian(rng, extent, spread, bound, cuts=(), kind=jnp.bfloat16):
    values = spread * jax.random.normal(rng, extent, jnp.float32)
    if cuts:
        values = values * level_of(rng, extent, cuts, -0.22, 0.18)
    return jnp.clip(values, -bound, bound).astype(kind)


def setup_inputs(seed: int = 0) -> dict:
    splits = jax.random.split(jax.random.key(seed), 21)
    field = gaussian(splits[0], (P_SIZE, LAT, LON, C), 1.0, 6.0, ((1, 8), (2, 16)))
    a_norm_one = jnp.clip(1.0 + 0.18 * jax.random.normal(splits[1], (C,), jnp.float32), 0.1, 1.9)
    a_project = gaussian(splits[2], (C, 3 * C), C ** -0.5, 0.4375)
    a_bias = draw_a_bias(jax.random.fold_in(splits[20], 71), 0)
    a_output = gaussian(splits[4], (C, C), C ** -0.5, 0.4375)
    a_norm_two = jnp.clip(1.0 + 0.18 * jax.random.normal(splits[5], (C,), jnp.float32), 0.1, 1.9)
    a_raise = gaussian(splits[6], (C, FF), C ** -0.5, 0.4375)
    a_lower = gaussian(splits[7], (FF, C), FF ** -0.5, 0.21875)
    merge_norm_gain = jnp.clip(1.0 + 0.18 * jax.random.normal(splits[8], (4 * C,), jnp.float32), 0.1, 1.9)
    merge_weight = gaussian(splits[9], (4 * C, C2), (4 * C) ** -0.5, 0.21875)
    b_norm_one = jnp.clip(1.0 + 0.18 * jax.random.normal(splits[10], (C2,), jnp.float32), 0.1, 1.9)
    b_project = gaussian(splits[11], (C2, 3 * C2), C2 ** -0.5, 0.3125)
    b_bias = draw_b_bias(jax.random.fold_in(splits[20], 71), 0)
    b_output = gaussian(splits[13], (C2, C2), C2 ** -0.5, 0.3125)
    b_norm_two = jnp.clip(1.0 + 0.18 * jax.random.normal(splits[14], (C2,), jnp.float32), 0.1, 1.9)
    b_raise = gaussian(splits[15], (C2, FF2), C2 ** -0.5, 0.3125)
    b_lower = gaussian(splits[16], (FF2, C2), FF2 ** -0.5, 0.15625)
    up_first = gaussian(splits[17], (C2, 4 * C), C2 ** -0.5, 0.3125)
    up_norm = jnp.clip(1.0 + 0.18 * jax.random.normal(splits[18], (C,), jnp.float32), 0.1, 1.9)
    up_second = gaussian(splits[19], (C, C), C ** -0.5, 0.4375)
    return {"field": field, "a_norm_one": a_norm_one, "a_project": a_project, "a_bias": a_bias, "a_output": a_output, "a_norm_two": a_norm_two, "a_raise": a_raise, "a_lower": a_lower, "merge_norm_gain": merge_norm_gain, "merge_weight": merge_weight, "b_norm_one": b_norm_one, "b_project": b_project, "b_bias": b_bias, "b_output": b_output, "b_norm_two": b_norm_two, "b_raise": b_raise, "b_lower": b_lower, "up_first": up_first, "up_norm": up_norm, "up_second": up_second}


EPS = 1e-05

def layer_norm(values, norm_gain):
    average = lax.optimization_barrier(jnp.mean(values, axis=-1, keepdims=True))
    centred = values - average
    variance = lax.optimization_barrier(jnp.mean(centred * centred, axis=-1, keepdims=True))
    return centred * lax.rsqrt(variance + EPS) * norm_gain.astype(jnp.float32)

def norm_project(block, norm_gain, weight_matrix):
    flat = block.reshape(-1, block.shape[-1]).astype(jnp.float32)
    normed = layer_norm(flat, norm_gain).astype(jnp.bfloat16)
    result = jnp.dot(normed, weight_matrix, preferred_element_type=jnp.float32).astype(jnp.bfloat16)
    return result.reshape(block.shape[:-1] + (weight_matrix.shape[1],))

def partition(grid):
    depth, height, breadth, features = grid.shape
    tiles = grid.reshape(depth // WIN_P, WIN_P, height // WIN_LAT, WIN_LAT, breadth // WIN_LON, WIN_LON, features)
    return tiles.transpose(0, 2, 4, 1, 3, 5, 6).reshape(-1, WIN_P * WIN_LAT * WIN_LON, features)

def assemble(tiles, depth, height, breadth):
    features = tiles.shape[-1]
    grid = tiles.reshape(depth // WIN_P, height // WIN_LAT, breadth // WIN_LON, WIN_P, WIN_LAT, WIN_LON, features)
    return grid.transpose(0, 3, 1, 4, 2, 5, 6).reshape(depth, height, breadth, features)

def regions(depth, height, breadth, lat_start, lat_total):
    level_edge = (jnp.arange(depth, dtype=jnp.int32) == depth - 1).astype(jnp.int32)
    lat_edge = (lat_start + jnp.arange(height, dtype=jnp.int32) >= lat_total - WIN_LAT // 2).astype(jnp.int32)
    grid = 2 * level_edge[:, None, None] + lat_edge[None, :, None] + jnp.zeros((1, 1, breadth), jnp.int32)
    return partition(grid[..., None])[..., 0]

def attend(tiles, region, bias):
    heads = bias.shape[0]
    count, size, triple = tiles.shape
    width = triple // 3
    split = tiles.reshape(count, size, 3, heads, width // heads).astype(jnp.float32)
    scores = jnp.einsum('wqhd,wkhd->whqk', split[:, :, 0], split[:, :, 1])
    scores = scores * (1.0 / math.sqrt(width // heads)) + bias[None].astype(jnp.float32)
    allowed = region[:, :, None] == region[:, None, :]
    scores = jnp.where(allowed[:, None], scores, -1e+30)
    highest = lax.optimization_barrier(jnp.max(scores, axis=-1, keepdims=True))
    raised = jnp.exp(scores - highest)
    weights = (raised / lax.optimization_barrier(jnp.sum(raised, axis=-1, keepdims=True))).astype(jnp.bfloat16)
    mixed = jnp.einsum('whqk,wkhd->wqhd', weights.astype(jnp.float32), split[:, :, 2])
    return mixed.astype(jnp.bfloat16).reshape(count, size, width)

def shifted_block(field, gain_one, weight_qkv, bias, weight_out, gain_two, weight_up, weight_down):
    depth, height, breadth, width = field.shape

    def project_level(level):
        return norm_project(level, gain_one, weight_qkv)
    projected = lax.map(project_level, field)
    moved = jnp.roll(projected, (-(WIN_P // 2), -(WIN_LAT // 2), -(WIN_LON // 2)), axis=(0, 1, 2))
    tiles = partition(moved)
    region = regions(depth, height, breadth, 0, height)
    groups = depth // WIN_P * (height // WIN_LAT)
    size = tiles.shape[1]
    tiles = tiles.reshape(groups, -1, size, tiles.shape[2])
    region = region.reshape(groups, -1, size)

    def attend_group(pair):
        return attend(pair[0], pair[1], bias)
    mixed = lax.map(attend_group, (tiles, region))
    mixed = assemble(mixed.reshape(-1, size, width), depth, height, breadth)
    mixed = jnp.roll(mixed, (WIN_P // 2, WIN_LAT // 2, WIN_LON // 2), axis=(0, 1, 2))

    def finish(pair):
        level, attended = pair
        flat = level.reshape(-1, width).astype(jnp.float32)
        after = flat + jnp.dot(attended.reshape(-1, width), weight_out, preferred_element_type=jnp.float32)
        after = after.astype(jnp.bfloat16)
        normed = layer_norm(after.astype(jnp.float32), gain_two).astype(jnp.bfloat16)
        hidden = jax.nn.gelu(jnp.dot(normed, weight_up, preferred_element_type=jnp.float32), approximate=False)
        hidden = hidden.astype(jnp.bfloat16)
        result = after.astype(jnp.float32) + jnp.dot(hidden, weight_down, preferred_element_type=jnp.float32)
        return result.astype(jnp.bfloat16).reshape(height, breadth, width)
    return lax.map(finish, (field, mixed))

def merge_patches(field, norm_gain, weight_matrix):
    depth, height, breadth, width = field.shape
    merged = field.reshape(depth, height // 2, 2, breadth // 2, 2, width).transpose(0, 1, 3, 2, 4, 5)
    merged = merged.reshape(depth, height // 2, breadth // 2, 4 * width)
    return norm_project(merged, norm_gain, weight_matrix)

def upsample(coarse_grid, skip_state, first, norm_gain, second):
    depth, height, breadth, width = skip_state.shape
    flat = coarse_grid.reshape(-1, coarse_grid.shape[-1])
    raised = jnp.dot(flat, first, preferred_element_type=jnp.float32).astype(jnp.bfloat16)
    raised = raised.reshape(depth, height // 2, breadth // 2, 2, 2, width).transpose(0, 1, 3, 2, 4, 5)
    raised = raised.reshape(-1, width).astype(jnp.float32)
    normed = layer_norm(raised, norm_gain).astype(jnp.bfloat16)
    total = skip_state.reshape(-1, width).astype(jnp.float32) + jnp.dot(normed, second, preferred_element_type=jnp.float32)
    return total.astype(jnp.bfloat16).reshape(depth, height, breadth, width)

def reference(field, a_norm_one, a_project, a_bias, a_output, a_norm_two, a_raise, a_lower, merge_norm_gain, merge_weight, b_norm_one, b_project, b_bias, b_output, b_norm_two, b_raise, b_lower, up_first, up_norm, up_second):
    skip_state = shifted_block(field, a_norm_one, a_project, a_bias, a_output, a_norm_two, a_raise, a_lower)
    coarse_grid = merge_patches(skip_state, merge_norm_gain, merge_weight)
    coarse_grid = shifted_block(coarse_grid, b_norm_one, b_project, b_bias, b_output, b_norm_two, b_raise, b_lower)
    return upsample(coarse_grid, skip_state, up_first, up_norm, up_second)
```

```python
import math

import jax
import jax.numpy as jnp
from jax import lax
from jax.experimental import pallas as pl
from jax.experimental.pallas import tpu as pltpu
from jax.sharding import PartitionSpec as P

WIN_P = 2
WIN_LAT = 6
WIN_LON = 12
WIN = WIN_P * WIN_LAT * WIN_LON
HALF_LAT = WIN_LAT // 2
HALF_LON = WIN_LON // 2
HEAD = 32
MAIN = 128
REST = WIN - MAIN
EPS = 1e-05
LOG2E = math.log2(math.e)
EXCLUDED = -1e30
PITCH = 32

F32 = jnp.float32
BF16 = jnp.bfloat16


def dot(a, b, contract=((1,), (0,))):
    return lax.dot_general(a, b, (contract, ((), ())), preferred_element_type=F32)


def layer_norm(values, gain):
    average = jnp.mean(values, axis=-1, keepdims=True)
    centred = values - average
    variance = jnp.mean(centred * centred, axis=-1, keepdims=True)
    return centred * lax.rsqrt(variance + EPS) * gain


def gelu(x):
    return 0.5 * x * (1.0 + lax.erf(x * (1.0 / math.sqrt(2.0))))


def token_index(shape, heads):
    key = lax.broadcasted_iota(jnp.int32, shape, 0)
    column = lax.broadcasted_iota(jnp.int32, shape, 1)
    rest = column - heads * MAIN
    query = jnp.where(rest < 0, jnp.bitwise_and(column, MAIN - 1), MAIN + jnp.bitwise_and(rest, REST - 1))
    return key, query


def level_mask(heads):
    key, query = token_index((WIN, heads * WIN), heads)
    half = WIN // 2
    return jnp.where((key >= half) != (query >= half), EXCLUDED, 0.0)


def lat_mask(heads):
    key, query = token_index((WIN, heads * WIN), heads)
    half, quarter = WIN // 2, WIN // 4

    def late(t):
        return jnp.where(t >= half, t - half, t) >= quarter

    return jnp.where(late(key) != late(query), EXCLUDED, 0.0)


def attend(q, k, vt, table, heads):
    width = heads * HEAD
    lane = lax.broadcasted_iota(jnp.int32, (1, MAIN), 1) // HEAD
    zero = jnp.zeros((), BF16)
    pieces = []
    rests = []
    for start in range(0, width, MAIN):
        stop = min(start + MAIN, width)
        span = stop - start
        qs = q[:, start:stop]
        here = span // HEAD
        masked = [jnp.where(lane[:, :span] == h, qs, zero) for h in range(here)]
        main = jnp.concatenate([m[:MAIN] for m in masked], axis=0)
        rest = jnp.concatenate([m[MAIN:] for m in masked], axis=0)
        ks = k[:, start:stop]
        pieces.append(dot(ks, main, ((1,), (1,))))
        rests.append(dot(ks, rest, ((1,), (1,))))
    outs = []
    base = 0
    for piece in pieces:
        span = piece.shape[1]
        s = piece + table[:, base : base + span]
        s = s - jnp.max(s, axis=0, keepdims=True)
        e = jnp.exp2(s)
        inv = 1.0 / jnp.sum(e, axis=0, keepdims=True)
        p = e.astype(BF16)
        for h in range(span // MAIN):
            row = base // MAIN + h
            cut = slice(h * MAIN, (h + 1) * MAIN)
            outs.append(dot(vt[row * HEAD : (row + 1) * HEAD], p[:, cut]) * inv[:, cut])
        base += span
    main_out = jnp.concatenate(outs, axis=0)
    s = jnp.concatenate(rests, axis=1) + table[:, base:]
    s = s - jnp.max(s, axis=0, keepdims=True)
    e = jnp.exp2(s)
    inv = 1.0 / jnp.sum(e, axis=0, keepdims=True)
    full = dot(vt, e.astype(BF16)) * inv
    row = lax.broadcasted_iota(jnp.int32, full.shape, 0) // HEAD
    column = lax.broadcasted_iota(jnp.int32, full.shape, 1) // REST
    full = jnp.where(row == column, full, 0.0).astype(BF16)
    fold_row = lax.broadcasted_iota(jnp.int32, (heads * REST, REST), 0)
    fold_column = lax.broadcasted_iota(jnp.int32, (heads * REST, REST), 1)
    fold = jnp.where(jnp.bitwise_and(fold_row, REST - 1) == fold_column, 1.0, 0.0).astype(BF16)
    rest_out = dot(full, fold)
    return jnp.concatenate([main_out.astype(BF16), rest_out.astype(BF16)], axis=1)


def block_rows(x_ref, count, tables, heads, gain_one, wq, wk, wvt, wo, gain_two, w1, w2, out_ref):
    width = heads * HEAD
    x = x_ref[...]
    xn = layer_norm(x, gain_one[...]).astype(BF16)
    q = (dot(xn, wq[...]) * (LOG2E / math.sqrt(HEAD))).astype(BF16)
    k = dot(xn, wk[...]).astype(BF16)
    mixed = []
    for w in range(count):
        rows = slice(w * WIN, (w + 1) * WIN)
        vt = dot(wvt[...], xn[rows], ((1,), (1,))).astype(BF16)
        attended = attend(q[rows], k[rows], vt, tables[w][...], heads)
        mixed.append(dot(attended, wo[...], ((0,), (0,))))
    after = (x + jnp.concatenate(mixed, axis=0)).astype(BF16).astype(F32)
    normed = layer_norm(after, gain_two[...]).astype(BF16)
    hidden = gelu(dot(normed, w1[...])).astype(BF16)
    out_ref[...] = after + dot(hidden, w2[...])


def fill_frame(put, base, own, lat, lon, diag):
    height = own.shape[0]
    for i in range(height):
        at = base + i * PITCH
        if i < height - HALF_LAT:
            put(at, own[i + HALF_LAT].astype(F32))
            put(at + 24, lon[i].astype(F32))
        else:
            j = i - (height - HALF_LAT)
            put(at + 6, lat[j].astype(F32))
            put(at + 24, diag[j].astype(F32))


def fine_kernel(
    edge_ref, own0, own1, lat0, lat1, lon0, lon1, diag0, diag1, table_ref,
    gain_one, wq, wk, wvt, wo, gain_two, w1, w2,
    keep_ref, to_lat_ref, to_lon_ref, to_diag_ref,
    g_ref, x_ref, y_ref, tables_ref,
):
    heads = 6
    step = pl.program_id(0)

    @pl.when(step == 0)
    def _():
        table = table_ref[...]
        tables_ref[0] = table
        tables_ref[1] = table + lat_mask(heads) * edge_ref[0].astype(F32)

    @pl.when(step == pl.num_programs(0) - 1)
    def _():
        mask = level_mask(heads)
        tables_ref[0] = tables_ref[0] + mask
        tables_ref[1] = tables_ref[1] + mask

    def put(at, value):
        g_ref[at : at + value.shape[0], :] = value

    rows = own0.shape[1]
    for lev, parts in enumerate(((own0, lat0, lon0, diag0), (own1, lat1, lon1, diag1))):
        fill_frame(put, lev * rows * PITCH, *[part.at[0] for part in parts])
    at = 0
    for i in range(2):
        for j in range(2):
            for lev in range(WIN_P):
                for r in range(WIN_LAT):
                    start = (lev * rows + i * WIN_LAT + r) * PITCH + HALF_LON + j * WIN_LON
                    x_ref[at : at + WIN_LON, :] = g_ref[start : start + WIN_LON, :]
                    at += WIN_LON
    tables = [tables_ref.at[w // 2] for w in range(4)]
    block_rows(x_ref, 4, tables, heads, gain_one, wq, wk, wvt, wo, gain_two, w1, w2, y_ref)
    at = 0
    for i in range(2):
        for j in range(2):
            for lev in range(WIN_P):
                for r in range(WIN_LAT):
                    start = (lev * rows + i * WIN_LAT + r) * PITCH + j * WIN_LON
                    g_ref[start : start + WIN_LON, :] = y_ref[at : at + WIN_LON, :]
                    at += WIN_LON
    for lev in range(WIN_P):
        for r in range(rows):
            start = (lev * rows + r) * PITCH
            line = g_ref[start : start + 24, :].astype(BF16)
            keep_ref[lev, r] = line
            if r < HALF_LAT:
                to_diag_ref[lev, r] = line[:HALF_LON]
                to_lat_ref[lev, r] = g_ref[start + 6 : start + 24, :].astype(BF16)
            else:
                to_lon_ref[lev, r - HALF_LAT] = line[:HALF_LON]


def coarse_kernel(
    edge_ref, own, lat, lon, diag, table_ref,
    merge_gain, merge_weight,
    gain_one, wq, wk, wvt, wo, gain_two, w1, w2,
    up_first, up_norm, up_second,
    stay_ref, to_lat_ref, to_lon_ref, to_diag_ref,
    low_ref, high_ref, parts_ref, x_ref, y_ref, tables_ref,
):
    heads = 12
    width = own.shape[3]

    def put(at, value):
        low_ref[at : at + value.shape[0], :] = value[:, :MAIN]
        high_ref[at : at + value.shape[0], : width - MAIN] = value[:, MAIN:]

    pairs = own.shape[0] // WIN_P
    rows = own.shape[1]
    tables_ref[0] = table_ref[...] + lat_mask(heads) * edge_ref[0].astype(F32)
    tables_ref[1] = tables_ref[0] + level_mask(heads)
    for lev in range(own.shape[0]):
        fill_frame(put, lev * rows * PITCH, *[part.at[lev] for part in (own, lat, lon, diag)])
    for r in range(2):
        for t in range(2):
            at = 0
            for lev in range(own.shape[0]):
                for a in range(rows // 2):
                    start = (lev * rows + 2 * a + r) * PITCH + HALF_LON + t
                    parts_ref[2 * r + t, at : at + WIN_LON, :MAIN] = low_ref[pl.ds(start, WIN_LON, stride=2), :]
                    parts_ref[2 * r + t, at : at + WIN_LON, MAIN:] = high_ref[pl.ds(start, WIN_LON, stride=2), :]
                    at += WIN_LON
    parts = [parts_ref[n, :, :width] for n in range(4)]
    average = jnp.sum(parts[0] + parts[1] + parts[2] + parts[3], axis=-1, keepdims=True) * (1.0 / (4 * width))
    centred = [part - average for part in parts]
    squares = centred[0] * centred[0]
    for c in centred[1:]:
        squares += c * c
    scale = lax.rsqrt(jnp.sum(squares, axis=-1, keepdims=True) * (1.0 / (4 * width)) + EPS)
    total = None
    for n in range(4):
        normed = (centred[n] * scale * merge_gain[n : n + 1, :]).astype(BF16)
        term = dot(normed, merge_weight[n])
        total = term if total is None else total + term
    x_ref[...] = total.astype(BF16).astype(F32)
    tables = [tables_ref.at[1 if w == pairs - 1 else 0] for w in range(pairs)]
    block_rows(x_ref, pairs, tables, heads, gain_one, wq, wk, wvt, wo, gain_two, w1, w2, y_ref)
    coarse = y_ref[...].astype(BF16)
    for r in range(2):
        for t in range(2):
            n = 2 * r + t
            raised = dot(coarse, up_first[n]).astype(BF16).astype(F32)
            normed = layer_norm(raised, up_norm[...]).astype(BF16)
            parts_ref[n, :, :width] = parts_ref[n, :, :width] + dot(normed, up_second[...])
            at = 0
            for lev in range(own.shape[0]):
                for a in range(rows // 2):
                    start = (lev * rows + 2 * a + r) * PITCH + t
                    low_ref[pl.ds(start, WIN_LON, stride=2), :] = parts_ref[n, at : at + WIN_LON, :MAIN]
                    high_ref[pl.ds(start, WIN_LON, stride=2), :] = parts_ref[n, at : at + WIN_LON, MAIN:]
                    at += WIN_LON
    half = rows // 2
    for lev in range(own.shape[0]):
        for r in range(rows):
            start = (lev * rows + r) * PITCH
            targets = (stay_ref, to_lon_ref) if r < half else (to_lat_ref, to_diag_ref)
            for side, target in enumerate(targets):
                cut = slice(start + side * WIN_LON, start + (side + 1) * WIN_LON)
                target[lev, r % half, :, :MAIN] = low_ref[cut, :].astype(BF16)
                target[lev, r % half, :, MAIN:] = high_ref[cut, : width - MAIN].astype(BF16)


def whole(array):
    zeros = (0,) * array.ndim
    return pl.BlockSpec(array.shape, lambda *_: zeros)


def level_spec(array, lev, levels):
    shape = (1,) + array.shape[1:]
    return pl.BlockSpec(shape, lambda g: (lax.rem(WIN_P * g + lev + WIN_P // 2, levels), 0, 0, 0))


def fine_stage(edge, field, lat, lon, diag, table, weights):
    levels, rows, columns, width = field.shape
    smem = pl.BlockSpec(memory_space=pltpu.SMEM)
    operands = [edge]
    specs = [smem]
    for array in (field, lat, lon, diag):
        for lev in range(WIN_P):
            operands.append(array)
            specs.append(level_spec(array, lev, levels))
    for array in (table, *weights):
        operands.append(array)
        specs.append(whole(array))
    shapes = [
        (levels, rows, columns, width),
        (levels, HALF_LAT, columns - HALF_LON, width),
        (levels, rows - HALF_LAT, HALF_LON, width),
        (levels, HALF_LAT, HALF_LON, width),
    ]
    tokens = WIN_P * rows * columns
    return pl.pallas_call(
        fine_kernel,
        grid=(levels // WIN_P,),
        in_specs=specs,
        out_specs=[pl.BlockSpec((WIN_P,) + s[1:], lambda g: (g, 0, 0, 0)) for s in shapes],
        out_shape=[jax.ShapeDtypeStruct(s, BF16) for s in shapes],
        scratch_shapes=[
            pltpu.VMEM((WIN_P * rows * PITCH, width), F32),
            pltpu.VMEM((tokens, width), F32),
            pltpu.VMEM((tokens, width), F32),
            pltpu.VMEM((2,) + table.shape, F32),
        ],
        compiler_params=pltpu.CompilerParams(vmem_limit_bytes=48 * 1024 * 1024),
        name="fine_stage",
    )(*operands)


def coarse_stage(edge, field, lat, lon, diag, table, weights):
    levels, rows, columns, width = field.shape
    smem = pl.BlockSpec(memory_space=pltpu.SMEM)
    operands = [edge, field, lat, lon, diag, table, *weights]
    vmem = pl.BlockSpec(memory_space=pltpu.VMEM)
    quarter = (levels, rows // 2, columns // 2, width)
    tokens = levels * rows * columns // 4
    return pl.pallas_call(
        coarse_kernel,
        in_specs=[smem] + [vmem] * (len(operands) - 1),
        out_specs=[vmem] * 4,
        out_shape=[jax.ShapeDtypeStruct(quarter, BF16)] * 4,
        scratch_shapes=[
            pltpu.VMEM((levels * rows * PITCH, MAIN), F32),
            pltpu.VMEM((levels * rows * PITCH, MAIN), F32),
            pltpu.VMEM((4, tokens, 2 * MAIN), F32),
            pltpu.VMEM((tokens, 2 * width), F32),
            pltpu.VMEM((tokens, 2 * width), F32),
            pltpu.VMEM((2,) + table.shape, F32),
        ],
        compiler_params=pltpu.CompilerParams(vmem_limit_bytes=56 * 1024 * 1024),
        name="coarse_stage",
    )(*operands)


def shift(array, lat_by, lon_by):
    lats, lons = lax.axis_size("lat"), lax.axis_size("lon")
    if lat_by and lon_by:
        pairs = [
            (((a + lat_by) % lats) * lons + (b + lon_by) % lons, a * lons + b)
            for a in range(lats)
            for b in range(lons)
        ]
        return lax.ppermute(array, ("lat", "lon"), pairs)
    if lat_by:
        return lax.ppermute(array, "lat", [((i + lat_by) % lats, i) for i in range(lats)])
    return lax.ppermute(array, "lon", [((i + lon_by) % lons, i) for i in range(lons)])


def score_table(bias):
    heads = bias.shape[0]
    turned = (bias * LOG2E).transpose(2, 0, 1)
    main = turned[:, :, :MAIN].reshape(WIN, heads * MAIN)
    rest = turned[:, :, MAIN:].reshape(WIN, heads * REST)
    return jnp.concatenate([main, rest], axis=1)


def block_weights(gain_one, project, output, gain_two, raise_, lower):
    width = output.shape[0]
    return [
        gain_one.reshape(1, -1),
        project[:, :width],
        project[:, width : 2 * width],
        project[:, 2 * width :].T,
        output,
        gain_two.reshape(1, -1),
        raise_,
        lower,
    ]


def body(
    field, a_norm_one, a_project, a_bias, a_output, a_norm_two, a_raise, a_lower,
    merge_norm_gain, merge_weight,
    b_norm_one, b_project, b_bias, b_output, b_norm_two, b_raise, b_lower,
    up_first, up_norm, up_second,
):
    width = field.shape[-1]
    edge = (lax.axis_index("lat") == lax.axis_size("lat") - 1).astype(jnp.int32).reshape(1)
    lon = shift(field[:, HALF_LAT:, :HALF_LON], 0, 1)
    lat = shift(field[:, :HALF_LAT, HALF_LON:], 1, 0)
    diag = shift(field[:, :HALF_LAT, :HALF_LON], 1, 1)
    fine_weights = block_weights(a_norm_one, a_project, a_output, a_norm_two, a_raise, a_lower)
    skip, lat, lon, diag = fine_stage(edge, field, lat, lon, diag, score_table(a_bias), fine_weights)
    diag = shift(diag, 1, 1)
    lat = shift(lat, 1, 0)
    lon = shift(lon, 0, 1)
    coarse_weights = [
        merge_norm_gain.reshape(4, width),
        merge_weight.reshape(4, width, -1),
        *block_weights(b_norm_one, b_project, b_output, b_norm_two, b_raise, b_lower),
        up_first.reshape(-1, 4, width).transpose(1, 0, 2),
        up_norm.reshape(1, -1),
        up_second,
    ]
    stay, lat, lon, diag = coarse_stage(edge, skip, lat, lon, diag, score_table(b_bias), coarse_weights)
    diag = shift(diag, -1, -1)
    lat = shift(lat, -1, 0)
    lon = shift(lon, 0, -1)
    upper = jnp.concatenate([diag, lat], axis=2)
    lower = jnp.concatenate([lon, stay], axis=2)
    return jnp.roll(jnp.concatenate([upper, lower], axis=1), WIN_P // 2, axis=0)


def solution(mesh):
    in_specs = (P(None, "lat", "lon", None),) + (P(),) * 19
    out_specs = P(None, "lat", "lon", None)
    return jax.shard_map(body, mesh=mesh, in_specs=in_specs, out_specs=out_specs, check_vma=False)
```

```python
import math

import jax
import jax.numpy as jnp
from jax import lax
from jax.experimental import pallas as pl
from jax.experimental.pallas import tpu as pltpu
from jax.sharding import PartitionSpec as P

WIN_P = 2
WIN_LAT = 6
WIN_LON = 12
WIN = WIN_P * WIN_LAT * WIN_LON
HALF_LAT = WIN_LAT // 2
HALF_LON = WIN_LON // 2
HEAD = 32
MAIN = 128
REST = WIN - MAIN
EPS = 1e-05
LOG2E = math.log2(math.e)
EXCLUDED = -1e30
PITCH = 32

F32 = jnp.float32
BF16 = jnp.bfloat16


def dot(a, b, contract=((1,), (0,))):
    return lax.dot_general(a, b, (contract, ((), ())), preferred_element_type=F32)


def layer_norm(values, gain):
    average = jnp.mean(values, axis=-1, keepdims=True)
    centred = values - average
    variance = jnp.mean(centred * centred, axis=-1, keepdims=True)
    return centred * lax.rsqrt(variance + EPS) * gain


def gelu(x):
    return 0.5 * x * (1.0 + lax.erf(x * (1.0 / math.sqrt(2.0))))


def token_index(shape, heads):
    key = lax.broadcasted_iota(jnp.int32, shape, 0)
    column = lax.broadcasted_iota(jnp.int32, shape, 1)
    rest = column - heads * MAIN
    query = jnp.where(rest < 0, jnp.bitwise_and(column, MAIN - 1), MAIN + jnp.bitwise_and(rest, REST - 1))
    return key, query


def level_mask(heads):
    key, query = token_index((WIN, heads * WIN), heads)
    half = WIN // 2
    return jnp.where((key >= half) != (query >= half), EXCLUDED, 0.0)


def lat_mask(heads):
    key, query = token_index((WIN, heads * WIN), heads)
    half, quarter = WIN // 2, WIN // 4

    def late(t):
        return jnp.where(t >= half, t - half, t) >= quarter

    return jnp.where(late(key) != late(query), EXCLUDED, 0.0)


def attend(q, k, vt, table, heads):
    width = heads * HEAD
    lane = lax.broadcasted_iota(jnp.int32, (1, MAIN), 1) // HEAD
    zero = jnp.zeros((), BF16)
    pieces = []
    rests = []
    for start in range(0, width, MAIN):
        stop = min(start + MAIN, width)
        span = stop - start
        qs = q[:, start:stop]
        here = span // HEAD
        masked = [jnp.where(lane[:, :span] == h, qs, zero) for h in range(here)]
        main = jnp.concatenate([m[:MAIN] for m in masked], axis=0)
        rest = jnp.concatenate([m[MAIN:] for m in masked], axis=0)
        ks = k[:, start:stop]
        pieces.append(dot(ks, main, ((1,), (1,))))
        rests.append(dot(ks, rest, ((1,), (1,))))
    outs = []
    base = 0
    for piece in pieces:
        span = piece.shape[1]
        s = piece + table[:, base : base + span]
        s = s - jnp.max(s, axis=0, keepdims=True)
        e = jnp.exp2(s)
        inv = 1.0 / jnp.sum(e, axis=0, keepdims=True)
        p = e.astype(BF16)
        for h in range(span // MAIN):
            row = base // MAIN + h
            cut = slice(h * MAIN, (h + 1) * MAIN)
            outs.append(dot(vt[row * HEAD : (row + 1) * HEAD], p[:, cut]) * inv[:, cut])
        base += span
    main_out = jnp.concatenate(outs, axis=0)
    s = jnp.concatenate(rests, axis=1) + table[:, base:]
    s = s - jnp.max(s, axis=0, keepdims=True)
    e = jnp.exp2(s)
    inv = 1.0 / jnp.sum(e, axis=0, keepdims=True)
    full = dot(vt, e.astype(BF16)) * inv
    row = lax.broadcasted_iota(jnp.int32, full.shape, 0) // HEAD
    column = lax.broadcasted_iota(jnp.int32, full.shape, 1) // REST
    full = jnp.where(row == column, full, 0.0).astype(BF16)
    fold_row = lax.broadcasted_iota(jnp.int32, (heads * REST, REST), 0)
    fold_column = lax.broadcasted_iota(jnp.int32, (heads * REST, REST), 1)
    fold = jnp.where(jnp.bitwise_and(fold_row, REST - 1) == fold_column, 1.0, 0.0).astype(BF16)
    rest_out = dot(full, fold)
    return jnp.concatenate([main_out.astype(BF16), rest_out.astype(BF16)], axis=1)


def block_rows(x_ref, count, table_ref, heads, gain_one, wq, wk, wvt, wo, gain_two, w1, w2, w2_dims, out_ref):
    x = x_ref[...]
    xn = layer_norm(x, gain_one[...][None, :]).astype(BF16)
    q = (dot(xn, wq) * (LOG2E / math.sqrt(HEAD))).astype(BF16)
    k = dot(xn, wk).astype(BF16)
    mixed = []
    for w in range(count):
        rows = slice(w * WIN, (w + 1) * WIN)
        vt = dot(wvt, xn[rows], ((1,), (1,))).astype(BF16)
        table = table_ref.at[1 if w == count - 1 else 0]
        attended = attend(q[rows], k[rows], vt, table, heads)
        mixed.append(dot(attended, wo[...], ((0,), (0,))))
    after = (x + jnp.concatenate(mixed, axis=0)).astype(BF16).astype(F32)
    normed = layer_norm(after, gain_two[...][None, :]).astype(BF16)
    hidden = gelu(dot(normed, w1[...])).astype(BF16)
    out_ref[...] = (after + dot(hidden, w2[...], w2_dims)).astype(BF16).astype(F32)


class Packed:
    def __init__(self, low_ref, high_ref, rows):
        self.low, self.high, self.rows = low_ref, high_ref, rows
        self.pairs = low_ref.shape[0]

    def put(self, p, at, value):
        n = value.shape[0]
        self.low[p, at : at + n, :] = value[:, :MAIN]
        self.high[p, at : at + n, : value.shape[1] - MAIN] = value[:, MAIN:]

    def get(self, p, at, n):
        return jnp.concatenate([self.low[p, at : at + n, :], self.high[p, at : at + n, : MAIN // 2]], axis=1)

    def store(self, out_ref):
        half = self.pairs // 2
        rows = slice(0, self.rows)
        for p in range(self.pairs):
            out_ref[p] = self.low[p, rows, :].astype(BF16)
        for p in range(half):
            sides = [self.high[p + s * half, rows, : MAIN // 2] for s in range(2)]
            out_ref[self.pairs + p] = jnp.concatenate(sides, axis=1).astype(BF16)

    def load(self, in_ref):
        half = self.pairs // 2
        rows = slice(0, self.rows)
        for p in range(self.pairs):
            self.low[p, rows, :] = in_ref[p].astype(F32)
        for p in range(half):
            both = in_ref[self.pairs + p].astype(F32)
            for s in range(2):
                self.high[p + s * half, rows, : MAIN // 2] = both[:, s * MAIN // 2 : (s + 1) * MAIN // 2]
        return self


def packed_rows(tokens):
    return -(-tokens // 16) * 16


def pair_levels(p, levels):
    return [(WIN_P * p + WIN_P // 2 + lev) % levels for lev in range(WIN_P)]


def start_kernel(field, lat_ref, lon_ref, diag_ref, line_ref, low_ref, high_ref):
    levels, rows, columns, _ = field.shape
    packs = [Packed(low_ref.at[n], high_ref.at[n], ref.shape[1]) for n, ref in enumerate((lat_ref, lon_ref, diag_ref))]
    lat, lon, diag = packs
    for p in range(levels // WIN_P):
        for lev, level in enumerate(pair_levels(p, levels)):
            for r in range(rows):
                line = field[level, r].astype(F32)
                if r < HALF_LAT:
                    slot = level * HALF_LAT + r
                    line_ref[slot] = line
                    diag.put(p, (lev * HALF_LAT + r) * HALF_LON, line[:HALF_LON])
                    span = columns - HALF_LON
                    lat.put(p, (lev * HALF_LAT + r) * span, line_ref[slot, HALF_LON:, :])
                else:
                    lon.put(p, (lev * (rows - HALF_LAT) + r - HALF_LAT) * HALF_LON, line[:HALF_LON])
    for pack, ref in zip(packs, (lat_ref, lon_ref, diag_ref)):
        pack.store(ref)


def table_kernel(edge_ref, a_bias, b_bias, project, plain_ref, late_ref, coarse_ref, wq_ref, wk_ref, wvt_ref):
    edge = edge_ref[0].astype(F32)
    for bias, out in ((a_bias, plain_ref), (b_bias, coarse_ref)):
        heads = bias.shape[0]
        for h in range(heads):
            turned = (bias[h] * LOG2E).T
            out[0, :, h * MAIN : (h + 1) * MAIN] = turned[:, :MAIN]
            out[0, :, heads * MAIN + h * REST : heads * MAIN + (h + 1) * REST] = turned[:, MAIN:]
        level = level_mask(heads)
        late = lat_mask(heads) * edge
        if out is coarse_ref:
            out[0] = out[0] + late
        else:
            late_ref[0] = out[0] + late
            late_ref[1] = late_ref[0] + level
        out[1] = out[0] + level
    width = wq_ref.shape[0]
    wq_ref[...] = project[:, :width]
    wk_ref[...] = project[:, width : 2 * width]
    wvt_ref[...] = project[:, 2 * width :].astype(F32).T.astype(BF16)


def fine_kernel(i, j, *refs):
    refs = list(refs)
    field = refs.pop(0)
    lat_in = refs.pop(0) if i else None
    lon_in = refs.pop(0) if j else None
    diag_in = refs.pop(0) if i and j else None
    first = refs.pop(0) if i != j else None
    table_ref, gain_one, wq, wk, wvt, wo, gain_two, w1, w2t, out_ref = refs[:10]
    refs = refs[10:]
    send_ref = None if i and j else refs.pop(0)
    line_ref, x_ref, low_ref, high_ref = refs
    levels, rows, columns, _ = field.shape
    pairs = levels // WIN_P
    lat, lon, diag = [
        Packed(low_ref.at[n], high_ref.at[n], ref.shape[1]).load(ref) if ref is not None else None
        for n, ref in enumerate((lat_in, lon_in, diag_in))
    ]
    at = 0
    slot = 0
    for p in range(pairs):
        for lev, level in enumerate(pair_levels(p, levels)):
            for row in range(i * WIN_LAT, (i + 1) * WIN_LAT):
                start = HALF_LON + j * WIN_LON
                own = min(columns - start, WIN_LON)
                if row + HALF_LAT < rows:
                    line_ref[slot] = field[level, row + HALF_LAT].astype(F32)
                    x_ref[at : at + own, :] = line_ref[slot, start : start + own, :]
                    slot += 1
                    if own < WIN_LON:
                        x_ref[at + own : at + WIN_LON, :] = lon.get(p, (lev * (rows - HALF_LAT) + row) * HALF_LON, HALF_LON)
                else:
                    below = lev * HALF_LAT + row + HALF_LAT - rows
                    x_ref[at : at + own, :] = lat.get(p, below * (columns - HALF_LON) + j * WIN_LON, own)
                    if own < WIN_LON:
                        x_ref[at + own : at + WIN_LON, :] = diag.get(p, below * HALF_LON, HALF_LON)
                at += WIN_LON
    block_rows(
        x_ref, pairs, table_ref, 6, gain_one, wq[...], wk[...], wvt[...], wo, gain_two, w1, w2t, ((1,), (1,)), out_ref
    )
    if send_ref is None:
        return
    send = Packed(low_ref.at[3], high_ref.at[3], send_ref.shape[1])
    for p in range(pairs):
        at = 0
        for lev in range(WIN_P):
            base = (p * WIN_P + lev) * WIN_LAT * WIN_LON
            if not i:
                for row in range(HALF_LAT):
                    here = base + row * WIN_LON
                    if j:
                        send.put(p, at, first[here + HALF_LON : here + WIN_LON, :])
                        send.put(p, at + HALF_LON, out_ref[here : here + WIN_LON, :])
                        at += WIN_LON + HALF_LON
                    else:
                        send.put(p, at, out_ref[here : here + HALF_LON, :])
                        at += HALF_LON
            else:
                for row in range(HALF_LAT, rows):
                    source, here = (first, row) if row < WIN_LAT else (out_ref, row - WIN_LAT)
                    here = base + here * WIN_LON
                    send.put(p, at, source[here : here + HALF_LON, :])
                    at += HALF_LON
    send.store(send_ref)


def coarse_kernel(
    w00, w01, w10, w11, lat_in, lon_in, diag_in, table_ref,
    merge_gain, merge_weight,
    gain_one, project, wo, gain_two, w1, w2,
    up_first, up_norm, up_second,
    stay_ref, to_lat_ref, to_lon_ref, to_diag_ref,
    low_ref, high_ref, grid_low, grid_high, quad_low, quad_high, parts_ref, x_ref, y_ref,
):
    heads = 12
    width = w00.shape[1]
    rows, columns = 2 * WIN_LAT, 2 * WIN_LON
    pairs = w00.shape[0] // WIN
    levels = pairs * WIN_P
    windows = ((w00, w01), (w10, w11))
    lat, lon, diag = [
        Packed(low_ref.at[n], high_ref.at[n], ref.shape[1]).load(ref) for n, ref in enumerate((lat_in, lon_in, diag_in))
    ]

    def put(at, value):
        grid_low[at : at + value.shape[0], :] = value[:, :MAIN]
        grid_high[at : at + value.shape[0], : width - MAIN] = value[:, MAIN:]

    for p in range(pairs):
        for lev in range(WIN_P):
            for row in range(rows):
                at = ((p * WIN_P + lev) * rows + row) * PITCH
                if row + HALF_LAT < rows:
                    left, right = windows[(row + HALF_LAT) // WIN_LAT]
                    here = ((p * WIN_P + lev) * WIN_LAT + (row + HALF_LAT) % WIN_LAT) * WIN_LON
                    put(at + HALF_LON, left[here + HALF_LON : here + WIN_LON, :])
                    put(at + WIN_LON, right[here : here + WIN_LON, :])
                    put(at + columns, lon.get(p, (lev * (rows - HALF_LAT) + row) * HALF_LON, HALF_LON))
                else:
                    below = lev * HALF_LAT + row + HALF_LAT - rows
                    span = columns - HALF_LON
                    put(at + HALF_LON, lat.get(p, below * span, span))
                    put(at + columns, diag.get(p, below * HALF_LON, HALF_LON))
    for r in range(2):
        for t in range(2):
            n = 2 * r + t
            at = 0
            for level in range(levels):
                for a in range(rows // 2):
                    start = (level * rows + 2 * a + r) * PITCH + HALF_LON + t
                    parts_ref[n, at : at + WIN_LON, :MAIN] = grid_low[pl.ds(start, WIN_LON, stride=2), :]
                    parts_ref[n, at : at + WIN_LON, MAIN:] = grid_high[pl.ds(start, WIN_LON, stride=2), :]
                    at += WIN_LON
    parts = [parts_ref[n, :, :width] for n in range(4)]
    average = jnp.sum(parts[0] + parts[1] + parts[2] + parts[3], axis=-1, keepdims=True) * (1.0 / (4 * width))
    centred = [part - average for part in parts]
    squares = centred[0] * centred[0]
    for c in centred[1:]:
        squares += c * c
    scale = lax.rsqrt(jnp.sum(squares, axis=-1, keepdims=True) * (1.0 / (4 * width)) + EPS)
    total = None
    for n in range(4):
        gain = merge_gain[n * width : (n + 1) * width][None, :]
        normed = (centred[n] * scale * gain).astype(BF16)
        term = dot(normed, merge_weight[n * width : (n + 1) * width, :])
        total = term if total is None else total + term
    x_ref[...] = total.astype(BF16).astype(F32)
    double = 2 * width
    wvt = project[:, 2 * double :].astype(F32).T.astype(BF16)
    block_rows(
        x_ref, pairs, table_ref, heads, gain_one, project[:, :double], project[:, double : 2 * double], wvt,
        wo, gain_two, w1, w2, ((1,), (0,)), y_ref,
    )
    coarse = y_ref[...].astype(BF16)
    half = rows // 2
    for r in range(2):
        for t in range(2):
            n = 2 * r + t
            raised = dot(coarse, up_first[:, n * width : (n + 1) * width]).astype(BF16).astype(F32)
            normed = layer_norm(raised, up_norm[...][None, :]).astype(BF16)
            parts_ref[n, :, :width] = parts_ref[n, :, :width] + dot(normed, up_second[...])
            for level in range(levels):
                for a in range(half):
                    row = 2 * a + r
                    for side in range(2):
                        at = (level * half + a) * WIN_LON + side * HALF_LON
                        quad, p = 2 * (row // half) + side, level // WIN_P
                        start = (level % WIN_P * half + row % half) * WIN_LON + t
                        to = pl.ds(start, HALF_LON, stride=2)
                        quad_low[quad, p, to, :] = parts_ref[n, at : at + HALF_LON, :MAIN]
                        quad_high[quad, p, to, :] = parts_ref[n, at : at + HALF_LON, MAIN:]
    for quad, ref in enumerate((stay_ref, to_lon_ref, to_lat_ref, to_diag_ref)):
        Packed(quad_low.at[quad], quad_high.at[quad], WIN).store(ref)


def finish_kernel(upper_left, upper_right, lower_left, lower_right, out_ref, low_ref, high_ref, line_low, line_high):
    levels, rows, columns, width = out_ref.shape
    half = rows // 2
    for quad, ref in enumerate((upper_left, upper_right, lower_left, lower_right)):
        pack = Packed(low_ref.at[quad], high_ref.at[quad], WIN).load(ref)
        for p in range(levels // WIN_P):
            for lev, level in enumerate(pair_levels(p, levels)):
                for row in range(half):
                    at = (level * rows + (quad // 2) * half + row) * columns + quad % 2 * WIN_LON
                    here = (lev * half + row) * WIN_LON
                    line_low[at : at + WIN_LON, :] = pack.low[p, here : here + WIN_LON, :]
                    line_high[at : at + WIN_LON, :] = pack.high[p, here : here + WIN_LON, :]
    for level in range(levels):
        for row in range(rows):
            at = (level * rows + row) * columns
            out_ref[level, row, :, :MAIN] = line_low[at : at + columns, :].astype(BF16)
            out_ref[level, row, :, MAIN:] = line_high[at : at + columns, : width - MAIN].astype(BF16)


MIB = 1024 * 1024


def call(kernel, name, operands, outs, scratch, limit, flops=0, scalars=0):
    vmem = pl.BlockSpec(memory_space=pltpu.VMEM)
    smem = pl.BlockSpec(memory_space=pltpu.SMEM)
    moved = sum(x.size * x.dtype.itemsize for x in operands) + sum(math.prod(s) * jnp.dtype(d).itemsize for s, d in outs)
    return pl.pallas_call(
        kernel,
        in_specs=[smem] * scalars + [vmem] * (len(operands) - scalars),
        out_specs=[vmem] * len(outs),
        out_shape=[jax.ShapeDtypeStruct(s, d) for s, d in outs],
        scratch_shapes=[pltpu.VMEM(s, F32) for s in scratch],
        compiler_params=pltpu.CompilerParams(vmem_limit_bytes=limit * MIB),
        cost_estimate=pl.CostEstimate(flops=flops, bytes_accessed=moved, transcendentals=0),
        name=name,
    )(*operands)


def packed_shape(tokens, pairs):
    return (pairs * 3 // 2, packed_rows(tokens), MAIN)


def shift(array, lat_by, lon_by):
    lats, lons = lax.axis_size("lat"), lax.axis_size("lon")
    if lat_by and lon_by:
        pairs = [
            (((a + lat_by) % lats) * lons + (b + lon_by) % lons, a * lons + b)
            for a in range(lats)
            for b in range(lons)
        ]
        return lax.ppermute(array, ("lat", "lon"), pairs)
    if lat_by:
        return lax.ppermute(array, "lat", [((i + lat_by) % lats, i) for i in range(lats)])
    return lax.ppermute(array, "lon", [((i + lon_by) % lons, i) for i in range(lons)])


def body(
    field, a_norm_one, a_project, a_bias, a_output, a_norm_two, a_raise, a_lower,
    merge_norm_gain, merge_weight,
    b_norm_one, b_project, b_bias, b_output, b_norm_two, b_raise, b_lower,
    up_first, up_norm, up_second,
):
    levels, rows, columns, width = field.shape
    pairs = levels // WIN_P
    lat_tokens = WIN_P * HALF_LAT * (columns - HALF_LON)
    lon_tokens = WIN_P * (rows - HALF_LAT) * HALF_LON
    diag_tokens = WIN_P * HALF_LAT * HALF_LON
    lat_shape, lon_shape, diag_shape = [packed_shape(n, pairs) for n in (lat_tokens, lon_tokens, diag_tokens)]
    halo_rows = max(lat_shape[1], lon_shape[1])
    tokens = pairs * WIN

    edge = (lax.axis_index("lat") == lax.axis_size("lat") - 1).astype(jnp.int32).reshape(1)
    staging = (3, pairs, halo_rows, MAIN)
    lat, lon, diag = call(
        start_kernel, "start", [field],
        [(lat_shape, BF16), (lon_shape, BF16), (diag_shape, BF16)],
        [(levels * HALF_LAT, columns, width), staging, staging], 16,
    )
    lon = shift(lon, 0, 1)
    lat = shift(lat, 1, 0)
    diag = shift(diag, 1, 1)
    a_heads, b_heads = a_bias.shape[0], b_bias.shape[0]
    square = ((width, width), BF16)
    plain, late, coarse_table, wq, wk, wvt = call(
        table_kernel, "tables", [edge, a_bias, b_bias, a_project],
        [((2, WIN, a_heads * WIN), F32)] * 2 + [((2, WIN, b_heads * WIN), F32)] + [square] * 3,
        [], 24, scalars=1,
    )
    weights = [a_norm_one, wq, wk, wvt, a_output, a_norm_two, a_raise, a_lower.T]
    staging = (4, pairs, halo_rows, MAIN)
    scratch = [(levels * WIN_LAT, columns, width), (tokens, width), staging, staging]
    out = ((tokens, width), F32)
    work = 2 * tokens * width * (4 * width + 8 * width)

    def fine(i, j, halos, outs):
        def kernel(*refs):
            fine_kernel(i, j, *refs)

        operands = [field, *halos, late if i else plain, *weights]
        return call(kernel, f"fine_{i}{j}", operands, [out] + outs, scratch, 24, work)

    w00, diag_two = fine(0, 0, [], [(diag_shape, BF16)])
    diag_two = shift(diag_two, 1, 1)
    w01, lat_two = fine(0, 1, [lon, w00], [(lat_shape, BF16)])
    lat_two = shift(lat_two, 1, 0)
    w10, lon_two = fine(1, 0, [lat, w00], [(lon_shape, BF16)])
    lon_two = shift(lon_two, 0, 1)
    (w11,) = fine(1, 1, [lat, lon, diag], [])

    quarter = packed_shape(WIN, pairs)
    halos = (3, pairs, halo_rows, MAIN)
    quads = (4, pairs, WIN, MAIN)
    lines = (levels * rows * PITCH, MAIN)
    stay, lat, lon, diag = call(
        coarse_kernel, "coarse",
        [
            w00, w01, w10, w11, lat_two, lon_two, diag_two, coarse_table, merge_norm_gain, merge_weight,
            b_norm_one, b_project, b_output, b_norm_two, b_raise, b_lower, up_first, up_norm, up_second,
        ],
        [(quarter, BF16)] * 4,
        [halos, halos, lines, lines, quads, quads, (4, tokens, 2 * MAIN), (tokens, 2 * width), (tokens, 2 * width)],
        48, 8 * work,
    )
    diag = shift(diag, -1, -1)
    lat = shift(lat, -1, 0)
    lon = shift(lon, 0, -1)
    lines = (levels * rows * columns, MAIN)
    (fine_out,) = call(
        finish_kernel, "finish", [diag, lat, lon, stay], [(field.shape, BF16)], [quads, quads, lines, lines], 24
    )
    return fine_out


def solution(mesh):
    in_specs = (P(None, "lat", "lon", None),) + (P(),) * 19
    out_specs = P(None, "lat", "lon", None)
    return jax.shard_map(body, mesh=mesh, in_specs=in_specs, out_specs=out_specs, check_vma=False)
```

```python
import math

import jax
import jax.numpy as jnp
from jax import lax
from jax.experimental import pallas as pl
from jax.experimental.pallas import tpu as pltpu
from jax.sharding import PartitionSpec as P

WIN_P = 2
WIN_LAT = 6
WIN_LON = 12
WIN = WIN_P * WIN_LAT * WIN_LON
HALF_LAT = WIN_LAT // 2
HALF_LON = WIN_LON // 2
HEAD = 32
MAIN = 128
REST = WIN - MAIN
EPS = 1e-05
LOG2E = math.log2(math.e)
EXCLUDED = -1e30
PITCH = 32

F32 = jnp.float32
BF16 = jnp.bfloat16


def dot(a, b, contract=((1,), (0,))):
    return lax.dot_general(a, b, (contract, ((), ())), preferred_element_type=F32)


def layer_norm(values, gain):
    average = jnp.mean(values, axis=-1, keepdims=True)
    centred = values - average
    variance = jnp.mean(centred * centred, axis=-1, keepdims=True)
    return centred * lax.rsqrt(variance + EPS) * gain


def gelu(x):
    return 0.5 * x * (1.0 + lax.erf(x * (1.0 / math.sqrt(2.0))))


def token_index(shape, heads):
    key = lax.broadcasted_iota(jnp.int32, shape, 0)
    column = lax.broadcasted_iota(jnp.int32, shape, 1)
    rest = column - heads * MAIN
    query = jnp.where(rest < 0, jnp.bitwise_and(column, MAIN - 1), MAIN + jnp.bitwise_and(rest, REST - 1))
    return key, query


def level_mask(heads):
    key, query = token_index((WIN, heads * WIN), heads)
    half = WIN // 2
    return jnp.where((key >= half) != (query >= half), EXCLUDED, 0.0)


def lat_mask(heads):
    key, query = token_index((WIN, heads * WIN), heads)
    half, quarter = WIN // 2, WIN // 4

    def late(t):
        return jnp.where(t >= half, t - half, t) >= quarter

    return jnp.where(late(key) != late(query), EXCLUDED, 0.0)


def attend(q, k, vt, table, heads, step):
    width = heads * HEAD
    lane = lax.broadcasted_iota(jnp.int32, (1, MAIN), 1) // HEAD
    zero = jnp.zeros((), BF16)
    pieces = []
    rests = []
    for start in range(0, width, MAIN):
        stop = min(start + MAIN, width)
        span = stop - start
        qs = q[:, start:stop]
        here = span // HEAD
        masked = [jnp.where(lane[:, :span] == h, qs, zero) for h in range(here)]
        rest = jnp.concatenate([m[MAIN:] for m in masked], axis=0)
        ks = k[:, start:stop]
        for h in range(0, here, step):
            main = jnp.concatenate([m[:MAIN] for m in masked[h : h + step]], axis=0)
            pieces.append(dot(ks, main, ((1,), (1,))))
        rests.append(dot(ks, rest, ((1,), (1,))))
    outs = []
    base = 0
    for piece in pieces:
        span = piece.shape[1]
        s = piece + table[:, base : base + span]
        s = s - jnp.max(s, axis=0, keepdims=True)
        e = jnp.exp2(s)
        inv = 1.0 / jnp.sum(e, axis=0, keepdims=True)
        p = e.astype(BF16)
        for h in range(span // MAIN):
            row = base // MAIN + h
            cut = slice(h * MAIN, (h + 1) * MAIN)
            outs.append(dot(vt[row * HEAD : (row + 1) * HEAD], p[:, cut]) * inv[:, cut])
        base += span
    main_out = jnp.concatenate(outs, axis=0)
    s = jnp.concatenate(rests, axis=1) + table[:, base:]
    s = s - jnp.max(s, axis=0, keepdims=True)
    e = jnp.exp2(s)
    inv = 1.0 / jnp.sum(e, axis=0, keepdims=True)
    full = dot(vt, e.astype(BF16)) * inv
    row = lax.broadcasted_iota(jnp.int32, full.shape, 0) // HEAD
    column = lax.broadcasted_iota(jnp.int32, full.shape, 1) // REST
    full = jnp.where(row == column, full, 0.0).astype(BF16)
    fold_row = lax.broadcasted_iota(jnp.int32, (heads * REST, REST), 0)
    fold_column = lax.broadcasted_iota(jnp.int32, (heads * REST, REST), 1)
    fold = jnp.where(jnp.bitwise_and(fold_row, REST - 1) == fold_column, 1.0, 0.0).astype(BF16)
    rest_out = dot(full, fold)
    return jnp.concatenate([main_out.astype(BF16), rest_out.astype(BF16)], axis=1)


def block_rows(x_ref, count, table_ref, heads, gain_one, wq, wk, wvt, wo, gain_two, w1, w2, w2_dims, out_ref):
    x = x_ref[...]
    xn = layer_norm(x, gain_one[...][None, :]).astype(BF16)
    q = (dot(xn, wq) * (LOG2E / math.sqrt(HEAD))).astype(BF16)
    k = dot(xn, wk).astype(BF16)
    mixed = []
    for w in range(count):
        rows = slice(w * WIN, (w + 1) * WIN)
        vt = dot(wvt, xn[rows], ((1,), (1,))).astype(BF16)
        table = table_ref.at[1 if w == count - 1 else 0]
        attended = attend(q[rows], k[rows], vt, table, heads, 4 if heads == 6 else 2)
        mixed.append(dot(attended, wo[...], ((0,), (0,))))
    after = (x + jnp.concatenate(mixed, axis=0)).astype(BF16).astype(F32)
    normed = layer_norm(after, gain_two[...][None, :]).astype(BF16)
    hidden = gelu(dot(normed, w1[...])).astype(BF16)
    out_ref[...] = (after + dot(hidden, w2[...], w2_dims)).astype(BF16).astype(F32)


class Packed:
    def __init__(self, low_ref, high_ref, rows):
        self.low, self.high, self.rows = low_ref, high_ref, rows
        self.pairs = low_ref.shape[0]

    def put(self, p, at, value):
        n = value.shape[0]
        self.low[p, at : at + n, :] = value[:, :MAIN]
        self.high[p, at : at + n, : value.shape[1] - MAIN] = value[:, MAIN:]

    def get(self, p, at, n):
        return jnp.concatenate([self.low[p, at : at + n, :], self.high[p, at : at + n, : MAIN // 2]], axis=1)

    def store(self, out_ref):
        half = self.pairs // 2
        rows = slice(0, self.rows)
        for p in range(self.pairs):
            out_ref[p] = self.low[p, rows, :].astype(BF16)
        for p in range(half):
            sides = [self.high[p + s * half, rows, : MAIN // 2] for s in range(2)]
            out_ref[self.pairs + p] = jnp.concatenate(sides, axis=1).astype(BF16)

    def load(self, in_ref):
        half = self.pairs // 2
        rows = slice(0, self.rows)
        for p in range(self.pairs):
            self.low[p, rows, :] = in_ref[p].astype(F32)
        for p in range(half):
            both = in_ref[self.pairs + p].astype(F32)
            for s in range(2):
                self.high[p + s * half, rows, : MAIN // 2] = both[:, s * MAIN // 2 : (s + 1) * MAIN // 2]
        return self


def packed_rows(tokens):
    return -(-tokens // 16) * 16


def pair_levels(p, levels):
    return [(WIN_P * p + WIN_P // 2 + lev) % levels for lev in range(WIN_P)]


def pack_lon(field, out_ref, low_ref, high_ref):
    levels, rows, _, _ = field.shape
    send = Packed(low_ref, high_ref, out_ref.shape[1])
    for p in range(levels // WIN_P):
        for lev, level in enumerate(pair_levels(p, levels)):
            for r in range(rows):
                send.put(p, (lev * rows + r) * HALF_LON, field[level, r, :8].astype(F32)[:HALF_LON])
    send.store(out_ref)


def pack_lat(field, lon_in, out_ref, line_ref, low_ref, high_ref):
    levels, rows, columns, _ = field.shape
    lon = Packed(low_ref.at[0], high_ref.at[0], lon_in.shape[1]).load(lon_in)
    send = Packed(low_ref.at[1], high_ref.at[1], out_ref.shape[1])
    for p in range(levels // WIN_P):
        for lev, level in enumerate(pair_levels(p, levels)):
            for r in range(HALF_LAT):
                slot = level * HALF_LAT + r
                at = (lev * HALF_LAT + r) * columns
                line_ref[slot] = field[level, r].astype(F32)
                send.put(p, at, line_ref[slot, HALF_LON:, :])
                send.put(p, at + columns - HALF_LON, lon.get(p, (lev * rows + r) * HALF_LON, HALF_LON))
    send.store(out_ref)


def pack_second(w00, w10, lat_in, out_ref, low_ref, high_ref):
    rows, columns = 2 * WIN_LAT, 2 * WIN_LON
    lat = Packed(low_ref.at[0], high_ref.at[0], lat_in.shape[1]).load(lat_in)
    send = Packed(low_ref.at[1], high_ref.at[1], out_ref.shape[1])
    for p in range(w00.shape[0] // WIN):
        for lev in range(WIN_P):
            for r in range(rows):
                row = r + HALF_LAT
                if row < rows:
                    source = (w00, w10)[row // WIN_LAT]
                    here = ((p * WIN_P + lev) * WIN_LAT + row % WIN_LAT) * WIN_LON
                    value = source[here : here + HALF_LON, :]
                else:
                    value = lat.get(p, (lev * HALF_LAT + row - rows) * columns, HALF_LON)
                send.put(p, (lev * rows + r) * HALF_LON, value)
    send.store(out_ref)


def table_kernel(edge_ref, bias, *outs):
    heads = bias.shape[0]
    out = outs[0]
    for h in range(heads):
        turned = (bias[h] * LOG2E).T
        out[0, :, h * MAIN : (h + 1) * MAIN] = turned[:, :MAIN]
        out[0, :, heads * MAIN + h * REST : heads * MAIN + (h + 1) * REST] = turned[:, MAIN:]
    level = level_mask(heads)
    late = lat_mask(heads) * edge_ref[0].astype(F32)
    outs[-1][0] = out[0] + late
    for ref in outs:
        ref[1] = ref[0] + level


def fine_table_kernel(edge_ref, bias, project, plain_ref, late_ref, wq_ref, wk_ref, wvt_ref):
    table_kernel(edge_ref, bias, plain_ref, late_ref)
    width = wq_ref.shape[0]
    wq_ref[...] = project[:, :width]
    wk_ref[...] = project[:, width : 2 * width]
    wvt_ref[...] = project[:, 2 * width :].astype(F32).T.astype(BF16)


def fine_kernel(i, j, *refs):
    refs = list(refs)
    field = refs.pop(0)
    lat_in = refs.pop(0) if i else None
    lon_in = refs.pop(0) if j else None
    sends = j and not i
    first = refs.pop(0) if sends else None
    table_ref, gain_one, wq, wk, wvt, wo, gain_two, w1, w2t, out_ref = refs[:10]
    refs = refs[10:]
    send_ref = refs.pop(0) if sends else None
    line_ref, x_ref, low_ref, high_ref = refs
    levels, rows, columns, _ = field.shape
    pairs = levels // WIN_P
    lat, lon = [
        Packed(low_ref.at[n], high_ref.at[n], ref.shape[1]).load(ref) if ref is not None else None
        for n, ref in enumerate((lat_in, lon_in))
    ]
    at = 0
    slot = 0
    start = HALF_LON + j * WIN_LON
    own = min(columns - start, WIN_LON)
    for p in range(pairs):
        for lev, level in enumerate(pair_levels(p, levels)):
            for row in range(i * WIN_LAT + HALF_LAT, (i + 1) * WIN_LAT + HALF_LAT):
                if row < rows:
                    line_ref[slot] = field[level, row].astype(F32)
                    x_ref[at : at + own, :] = line_ref[slot, start : start + own, :]
                    slot += 1
                    if own < WIN_LON:
                        x_ref[at + own : at + WIN_LON, :] = lon.get(p, (lev * rows + row) * HALF_LON, HALF_LON)
                else:
                    below = lev * HALF_LAT + row - rows
                    x_ref[at : at + WIN_LON, :] = lat.get(p, below * columns + j * WIN_LON, WIN_LON)
                at += WIN_LON
    block_rows(
        x_ref, pairs, table_ref, 6, gain_one, wq[...], wk[...], wvt[...], wo, gain_two, w1, w2t, ((1,), (1,)), out_ref
    )
    if not sends:
        return
    send = Packed(low_ref.at[0], high_ref.at[0], send_ref.shape[1])
    for p in range(pairs):
        for lev in range(WIN_P):
            for row in range(HALF_LAT):
                at = (lev * HALF_LAT + row) * columns
                here = ((p * WIN_P + lev) * WIN_LAT + row) * WIN_LON
                send.put(p, at, first[here : here + WIN_LON, :])
                send.put(p, at + WIN_LON, out_ref[here : here + WIN_LON, :])
    send.store(send_ref)


def coarse_kernel(
    w00, w01, w10, w11, lat_in, lon_in, table_ref,
    merge_gain, merge_weight,
    gain_one, project, wo, gain_two, w1, w2,
    up_first, up_norm, up_second,
    stay_ref, to_lat_ref, to_lon_ref, to_diag_ref,
    low_ref, high_ref, grid_low, grid_high, quad_low, quad_high, parts_ref, x_ref, y_ref,
):
    heads = 12
    width = w00.shape[1]
    rows, columns = 2 * WIN_LAT, 2 * WIN_LON
    pairs = w00.shape[0] // WIN
    levels = pairs * WIN_P
    windows = ((w00, w01), (w10, w11))
    lat, lon = [Packed(low_ref.at[n], high_ref.at[n], ref.shape[1]).load(ref) for n, ref in enumerate((lat_in, lon_in))]

    def put(at, value):
        grid_low[at : at + value.shape[0], :] = value[:, :MAIN]
        grid_high[at : at + value.shape[0], : width - MAIN] = value[:, MAIN:]

    for p in range(pairs):
        for lev in range(WIN_P):
            for row in range(rows):
                at = ((p * WIN_P + lev) * rows + row) * PITCH
                if row + HALF_LAT < rows:
                    left, right = windows[(row + HALF_LAT) // WIN_LAT]
                    here = ((p * WIN_P + lev) * WIN_LAT + (row + HALF_LAT) % WIN_LAT) * WIN_LON
                    put(at + HALF_LON, left[here + HALF_LON : here + WIN_LON, :])
                    put(at + WIN_LON, right[here : here + WIN_LON, :])
                else:
                    below = lev * HALF_LAT + row + HALF_LAT - rows
                    put(at + HALF_LON, lat.get(p, below * columns + HALF_LON, columns - HALF_LON))
                put(at + columns, lon.get(p, (lev * rows + row) * HALF_LON, HALF_LON))
    for r in range(2):
        for t in range(2):
            n = 2 * r + t
            at = 0
            for level in range(levels):
                for a in range(rows // 2):
                    start = (level * rows + 2 * a + r) * PITCH + HALF_LON + t
                    parts_ref[n, at : at + WIN_LON, :MAIN] = grid_low[pl.ds(start, WIN_LON, stride=2), :]
                    parts_ref[n, at : at + WIN_LON, MAIN:] = grid_high[pl.ds(start, WIN_LON, stride=2), :]
                    at += WIN_LON
    parts = [parts_ref[n, :, :width] for n in range(4)]
    average = jnp.sum(parts[0] + parts[1] + parts[2] + parts[3], axis=-1, keepdims=True) * (1.0 / (4 * width))
    centred = [part - average for part in parts]
    squares = centred[0] * centred[0]
    for c in centred[1:]:
        squares += c * c
    scale = lax.rsqrt(jnp.sum(squares, axis=-1, keepdims=True) * (1.0 / (4 * width)) + EPS)
    total = None
    for n in range(4):
        gain = merge_gain[n * width : (n + 1) * width][None, :]
        normed = (centred[n] * scale * gain).astype(BF16)
        term = dot(normed, merge_weight[n * width : (n + 1) * width, :])
        total = term if total is None else total + term
    x_ref[...] = total.astype(BF16).astype(F32)
    double = 2 * width
    wvt = project[:, 2 * double :].astype(F32).T.astype(BF16)
    block_rows(
        x_ref, pairs, table_ref, heads, gain_one, project[:, :double], project[:, double : 2 * double], wvt,
        wo, gain_two, w1, w2, ((1,), (0,)), y_ref,
    )
    coarse = y_ref[...].astype(BF16)
    half = rows // 2
    for r in range(2):
        for t in range(2):
            n = 2 * r + t
            raised = dot(coarse, up_first[:, n * width : (n + 1) * width]).astype(BF16).astype(F32)
            normed = layer_norm(raised, up_norm[...][None, :]).astype(BF16)
            parts_ref[n, :, :width] = parts_ref[n, :, :width] + dot(normed, up_second[...])
            for level in range(levels):
                for a in range(half):
                    row = 2 * a + r
                    for side in range(2):
                        at = (level * half + a) * WIN_LON + side * HALF_LON
                        quad, p = 2 * (row // half) + side, level // WIN_P
                        start = (level % WIN_P * half + row % half) * WIN_LON + t
                        to = pl.ds(start, HALF_LON, stride=2)
                        quad_low[quad, p, to, :] = parts_ref[n, at : at + HALF_LON, :MAIN]
                        quad_high[quad, p, to, :] = parts_ref[n, at : at + HALF_LON, MAIN:]
    for quad, ref in enumerate((stay_ref, to_lon_ref, to_lat_ref, to_diag_ref)):
        Packed(quad_low.at[quad], quad_high.at[quad], WIN).store(ref)


def finish_kernel(upper_left, upper_right, lower_left, lower_right, out_ref, low_ref, high_ref, line_low, line_high):
    levels, rows, columns, width = out_ref.shape
    half = rows // 2
    for quad, ref in enumerate((upper_left, upper_right, lower_left, lower_right)):
        pack = Packed(low_ref.at[quad], high_ref.at[quad], WIN).load(ref)
        for p in range(levels // WIN_P):
            for lev, level in enumerate(pair_levels(p, levels)):
                for row in range(half):
                    at = (level * rows + (quad // 2) * half + row) * columns + quad % 2 * WIN_LON
                    here = (lev * half + row) * WIN_LON
                    line_low[at : at + WIN_LON, :] = pack.low[p, here : here + WIN_LON, :]
                    line_high[at : at + WIN_LON, :] = pack.high[p, here : here + WIN_LON, :]
    for level in range(levels):
        for row in range(rows):
            at = (level * rows + row) * columns
            out_ref[level, row, :, :MAIN] = line_low[at : at + columns, :].astype(BF16)
            out_ref[level, row, :, MAIN:] = line_high[at : at + columns, : width - MAIN].astype(BF16)


MIB = 1024 * 1024


def call(kernel, name, operands, outs, scratch, limit, scalars=0):
    vmem = pl.BlockSpec(memory_space=pltpu.VMEM)
    smem = pl.BlockSpec(memory_space=pltpu.SMEM)
    return pl.pallas_call(
        kernel,
        in_specs=[smem] * scalars + [vmem] * (len(operands) - scalars),
        out_specs=[vmem] * len(outs),
        out_shape=[jax.ShapeDtypeStruct(s, d) for s, d in outs],
        scratch_shapes=[pltpu.VMEM(s, F32) for s in scratch],
        compiler_params=pltpu.CompilerParams(vmem_limit_bytes=limit * MIB),
        cost_estimate=pl.CostEstimate(flops=0, bytes_accessed=0, transcendentals=0),
        name=name,
    )(*operands)


def packed_shape(tokens, pairs):
    return (pairs * 3 // 2, packed_rows(tokens), MAIN)


def shift(array, lat_by, lon_by):
    lats, lons = lax.axis_size("lat"), lax.axis_size("lon")
    if lat_by and lon_by:
        pairs = [
            (((a + lat_by) % lats) * lons + (b + lon_by) % lons, a * lons + b)
            for a in range(lats)
            for b in range(lons)
        ]
        return lax.ppermute(array, ("lat", "lon"), pairs)
    if lat_by:
        return lax.ppermute(array, "lat", [((i + lat_by) % lats, i) for i in range(lats)])
    return lax.ppermute(array, "lon", [((i + lon_by) % lons, i) for i in range(lons)])


def body(
    field, a_norm_one, a_project, a_bias, a_output, a_norm_two, a_raise, a_lower,
    merge_norm_gain, merge_weight,
    b_norm_one, b_project, b_bias, b_output, b_norm_two, b_raise, b_lower,
    up_first, up_norm, up_second,
):
    levels, rows, columns, width = field.shape
    pairs = levels // WIN_P
    halo = packed_shape(WIN, pairs)
    staging = (pairs, WIN, MAIN)
    both = (2,) + staging
    tokens = pairs * WIN

    edge = (lax.axis_index("lat") == lax.axis_size("lat") - 1).astype(jnp.int32).reshape(1)
    (lon,) = call(pack_lon, "pack_lon", [field], [(halo, BF16)], [staging, staging], 16)
    lon = shift(lon, 0, 1)
    a_heads, b_heads = a_bias.shape[0], b_bias.shape[0]
    square = ((width, width), BF16)
    plain, late, wq, wk, wvt = call(
        fine_table_kernel, "fine_tables", [edge, a_bias, a_project],
        [((2, WIN, a_heads * WIN), F32)] * 2 + [square] * 3, [], 16, scalars=1,
    )
    weights = [a_norm_one, wq, wk, wvt, a_output, a_norm_two, a_raise, a_lower.T]
    scratch = [(levels * WIN_LAT, columns, width), (tokens, width), both, both]
    out = ((tokens, width), F32)

    def fine(i, j, halos, outs):
        def kernel(*refs):
            fine_kernel(i, j, *refs)

        operands = [field, *halos, late if i else plain, *weights]
        return call(kernel, f"fine_{i}{j}", operands, [out] + outs, scratch, 20)

    (w00,) = fine(0, 0, [], [])
    lon, w00 = lax.optimization_barrier((lon, w00))
    lines = (levels * HALF_LAT, columns, width)
    (lat,) = call(pack_lat, "pack_lat", [field, lon], [(halo, BF16)], [lines, both, both], 16)
    lon, lat = lax.optimization_barrier((lon, lat))
    lat = shift(lat, 1, 0)
    w01, lat_two = fine(0, 1, [lon, w00], [(halo, BF16)])
    lat, lat_two = lax.optimization_barrier((lat, lat_two))
    lat_two = shift(lat_two, 1, 0)
    (w10,) = fine(1, 0, [lat], [])
    lat_two, w10 = lax.optimization_barrier((lat_two, w10))
    (lon_two,) = call(pack_second, "pack_second", [w00, w10, lat_two], [(halo, BF16)], [both, both], 16)
    lon, lon_two = lax.optimization_barrier((lon, lon_two))
    lon_two = shift(lon_two, 0, 1)
    (w11,) = fine(1, 1, [lat, lon], [])
    late_bias, w11 = lax.optimization_barrier((b_bias, w11))
    (coarse_table,) = call(
        table_kernel, "coarse_table", [edge, late_bias], [((2, WIN, b_heads * WIN), F32)], [], 16, scalars=1
    )

    quads = (4,) + staging
    lines = (levels * rows * PITCH, MAIN)
    stay, lat, lon, diag = call(
        coarse_kernel, "coarse",
        [
            w00, w01, w10, w11, lat_two, lon_two, coarse_table, merge_norm_gain, merge_weight,
            b_norm_one, b_project, b_output, b_norm_two, b_raise, b_lower, up_first, up_norm, up_second,
        ],
        [(halo, BF16)] * 4,
        [both, both, lines, lines, quads, quads, (4, tokens, 2 * MAIN), (tokens, 2 * width), (tokens, 2 * width)],
        32,
    )
    diag = shift(diag, -1, -1)
    lat = shift(lat, -1, 0)
    lon = shift(lon, 0, -1)
    lines = (levels * rows * columns, MAIN)
    (fine_out,) = call(
        finish_kernel, "finish", [diag, lat, lon, stay], [(field.shape, BF16)], [quads, quads, lines, lines], 24
    )
    return fine_out


def solution(mesh):
    in_specs = (P(None, "lat", "lon", None),) + (P(),) * 19
    out_specs = P(None, "lat", "lon", None)
    return jax.shard_map(body, mesh=mesh, in_specs=in_specs, out_specs=out_specs, check_vma=False)
```

```python
import math

import jax
import jax.numpy as jnp
from jax import lax
from jax.experimental import pallas as pl
from jax.experimental.pallas import tpu as pltpu
from jax.sharding import PartitionSpec as P

WIN_P = 2
WIN_LAT = 6
WIN_LON = 12
WIN = WIN_P * WIN_LAT * WIN_LON
HALF_LAT = WIN_LAT // 2
HALF_LON = WIN_LON // 2
HEAD = 32
MAIN = 128
REST = WIN - MAIN
EPS = 1e-05
LOG2E = math.log2(math.e)
EXCLUDED = -1e30
PITCH = 32

F32 = jnp.float32
BF16 = jnp.bfloat16


def dot(a, b, contract=((1,), (0,))):
    return lax.dot_general(a, b, (contract, ((), ())), preferred_element_type=F32)


def layer_norm(values, gain):
    average = jnp.mean(values, axis=-1, keepdims=True)
    centred = values - average
    variance = jnp.mean(centred * centred, axis=-1, keepdims=True)
    return centred * lax.rsqrt(variance + EPS) * gain


def gelu(x):
    return 0.5 * x * (1.0 + lax.erf(x * (1.0 / math.sqrt(2.0))))


def token_index(shape, heads):
    key = lax.broadcasted_iota(jnp.int32, shape, 0)
    column = lax.broadcasted_iota(jnp.int32, shape, 1)
    rest = column - heads * MAIN
    query = jnp.where(rest < 0, jnp.bitwise_and(column, MAIN - 1), MAIN + jnp.bitwise_and(rest, REST - 1))
    return key, query


def level_mask(heads):
    key, query = token_index((WIN, heads * WIN), heads)
    half = WIN // 2
    return jnp.where((key >= half) != (query >= half), EXCLUDED, 0.0)


def lat_mask(heads):
    key, query = token_index((WIN, heads * WIN), heads)
    half, quarter = WIN // 2, WIN // 4

    def late(t):
        return jnp.where(t >= half, t - half, t) >= quarter

    return jnp.where(late(key) != late(query), EXCLUDED, 0.0)


def attend(q, k, vt, table, heads, step):
    width = heads * HEAD
    lane = lax.broadcasted_iota(jnp.int32, (1, MAIN), 1) // HEAD
    zero = jnp.zeros((), BF16)
    pieces = []
    rests = []
    for start in range(0, width, MAIN):
        stop = min(start + MAIN, width)
        span = stop - start
        qs = q[:, start:stop]
        here = span // HEAD
        masked = [jnp.where(lane[:, :span] == h, qs, zero) for h in range(here)]
        rest = jnp.concatenate([m[MAIN:] for m in masked], axis=0)
        ks = k[:, start:stop]
        for h in range(0, here, step):
            main = jnp.concatenate([m[:MAIN] for m in masked[h : h + step]], axis=0)
            pieces.append(dot(ks, main, ((1,), (1,))))
        rests.append(dot(ks, rest, ((1,), (1,))))
    outs = []
    base = 0
    for piece in pieces:
        span = piece.shape[1]
        s = piece + table[:, base : base + span]
        s = s - jnp.max(s, axis=0, keepdims=True)
        e = jnp.exp2(s)
        inv = 1.0 / jnp.sum(e, axis=0, keepdims=True)
        p = e.astype(BF16)
        for h in range(span // MAIN):
            row = base // MAIN + h
            cut = slice(h * MAIN, (h + 1) * MAIN)
            outs.append(dot(vt[row * HEAD : (row + 1) * HEAD], p[:, cut]) * inv[:, cut])
        base += span
    main_out = jnp.concatenate(outs, axis=0)
    s = jnp.concatenate(rests, axis=1) + table[:, base:]
    s = s - jnp.max(s, axis=0, keepdims=True)
    e = jnp.exp2(s)
    inv = 1.0 / jnp.sum(e, axis=0, keepdims=True)
    full = dot(vt, e.astype(BF16)) * inv
    row = lax.broadcasted_iota(jnp.int32, full.shape, 0) // HEAD
    column = lax.broadcasted_iota(jnp.int32, full.shape, 1) // REST
    full = jnp.where(row == column, full, 0.0).astype(BF16)
    fold_row = lax.broadcasted_iota(jnp.int32, (heads * REST, REST), 0)
    fold_column = lax.broadcasted_iota(jnp.int32, (heads * REST, REST), 1)
    fold = jnp.where(jnp.bitwise_and(fold_row, REST - 1) == fold_column, 1.0, 0.0).astype(BF16)
    rest_out = dot(full, fold)
    return jnp.concatenate([main_out.astype(BF16), rest_out.astype(BF16)], axis=1)


def block_rows(x_ref, count, table_ref, heads, gain_one, wq, wk, wvt, wo, gain_two, w1, w2, w2_dims, out_ref):
    x = x_ref[...]
    xn = layer_norm(x, gain_one[...][None, :]).astype(BF16)
    q = (dot(xn, wq) * (LOG2E / math.sqrt(HEAD))).astype(BF16)
    k = dot(xn, wk).astype(BF16)
    mixed = []
    for w in range(count):
        rows = slice(w * WIN, (w + 1) * WIN)
        vt = dot(wvt, xn[rows], ((1,), (1,))).astype(BF16)
        table = table_ref.at[1 if w == count - 1 else 0]
        attended = attend(q[rows], k[rows], vt, table, heads, 4 if heads == 6 else 2)
        mixed.append(dot(attended, wo[...], ((0,), (0,))))
    after = (x + jnp.concatenate(mixed, axis=0)).astype(BF16).astype(F32)
    normed = layer_norm(after, gain_two[...][None, :]).astype(BF16)
    hidden = gelu(dot(normed, w1[...])).astype(BF16)
    out_ref[...] = (after + dot(hidden, w2[...], w2_dims)).astype(BF16).astype(F32)


class Packed:
    def __init__(self, low_ref, high_ref, rows):
        self.low, self.high, self.rows = low_ref, high_ref, rows
        self.pairs = low_ref.shape[0]

    def put(self, p, at, value):
        n = value.shape[0]
        self.low[p, at : at + n, :] = value[:, :MAIN]
        self.high[p, at : at + n, : value.shape[1] - MAIN] = value[:, MAIN:]

    def get(self, p, at, n):
        return jnp.concatenate([self.low[p, at : at + n, :], self.high[p, at : at + n, : MAIN // 2]], axis=1)

    def store(self, out_ref):
        half = self.pairs // 2
        rows = slice(0, self.rows)
        for p in range(self.pairs):
            out_ref[p] = self.low[p, rows, :].astype(BF16)
        for p in range(half):
            sides = [self.high[p + s * half, rows, : MAIN // 2] for s in range(2)]
            out_ref[self.pairs + p] = jnp.concatenate(sides, axis=1).astype(BF16)

    def load(self, in_ref):
        half = self.pairs // 2
        rows = slice(0, self.rows)
        for p in range(self.pairs):
            self.low[p, rows, :] = in_ref[p].astype(F32)
        for p in range(half):
            both = in_ref[self.pairs + p].astype(F32)
            for s in range(2):
                self.high[p + s * half, rows, : MAIN // 2] = both[:, s * MAIN // 2 : (s + 1) * MAIN // 2]
        return self


def packed_rows(tokens):
    return -(-tokens // 16) * 16


def pair_levels(p, levels):
    return [(WIN_P * p + WIN_P // 2 + lev) % levels for lev in range(WIN_P)]


def start_kernel(field, lat_ref, lon_ref, diag_ref, line_ref, low_ref, high_ref):
    levels, rows, columns, _ = field.shape
    packs = [Packed(low_ref.at[n], high_ref.at[n], ref.shape[1]) for n, ref in enumerate((lat_ref, lon_ref, diag_ref))]
    lat, lon, diag = packs
    for p in range(levels // WIN_P):
        for lev, level in enumerate(pair_levels(p, levels)):
            for r in range(rows):
                line = field[level, r].astype(F32)
                if r < HALF_LAT:
                    slot = level * HALF_LAT + r
                    line_ref[slot] = line
                    diag.put(p, (lev * HALF_LAT + r) * HALF_LON, line[:HALF_LON])
                    span = columns - HALF_LON
                    lat.put(p, (lev * HALF_LAT + r) * span, line_ref[slot, HALF_LON:, :])
                else:
                    lon.put(p, (lev * (rows - HALF_LAT) + r - HALF_LAT) * HALF_LON, line[:HALF_LON])
    for pack, ref in zip(packs, (lat_ref, lon_ref, diag_ref)):
        pack.store(ref)


def pack_second(w00, w10, lat_in, out_ref, low_ref, high_ref):
    rows, columns = 2 * WIN_LAT, 2 * WIN_LON
    lat = Packed(low_ref.at[0], high_ref.at[0], lat_in.shape[1]).load(lat_in)
    send = Packed(low_ref.at[1], high_ref.at[1], out_ref.shape[1])
    for p in range(w00.shape[0] // WIN):
        for lev in range(WIN_P):
            for r in range(rows):
                row = r + HALF_LAT
                if row < rows:
                    source = (w00, w10)[row // WIN_LAT]
                    here = ((p * WIN_P + lev) * WIN_LAT + row % WIN_LAT) * WIN_LON
                    value = source[here : here + HALF_LON, :]
                else:
                    value = lat.get(p, (lev * HALF_LAT + row - rows) * columns, HALF_LON)
                send.put(p, (lev * rows + r) * HALF_LON, value)
    send.store(out_ref)


def table_kernel(edge_ref, bias, *outs):
    heads = bias.shape[0]
    out = outs[0]
    for h in range(heads):
        turned = (bias[h] * LOG2E).T
        out[0, :, h * MAIN : (h + 1) * MAIN] = turned[:, :MAIN]
        out[0, :, heads * MAIN + h * REST : heads * MAIN + (h + 1) * REST] = turned[:, MAIN:]
    level = level_mask(heads)
    late = lat_mask(heads) * edge_ref[0].astype(F32)
    outs[-1][0] = out[0] + late
    for ref in outs:
        ref[1] = ref[0] + level


def fine_table_kernel(edge_ref, bias, project, plain_ref, late_ref, wq_ref, wk_ref, wvt_ref):
    table_kernel(edge_ref, bias, plain_ref, late_ref)
    width = wq_ref.shape[0]
    wq_ref[...] = project[:, :width]
    wk_ref[...] = project[:, width : 2 * width]
    wvt_ref[...] = project[:, 2 * width :].astype(F32).T.astype(BF16)


def fine_kernel(i, j, *refs):
    refs = list(refs)
    field = refs.pop(0)
    lat_in = refs.pop(0) if i else None
    lon_in = refs.pop(0) if j else None
    diag_in = refs.pop(0) if i and j else None
    sends = j and not i
    first = refs.pop(0) if sends else None
    table_ref, gain_one, wq, wk, wvt, wo, gain_two, w1, w2t, out_ref = refs[:10]
    refs = refs[10:]
    send_ref = refs.pop(0) if sends else None
    line_ref, x_ref, low_ref, high_ref = refs
    levels, rows, columns, _ = field.shape
    pairs = levels // WIN_P
    lat, lon, diag = [
        Packed(low_ref.at[n], high_ref.at[n], ref.shape[1]).load(ref) if ref is not None else None
        for n, ref in enumerate((lat_in, lon_in, diag_in))
    ]
    at = 0
    slot = 0
    start = HALF_LON + j * WIN_LON
    own = min(columns - start, WIN_LON)
    for p in range(pairs):
        for lev, level in enumerate(pair_levels(p, levels)):
            for row in range(i * WIN_LAT + HALF_LAT, (i + 1) * WIN_LAT + HALF_LAT):
                if row < rows:
                    line_ref[slot] = field[level, row].astype(F32)
                    x_ref[at : at + own, :] = line_ref[slot, start : start + own, :]
                    slot += 1
                    if own < WIN_LON:
                        late = lev * (rows - HALF_LAT) + row - HALF_LAT
                        x_ref[at + own : at + WIN_LON, :] = lon.get(p, late * HALF_LON, HALF_LON)
                else:
                    below = lev * HALF_LAT + row - rows
                    x_ref[at : at + own, :] = lat.get(p, below * (columns - HALF_LON) + j * WIN_LON, own)
                    if own < WIN_LON:
                        x_ref[at + own : at + WIN_LON, :] = diag.get(p, below * HALF_LON, HALF_LON)
                at += WIN_LON
    block_rows(
        x_ref, pairs, table_ref, 6, gain_one, wq[...], wk[...], wvt[...], wo, gain_two, w1, w2t, ((1,), (1,)), out_ref
    )
    if not sends:
        return
    send = Packed(low_ref.at[0], high_ref.at[0], send_ref.shape[1])
    for p in range(pairs):
        for lev in range(WIN_P):
            for row in range(HALF_LAT):
                at = (lev * HALF_LAT + row) * columns
                here = ((p * WIN_P + lev) * WIN_LAT + row) * WIN_LON
                send.put(p, at, first[here : here + WIN_LON, :])
                send.put(p, at + WIN_LON, out_ref[here : here + WIN_LON, :])
    send.store(send_ref)


def coarse_kernel(
    w00, w01, w10, w11, lat_in, lon_in, table_ref,
    merge_gain, merge_weight,
    gain_one, project, wo, gain_two, w1, w2,
    up_first, up_norm, up_second,
    stay_ref, to_lat_ref, to_lon_ref, to_diag_ref,
    low_ref, high_ref, grid_low, grid_high, quad_low, quad_high, parts_ref, x_ref, y_ref,
):
    heads = 12
    width = w00.shape[1]
    rows, columns = 2 * WIN_LAT, 2 * WIN_LON
    pairs = w00.shape[0] // WIN
    levels = pairs * WIN_P
    windows = ((w00, w01), (w10, w11))
    lat, lon = [Packed(low_ref.at[n], high_ref.at[n], ref.shape[1]).load(ref) for n, ref in enumerate((lat_in, lon_in))]

    def put(at, value):
        grid_low[at : at + value.shape[0], :] = value[:, :MAIN]
        grid_high[at : at + value.shape[0], : width - MAIN] = value[:, MAIN:]

    for p in range(pairs):
        for lev in range(WIN_P):
            for row in range(rows):
                at = ((p * WIN_P + lev) * rows + row) * PITCH
                if row + HALF_LAT < rows:
                    left, right = windows[(row + HALF_LAT) // WIN_LAT]
                    here = ((p * WIN_P + lev) * WIN_LAT + (row + HALF_LAT) % WIN_LAT) * WIN_LON
                    put(at + HALF_LON, left[here + HALF_LON : here + WIN_LON, :])
                    put(at + WIN_LON, right[here : here + WIN_LON, :])
                else:
                    below = lev * HALF_LAT + row + HALF_LAT - rows
                    put(at + HALF_LON, lat.get(p, below * columns + HALF_LON, columns - HALF_LON))
                put(at + columns, lon.get(p, (lev * rows + row) * HALF_LON, HALF_LON))
    for r in range(2):
        for t in range(2):
            n = 2 * r + t
            at = 0
            for level in range(levels):
                for a in range(rows // 2):
                    start = (level * rows + 2 * a + r) * PITCH + HALF_LON + t
                    parts_ref[n, at : at + WIN_LON, :MAIN] = grid_low[pl.ds(start, WIN_LON, stride=2), :]
                    parts_ref[n, at : at + WIN_LON, MAIN:] = grid_high[pl.ds(start, WIN_LON, stride=2), :]
                    at += WIN_LON
    parts = [parts_ref[n, :, :width] for n in range(4)]
    average = jnp.sum(parts[0] + parts[1] + parts[2] + parts[3], axis=-1, keepdims=True) * (1.0 / (4 * width))
    centred = [part - average for part in parts]
    squares = centred[0] * centred[0]
    for c in centred[1:]:
        squares += c * c
    scale = lax.rsqrt(jnp.sum(squares, axis=-1, keepdims=True) * (1.0 / (4 * width)) + EPS)
    total = None
    for n in range(4):
        gain = merge_gain[n * width : (n + 1) * width][None, :]
        normed = (centred[n] * scale * gain).astype(BF16)
        term = dot(normed, merge_weight[n * width : (n + 1) * width, :])
        total = term if total is None else total + term
    x_ref[...] = total.astype(BF16).astype(F32)
    double = 2 * width
    wvt = project[:, 2 * double :].astype(F32).T.astype(BF16)
    block_rows(
        x_ref, pairs, table_ref, heads, gain_one, project[:, :double], project[:, double : 2 * double], wvt,
        wo, gain_two, w1, w2, ((1,), (0,)), y_ref,
    )
    coarse = y_ref[...].astype(BF16)
    half = rows // 2
    for r in range(2):
        for t in range(2):
            n = 2 * r + t
            raised = dot(coarse, up_first[:, n * width : (n + 1) * width]).astype(BF16).astype(F32)
            normed = layer_norm(raised, up_norm[...][None, :]).astype(BF16)
            parts_ref[n, :, :width] = parts_ref[n, :, :width] + dot(normed, up_second[...])
            for level in range(levels):
                for a in range(half):
                    row = 2 * a + r
                    for side in range(2):
                        at = (level * half + a) * WIN_LON + side * HALF_LON
                        quad, p = 2 * (row // half) + side, level // WIN_P
                        start = (level % WIN_P * half + row % half) * WIN_LON + t
                        to = pl.ds(start, HALF_LON, stride=2)
                        quad_low[quad, p, to, :] = parts_ref[n, at : at + HALF_LON, :MAIN]
                        quad_high[quad, p, to, :] = parts_ref[n, at : at + HALF_LON, MAIN:]
    for quad, ref in enumerate((stay_ref, to_lon_ref, to_lat_ref, to_diag_ref)):
        Packed(quad_low.at[quad], quad_high.at[quad], WIN).store(ref)


def finish_kernel(upper_left, upper_right, lower_left, lower_right, out_ref, low_ref, high_ref, line_low, line_high):
    levels, rows, columns, width = out_ref.shape
    half = rows // 2
    for quad, ref in enumerate((upper_left, upper_right, lower_left, lower_right)):
        pack = Packed(low_ref.at[quad], high_ref.at[quad], WIN).load(ref)
        for p in range(levels // WIN_P):
            for lev, level in enumerate(pair_levels(p, levels)):
                for row in range(half):
                    at = (level * rows + (quad // 2) * half + row) * columns + quad % 2 * WIN_LON
                    here = (lev * half + row) * WIN_LON
                    line_low[at : at + WIN_LON, :] = pack.low[p, here : here + WIN_LON, :]
                    line_high[at : at + WIN_LON, :] = pack.high[p, here : here + WIN_LON, :]
    for level in range(levels):
        for row in range(rows):
            at = (level * rows + row) * columns
            out_ref[level, row, :, :MAIN] = line_low[at : at + columns, :].astype(BF16)
            out_ref[level, row, :, MAIN:] = line_high[at : at + columns, : width - MAIN].astype(BF16)


MIB = 1024 * 1024


def call(kernel, name, operands, outs, scratch, limit, scalars=0, us=1):
    vmem = pl.BlockSpec(memory_space=pltpu.VMEM)
    smem = pl.BlockSpec(memory_space=pltpu.SMEM)
    moved = sum(x.size * x.dtype.itemsize for x in operands) + sum(math.prod(s) * jnp.dtype(d).itemsize for s, d in outs)
    return pl.pallas_call(
        kernel,
        in_specs=[smem] * scalars + [vmem] * (len(operands) - scalars),
        out_specs=[vmem] * len(outs),
        out_shape=[jax.ShapeDtypeStruct(s, d) for s, d in outs],
        scratch_shapes=[pltpu.VMEM(s, F32) for s in scratch],
        compiler_params=pltpu.CompilerParams(vmem_limit_bytes=limit * MIB),
        cost_estimate=pl.CostEstimate(flops=us * 1000 * MIB, bytes_accessed=moved, transcendentals=0),
        name=name,
    )(*operands)


def packed_shape(tokens, pairs):
    return (pairs * 3 // 2, packed_rows(tokens), MAIN)


def shift(array, lat_by, lon_by):
    lats, lons = lax.axis_size("lat"), lax.axis_size("lon")
    if lat_by and lon_by:
        pairs = [
            (((a + lat_by) % lats) * lons + (b + lon_by) % lons, a * lons + b)
            for a in range(lats)
            for b in range(lons)
        ]
        return lax.ppermute(array, ("lat", "lon"), pairs)
    if lat_by:
        return lax.ppermute(array, "lat", [((i + lat_by) % lats, i) for i in range(lats)])
    return lax.ppermute(array, "lon", [((i + lon_by) % lons, i) for i in range(lons)])


def body(
    field, a_norm_one, a_project, a_bias, a_output, a_norm_two, a_raise, a_lower,
    merge_norm_gain, merge_weight,
    b_norm_one, b_project, b_bias, b_output, b_norm_two, b_raise, b_lower,
    up_first, up_norm, up_second,
):
    levels, rows, columns, width = field.shape
    pairs = levels // WIN_P
    halo = packed_shape(WIN, pairs)
    staging = (pairs, WIN, MAIN)
    both = (2,) + staging
    tokens = pairs * WIN

    edge = (lax.axis_index("lat") == lax.axis_size("lat") - 1).astype(jnp.int32).reshape(1)
    lat_shape = packed_shape(WIN_P * HALF_LAT * (columns - HALF_LON), pairs)
    lon_shape = packed_shape(WIN_P * (rows - HALF_LAT) * HALF_LON, pairs)
    diag_shape = packed_shape(WIN_P * HALF_LAT * HALF_LON, pairs)
    lat, lon, diag = call(
        start_kernel, "start", [field], [(lat_shape, BF16), (lon_shape, BF16), (diag_shape, BF16)],
        [(levels * HALF_LAT, columns, width), (3,) + staging, (3,) + staging], 16, us=3,
    )
    lon = shift(lon, 0, 1)
    lat = shift(lat, 1, 0)
    diag = shift(diag, 1, 1)
    a_heads, b_heads = a_bias.shape[0], b_bias.shape[0]
    square = ((width, width), BF16)
    plain, late, wq, wk, wvt = call(
        fine_table_kernel, "fine_tables", [edge, a_bias, a_project],
        [((2, WIN, a_heads * WIN), F32)] * 2 + [square] * 3, [], 16, scalars=1, us=3,
    )
    weights = [a_norm_one, wq, wk, wvt, a_output, a_norm_two, a_raise, a_lower.T]
    scratch = [(levels * WIN_LAT, columns, width), (tokens, width), (3,) + staging, (3,) + staging]
    out = ((tokens, width), F32)

    def fine(i, j, halos, outs):
        def kernel(*refs):
            fine_kernel(i, j, *refs)

        operands = [field, *halos, late if i else plain, *weights]
        return call(kernel, f"fine_{i}{j}", operands, [out] + outs, scratch, 20, us=5)

    (w00,) = fine(0, 0, [], [])
    lon, lat, diag, w00 = lax.optimization_barrier((lon, lat, diag, w00))
    w01, lat_two = fine(0, 1, [lon, w00], [(halo, BF16)])
    lat_two = shift(lat_two, 1, 0)
    lat, w01 = lax.optimization_barrier((lat, w01))
    (w10,) = fine(1, 0, [lat], [])
    lat_two, w10 = lax.optimization_barrier((lat_two, w10))
    (lon_two,) = call(pack_second, "pack_second", [w00, w10, lat_two], [(halo, BF16)], [both, both], 16)
    diag, lon_two = lax.optimization_barrier((diag, lon_two))
    lon_two = shift(lon_two, 0, 1)
    (w11,) = fine(1, 1, [lat, lon, diag], [])
    late_bias, w11 = lax.optimization_barrier((b_bias, w11))
    (coarse_table,) = call(
        table_kernel, "coarse_table", [edge, late_bias], [((2, WIN, b_heads * WIN), F32)], [], 16, scalars=1
    )

    quads = (4,) + staging
    lines = (levels * rows * PITCH, MAIN)
    stay, lat, lon, diag = call(
        coarse_kernel, "coarse",
        [
            w00, w01, w10, w11, lat_two, lon_two, coarse_table, merge_norm_gain, merge_weight,
            b_norm_one, b_project, b_output, b_norm_two, b_raise, b_lower, up_first, up_norm, up_second,
        ],
        [(halo, BF16)] * 4,
        [both, both, lines, lines, quads, quads, (4, tokens, 2 * MAIN), (tokens, 2 * width), (tokens, 2 * width)],
        32, us=12,
    )
    diag = shift(diag, -1, -1)
    lat = shift(lat, -1, 0)
    lon = shift(lon, 0, -1)
    lines = (levels * rows * columns, MAIN)
    (fine_out,) = call(
        finish_kernel, "finish", [diag, lat, lon, stay], [(field.shape, BF16)], [quads, quads, lines, lines], 24
    )
    return fine_out


def solution(mesh):
    in_specs = (P(None, "lat", "lon", None),) + (P(),) * 19
    out_specs = P(None, "lat", "lon", None)
    return jax.shard_map(body, mesh=mesh, in_specs=in_specs, out_specs=out_specs, check_vma=False)
```

```python
import math

import jax
import jax.numpy as jnp
from jax import lax
from jax.experimental import pallas as pl
from jax.experimental.pallas import tpu as pltpu
from jax.sharding import PartitionSpec as P

WIN_P = 2
WIN_LAT = 6
WIN_LON = 12
WIN = WIN_P * WIN_LAT * WIN_LON
HALF_LAT = WIN_LAT // 2
HALF_LON = WIN_LON // 2
HEAD = 32
MAIN = 128
REST = WIN - MAIN
EPS = 1e-05
LOG2E = math.log2(math.e)
EXCLUDED = -1e30
PITCH = 32

F32 = jnp.float32
BF16 = jnp.bfloat16


def dot(a, b, contract=((1,), (0,))):
    return lax.dot_general(a, b, (contract, ((), ())), preferred_element_type=F32)


def layer_norm(values, gain):
    average = jnp.mean(values, axis=-1, keepdims=True)
    centred = values - average
    variance = jnp.mean(centred * centred, axis=-1, keepdims=True)
    return centred * lax.rsqrt(variance + EPS) * gain


def gelu(x):
    return 0.5 * x * (1.0 + lax.erf(x * (1.0 / math.sqrt(2.0))))


def token_index(shape, heads):
    key = lax.broadcasted_iota(jnp.int32, shape, 0)
    column = lax.broadcasted_iota(jnp.int32, shape, 1)
    rest = column - heads * MAIN
    query = jnp.where(rest < 0, jnp.bitwise_and(column, MAIN - 1), MAIN + jnp.bitwise_and(rest, REST - 1))
    return key, query


def level_mask(heads):
    key, query = token_index((WIN, heads * WIN), heads)
    half = WIN // 2
    return jnp.where((key >= half) != (query >= half), EXCLUDED, 0.0)


def lat_mask(heads):
    key, query = token_index((WIN, heads * WIN), heads)
    half, quarter = WIN // 2, WIN // 4

    def late(t):
        return jnp.where(t >= half, t - half, t) >= quarter

    return jnp.where(late(key) != late(query), EXCLUDED, 0.0)


def attend(q, k, vt, table, heads, step):
    width = heads * HEAD
    lane = lax.broadcasted_iota(jnp.int32, (1, MAIN), 1) // HEAD
    zero = jnp.zeros((), BF16)
    pieces = []
    rests = []
    for start in range(0, width, MAIN):
        stop = min(start + MAIN, width)
        span = stop - start
        qs = q[:, start:stop]
        here = span // HEAD
        masked = [jnp.where(lane[:, :span] == h, qs, zero) for h in range(here)]
        rest = jnp.concatenate([m[MAIN:] for m in masked], axis=0)
        ks = k[:, start:stop]
        for h in range(0, here, step):
            main = jnp.concatenate([m[:MAIN] for m in masked[h : h + step]], axis=0)
            pieces.append(dot(ks, main, ((1,), (1,))))
        rests.append(dot(ks, rest, ((1,), (1,))))
    outs = []
    base = 0
    for piece in pieces:
        span = piece.shape[1]
        s = piece + table[:, base : base + span]
        s = s - jnp.max(s, axis=0, keepdims=True)
        e = jnp.exp2(s)
        inv = 1.0 / jnp.sum(e, axis=0, keepdims=True)
        p = e.astype(BF16)
        for h in range(span // MAIN):
            row = base // MAIN + h
            cut = slice(h * MAIN, (h + 1) * MAIN)
            outs.append(dot(vt[row * HEAD : (row + 1) * HEAD], p[:, cut]) * inv[:, cut])
        base += span
    main_out = jnp.concatenate(outs, axis=0)
    s = jnp.concatenate(rests, axis=1) + table[:, base:]
    s = s - jnp.max(s, axis=0, keepdims=True)
    e = jnp.exp2(s)
    inv = 1.0 / jnp.sum(e, axis=0, keepdims=True)
    full = dot(vt, e.astype(BF16)) * inv
    row = lax.broadcasted_iota(jnp.int32, full.shape, 0) // HEAD
    column = lax.broadcasted_iota(jnp.int32, full.shape, 1) // REST
    full = jnp.where(row == column, full, 0.0).astype(BF16)
    fold_row = lax.broadcasted_iota(jnp.int32, (heads * REST, REST), 0)
    fold_column = lax.broadcasted_iota(jnp.int32, (heads * REST, REST), 1)
    fold = jnp.where(jnp.bitwise_and(fold_row, REST - 1) == fold_column, 1.0, 0.0).astype(BF16)
    rest_out = dot(full, fold)
    return jnp.concatenate([main_out.astype(BF16), rest_out.astype(BF16)], axis=1)


def block_rows(x_ref, count, table_ref, heads, gain_one, wq, wk, wvt, wo, gain_two, w1, w2, w2_dims, out_ref, ends=True):
    x = x_ref[...]
    xn = layer_norm(x, gain_one[...][None, :]).astype(BF16)
    q = (dot(xn, wq) * (LOG2E / math.sqrt(HEAD))).astype(BF16)
    k = dot(xn, wk).astype(BF16)
    mixed = []
    for w in range(count):
        rows = slice(w * WIN, (w + 1) * WIN)
        vt = dot(wvt, xn[rows], ((1,), (1,))).astype(BF16)
        table = table_ref.at[1 if ends and w == count - 1 else 0]
        attended = attend(q[rows], k[rows], vt, table, heads, 4 if heads == 6 else 2)
        mixed.append(dot(attended, wo[...], ((0,), (0,))))
    after = (x + jnp.concatenate(mixed, axis=0)).astype(BF16).astype(F32)
    normed = layer_norm(after, gain_two[...][None, :]).astype(BF16)
    hidden = gelu(dot(normed, w1[...])).astype(BF16)
    out_ref[...] = (after + dot(hidden, w2[...], w2_dims)).astype(BF16).astype(F32)


class Packed:
    def __init__(self, low_ref, high_ref, rows):
        self.low, self.high, self.rows = low_ref, high_ref, rows
        self.pairs = low_ref.shape[0]

    def put(self, p, at, value):
        n = value.shape[0]
        self.low[p, at : at + n, :] = value[:, :MAIN]
        self.high[p, at : at + n, : value.shape[1] - MAIN] = value[:, MAIN:]

    def get(self, p, at, n):
        return jnp.concatenate([self.low[p, at : at + n, :], self.high[p, at : at + n, : MAIN // 2]], axis=1)

    def store(self, out_ref):
        half = self.pairs // 2
        rows = slice(0, self.rows)
        for p in range(self.pairs):
            out_ref[p] = self.low[p, rows, :].astype(BF16)
        for p in range(half):
            sides = [self.high[p + s * half, rows, : MAIN // 2] for s in range(2)]
            out_ref[self.pairs + p] = jnp.concatenate(sides, axis=1).astype(BF16)

    def load(self, in_ref, first=0):
        pairs = in_ref.shape[0] * 2 // 3
        half = pairs // 2
        rows = slice(0, self.rows)
        for p in range(self.pairs):
            self.low[p, rows, :] = in_ref[first + p].astype(F32)
            side, row = divmod(first + p, half)
            both = in_ref[pairs + row].astype(F32)
            self.high[p, rows, : MAIN // 2] = both[:, side * MAIN // 2 : (side + 1) * MAIN // 2]
        return self


def packed_rows(tokens):
    return -(-tokens // 16) * 16


def pair_levels(p, levels):
    return [(WIN_P * p + WIN_P // 2 + lev) % levels for lev in range(WIN_P)]


def start_kernel(field, lat_ref, lon_ref, diag_ref, line_ref, low_ref, high_ref):
    levels, rows, columns, _ = field.shape
    packs = [Packed(low_ref.at[n], high_ref.at[n], ref.shape[1]) for n, ref in enumerate((lat_ref, lon_ref, diag_ref))]
    lat, lon, diag = packs
    for p in range(levels // WIN_P):
        for lev, level in enumerate(pair_levels(p, levels)):
            for r in range(rows):
                line = field[level, r].astype(F32)
                if r < HALF_LAT:
                    slot = level * HALF_LAT + r
                    line_ref[slot] = line
                    diag.put(p, (lev * HALF_LAT + r) * HALF_LON, line[:HALF_LON])
                    span = columns - HALF_LON
                    lat.put(p, (lev * HALF_LAT + r) * span, line_ref[slot, HALF_LON:, :])
                else:
                    lon.put(p, (lev * (rows - HALF_LAT) + r - HALF_LAT) * HALF_LON, line[:HALF_LON])
    for pack, ref in zip(packs, (lat_ref, lon_ref, diag_ref)):
        pack.store(ref)


def pack_second(w00, w10, lat_in, out_ref, low_ref, high_ref):
    rows, columns = 2 * WIN_LAT, 2 * WIN_LON
    lat = Packed(low_ref.at[0], high_ref.at[0], lat_in.shape[1]).load(lat_in)
    send = Packed(low_ref.at[1], high_ref.at[1], out_ref.shape[1])
    for p in range(w00.shape[0] // WIN):
        for lev in range(WIN_P):
            for r in range(rows):
                row = r + HALF_LAT
                if row < rows:
                    source = (w00, w10)[row // WIN_LAT]
                    here = ((p * WIN_P + lev) * WIN_LAT + row % WIN_LAT) * WIN_LON
                    value = source[here : here + HALF_LON, :]
                else:
                    value = lat.get(p, (lev * HALF_LAT + row - rows) * columns, HALF_LON)
                send.put(p, (lev * rows + r) * HALF_LON, value)
    send.store(out_ref)


def table_kernel(edge_ref, bias, *outs):
    heads = bias.shape[0]
    out = outs[0]
    for h in range(heads):
        turned = (bias[h] * LOG2E).T
        out[0, :, h * MAIN : (h + 1) * MAIN] = turned[:, :MAIN]
        out[0, :, heads * MAIN + h * REST : heads * MAIN + (h + 1) * REST] = turned[:, MAIN:]
    level = level_mask(heads)
    late = lat_mask(heads) * edge_ref[0].astype(F32)
    outs[-1][0] = out[0] + late
    for ref in outs:
        ref[1] = ref[0] + level


def fine_table_kernel(edge_ref, bias, project, plain_ref, late_ref, wq_ref, wk_ref, wvt_ref):
    table_kernel(edge_ref, bias, plain_ref, late_ref)
    width = wq_ref.shape[0]
    wq_ref[...] = project[:, :width]
    wk_ref[...] = project[:, width : 2 * width]
    wvt_ref[...] = project[:, 2 * width :].astype(F32).T.astype(BF16)


def fine_kernel(i, j, *refs):
    refs = list(refs)
    field = refs.pop(0)
    lat_in = refs.pop(0) if i else None
    lon_in = refs.pop(0) if j else None
    diag_in = refs.pop(0) if i and j else None
    sends = j and not i
    first = refs.pop(0) if sends else None
    table_ref, gain_one, wq, wk, wvt, wo, gain_two, w1, w2t, out_ref = refs[:10]
    refs = refs[10:]
    send_ref = refs.pop(0) if sends else None
    line_ref, x_ref, low_ref, high_ref = refs
    levels, rows, columns, _ = field.shape
    pairs = levels // WIN_P
    lat, lon, diag = [
        Packed(low_ref.at[n], high_ref.at[n], ref.shape[1]).load(ref) if ref is not None else None
        for n, ref in enumerate((lat_in, lon_in, diag_in))
    ]
    at = 0
    slot = 0
    start = HALF_LON + j * WIN_LON
    own = min(columns - start, WIN_LON)
    for p in range(pairs):
        for lev, level in enumerate(pair_levels(p, levels)):
            for row in range(i * WIN_LAT + HALF_LAT, (i + 1) * WIN_LAT + HALF_LAT):
                if row < rows:
                    line_ref[slot] = field[level, row].astype(F32)
                    x_ref[at : at + own, :] = line_ref[slot, start : start + own, :]
                    slot += 1
                    if own < WIN_LON:
                        late = lev * (rows - HALF_LAT) + row - HALF_LAT
                        x_ref[at + own : at + WIN_LON, :] = lon.get(p, late * HALF_LON, HALF_LON)
                else:
                    below = lev * HALF_LAT + row - rows
                    x_ref[at : at + own, :] = lat.get(p, below * (columns - HALF_LON) + j * WIN_LON, own)
                    if own < WIN_LON:
                        x_ref[at + own : at + WIN_LON, :] = diag.get(p, below * HALF_LON, HALF_LON)
                at += WIN_LON
    block_rows(
        x_ref, pairs, table_ref, 6, gain_one, wq[...], wk[...], wvt[...], wo, gain_two, w1, w2t, ((1,), (1,)), out_ref
    )
    if not sends:
        return
    send = Packed(low_ref.at[0], high_ref.at[0], send_ref.shape[1])
    for p in range(pairs):
        for lev in range(WIN_P):
            for row in range(HALF_LAT):
                at = (lev * HALF_LAT + row) * columns
                here = ((p * WIN_P + lev) * WIN_LAT + row) * WIN_LON
                send.put(p, at, first[here : here + WIN_LON, :])
                send.put(p, at + WIN_LON, out_ref[here : here + WIN_LON, :])
    send.store(send_ref)


def coarse_kernel(
    first, w00, w01, w10, w11, lat_in, lon_in, table_ref,
    merge_gain, merge_weight,
    gain_one, project, wo, gain_two, w1, w2,
    up_first, up_norm, up_second,
    stay_ref, to_lat_ref, to_lon_ref, to_diag_ref,
    low_ref, high_ref, grid_low, grid_high, quad_low, quad_high, parts_ref, x_ref, y_ref,
):
    heads = 12
    width = w00.shape[1]
    rows, columns = 2 * WIN_LAT, 2 * WIN_LON
    pairs = x_ref.shape[0] // WIN
    levels = pairs * WIN_P
    windows = ((w00, w01), (w10, w11))
    lat, lon = [
        Packed(low_ref.at[n], high_ref.at[n], ref.shape[1]).load(ref, first) for n, ref in enumerate((lat_in, lon_in))
    ]

    def put(at, value):
        grid_low[at : at + value.shape[0], :] = value[:, :MAIN]
        grid_high[at : at + value.shape[0], : width - MAIN] = value[:, MAIN:]

    for p in range(pairs):
        for lev in range(WIN_P):
            for row in range(rows):
                at = ((p * WIN_P + lev) * rows + row) * PITCH
                if row + HALF_LAT < rows:
                    left, right = windows[(row + HALF_LAT) // WIN_LAT]
                    here = (((first + p) * WIN_P + lev) * WIN_LAT + (row + HALF_LAT) % WIN_LAT) * WIN_LON
                    put(at + HALF_LON, left[here + HALF_LON : here + WIN_LON, :])
                    put(at + WIN_LON, right[here : here + WIN_LON, :])
                else:
                    below = lev * HALF_LAT + row + HALF_LAT - rows
                    put(at + HALF_LON, lat.get(p, below * columns + HALF_LON, columns - HALF_LON))
                put(at + columns, lon.get(p, (lev * rows + row) * HALF_LON, HALF_LON))
    for r in range(2):
        for t in range(2):
            n = 2 * r + t
            at = 0
            for level in range(levels):
                for a in range(rows // 2):
                    start = (level * rows + 2 * a + r) * PITCH + HALF_LON + t
                    parts_ref[n, at : at + WIN_LON, :MAIN] = grid_low[pl.ds(start, WIN_LON, stride=2), :]
                    parts_ref[n, at : at + WIN_LON, MAIN:] = grid_high[pl.ds(start, WIN_LON, stride=2), :]
                    at += WIN_LON
    parts = [parts_ref[n, :, :width] for n in range(4)]
    average = jnp.sum(parts[0] + parts[1] + parts[2] + parts[3], axis=-1, keepdims=True) * (1.0 / (4 * width))
    centred = [part - average for part in parts]
    squares = centred[0] * centred[0]
    for c in centred[1:]:
        squares += c * c
    scale = lax.rsqrt(jnp.sum(squares, axis=-1, keepdims=True) * (1.0 / (4 * width)) + EPS)
    total = None
    for n in range(4):
        gain = merge_gain[n * width : (n + 1) * width][None, :]
        normed = (centred[n] * scale * gain).astype(BF16)
        term = dot(normed, merge_weight[n * width : (n + 1) * width, :])
        total = term if total is None else total + term
    x_ref[...] = total.astype(BF16).astype(F32)
    double = 2 * width
    wvt = project[:, 2 * double :].astype(F32).T.astype(BF16)
    block_rows(
        x_ref, pairs, table_ref, heads, gain_one, project[:, :double], project[:, double : 2 * double], wvt,
        wo, gain_two, w1, w2, ((1,), (0,)), y_ref, first + pairs == w00.shape[0] // WIN,
    )
    coarse = y_ref[...].astype(BF16)
    half = rows // 2
    for r in range(2):
        for t in range(2):
            n = 2 * r + t
            raised = dot(coarse, up_first[:, n * width : (n + 1) * width]).astype(BF16).astype(F32)
            normed = layer_norm(raised, up_norm[...][None, :]).astype(BF16)
            parts_ref[n, :, :width] = parts_ref[n, :, :width] + dot(normed, up_second[...])
            for level in range(levels):
                for a in range(half):
                    row = 2 * a + r
                    for side in range(2):
                        at = (level * half + a) * WIN_LON + side * HALF_LON
                        quad, p = 2 * (row // half) + side, level // WIN_P
                        start = (level % WIN_P * half + row % half) * WIN_LON + t
                        to = pl.ds(start, HALF_LON, stride=2)
                        quad_low[quad, p, to, :] = parts_ref[n, at : at + HALF_LON, :MAIN]
                        quad_high[quad, p, to, :] = parts_ref[n, at : at + HALF_LON, MAIN:]
    for quad, ref in enumerate((stay_ref, to_lon_ref, to_lat_ref, to_diag_ref)):
        Packed(quad_low.at[quad], quad_high.at[quad], WIN).store(ref)


def finish_kernel(*refs):
    quarters = refs[:-5]
    out_ref, low_ref, high_ref, line_low, line_high = refs[-5:]
    levels, rows, columns, width = out_ref.shape
    half = rows // 2
    pairs = low_ref.shape[1]
    for n, ref in enumerate(quarters):
        part, quad = divmod(n, 4)
        pack = Packed(low_ref.at[n], high_ref.at[n], WIN).load(ref)
        for p in range(pairs):
            for lev, level in enumerate(pair_levels(part * pairs + p, levels)):
                for row in range(half):
                    at = (level * rows + (quad // 2) * half + row) * columns + quad % 2 * WIN_LON
                    here = (lev * half + row) * WIN_LON
                    line_low[at : at + WIN_LON, :] = pack.low[p, here : here + WIN_LON, :]
                    line_high[at : at + WIN_LON, :] = pack.high[p, here : here + WIN_LON, :]
    for level in range(levels):
        for row in range(rows):
            at = (level * rows + row) * columns
            out_ref[level, row, :, :MAIN] = line_low[at : at + columns, :].astype(BF16)
            out_ref[level, row, :, MAIN:] = line_high[at : at + columns, : width - MAIN].astype(BF16)


MIB = 1024 * 1024


def call(kernel, name, operands, outs, scratch, limit, scalars=0, us=1):
    vmem = pl.BlockSpec(memory_space=pltpu.VMEM)
    smem = pl.BlockSpec(memory_space=pltpu.SMEM)
    moved = sum(x.size * x.dtype.itemsize for x in operands) + sum(math.prod(s) * jnp.dtype(d).itemsize for s, d in outs)
    return pl.pallas_call(
        kernel,
        in_specs=[smem] * scalars + [vmem] * (len(operands) - scalars),
        out_specs=[vmem] * len(outs),
        out_shape=[jax.ShapeDtypeStruct(s, d) for s, d in outs],
        scratch_shapes=[pltpu.VMEM(s, F32) for s in scratch],
        compiler_params=pltpu.CompilerParams(vmem_limit_bytes=limit * MIB),
        cost_estimate=pl.CostEstimate(flops=us * 1000 * MIB, bytes_accessed=moved, transcendentals=0),
        name=name,
    )(*operands)


def packed_shape(tokens, pairs):
    return (pairs * 3 // 2, packed_rows(tokens), MAIN)


def shift(array, lat_by, lon_by):
    lats, lons = lax.axis_size("lat"), lax.axis_size("lon")
    if lat_by and lon_by:
        pairs = [
            (((a + lat_by) % lats) * lons + (b + lon_by) % lons, a * lons + b)
            for a in range(lats)
            for b in range(lons)
        ]
        return lax.ppermute(array, ("lat", "lon"), pairs)
    if lat_by:
        return lax.ppermute(array, "lat", [((i + lat_by) % lats, i) for i in range(lats)])
    return lax.ppermute(array, "lon", [((i + lon_by) % lons, i) for i in range(lons)])


def body(
    field, a_norm_one, a_project, a_bias, a_output, a_norm_two, a_raise, a_lower,
    merge_norm_gain, merge_weight,
    b_norm_one, b_project, b_bias, b_output, b_norm_two, b_raise, b_lower,
    up_first, up_norm, up_second,
):
    levels, rows, columns, width = field.shape
    pairs = levels // WIN_P
    halo = packed_shape(WIN, pairs)
    staging = (pairs, WIN, MAIN)
    both = (2,) + staging
    tokens = pairs * WIN

    edge = (lax.axis_index("lat") == lax.axis_size("lat") - 1).astype(jnp.int32).reshape(1)
    lat_shape = packed_shape(WIN_P * HALF_LAT * (columns - HALF_LON), pairs)
    lon_shape = packed_shape(WIN_P * (rows - HALF_LAT) * HALF_LON, pairs)
    diag_shape = packed_shape(WIN_P * HALF_LAT * HALF_LON, pairs)
    lat, lon, diag = call(
        start_kernel, "start", [field], [(lat_shape, BF16), (lon_shape, BF16), (diag_shape, BF16)],
        [(levels * HALF_LAT, columns, width), (3,) + staging, (3,) + staging], 16, us=3,
    )
    lon = shift(lon, 0, 1)
    lat = shift(lat, 1, 0)
    diag = shift(diag, 1, 1)
    a_heads, b_heads = a_bias.shape[0], b_bias.shape[0]
    square = ((width, width), BF16)
    plain, late, wq, wk, wvt = call(
        fine_table_kernel, "fine_tables", [edge, a_bias, a_project],
        [((2, WIN, a_heads * WIN), F32)] * 2 + [square] * 3, [], 16, scalars=1, us=3,
    )
    weights = [a_norm_one, wq, wk, wvt, a_output, a_norm_two, a_raise, a_lower.T]
    scratch = [(levels * WIN_LAT, columns, width), (tokens, width), (3,) + staging, (3,) + staging]
    out = ((tokens, width), F32)

    def fine(i, j, halos, outs):
        def kernel(*refs):
            fine_kernel(i, j, *refs)

        operands = [field, *halos, late if i else plain, *weights]
        return call(kernel, f"fine_{i}{j}", operands, [out] + outs, scratch, 20, us=5)

    (w00,) = fine(0, 0, [], [])
    lon, lat, diag, w00 = lax.optimization_barrier((lon, lat, diag, w00))
    w01, lat_two = fine(0, 1, [lon, w00], [(halo, BF16)])
    lat_two = shift(lat_two, 1, 0)
    lat, w01 = lax.optimization_barrier((lat, w01))
    (w10,) = fine(1, 0, [lat], [])
    lat_two, w10 = lax.optimization_barrier((lat_two, w10))
    (lon_two,) = call(pack_second, "pack_second", [w00, w10, lat_two], [(halo, BF16)], [both, both], 16)
    diag, lon_two = lax.optimization_barrier((diag, lon_two))
    lon_two = shift(lon_two, 0, 1)
    (w11,) = fine(1, 1, [lat, lon, diag], [])
    late_bias, w11 = lax.optimization_barrier((b_bias, w11))
    (coarse_table,) = call(
        table_kernel, "coarse_table", [edge, late_bias], [((2, WIN, b_heads * WIN), F32)], [], 16, scalars=1
    )

    part = pairs // 2
    part_halo = (2, part, WIN, MAIN)
    quads = (4, part, WIN, MAIN)
    lines = (part * WIN_P * rows * PITCH, MAIN)

    def coarse(first):
        def kernel(*refs):
            coarse_kernel(first, *refs)

        return call(
            kernel, f"coarse_{first}",
            [
                w00, w01, w10, w11, lat_two, lon_two, coarse_table, merge_norm_gain, merge_weight,
                b_norm_one, b_project, b_output, b_norm_two, b_raise, b_lower, up_first, up_norm, up_second,
            ],
            [(packed_shape(WIN, part), BF16)] * 4,
            [part_halo, part_halo, lines, lines, quads, quads, (4, part * WIN, 2 * MAIN)] + [(part * WIN, 2 * width)] * 2,
            32, us=7,
        )

    quarters = []
    for first in range(0, pairs, part):
        stay, lat, lon, diag = coarse(first)
        quarters += [shift(diag, -1, -1), shift(lat, -1, 0), shift(lon, 0, -1), stay]
    quads = (8, part, WIN, MAIN)
    lines = (levels * rows * columns, MAIN)
    (fine_out,) = call(finish_kernel, "finish", quarters, [(field.shape, BF16)], [quads, quads, lines, lines], 24)
    return fine_out


def solution(mesh):
    in_specs = (P(None, "lat", "lon", None),) + (P(),) * 19
    out_specs = P(None, "lat", "lon", None)
    return jax.shard_map(body, mesh=mesh, in_specs=in_specs, out_specs=out_specs, check_vma=False)
```

```python
import math

import jax
import jax.numpy as jnp
from jax import lax
from jax.experimental import pallas as pl
from jax.experimental.pallas import tpu as pltpu
from jax.sharding import PartitionSpec as P

WIN_P = 2
WIN_LAT = 6
WIN_LON = 12
WIN = WIN_P * WIN_LAT * WIN_LON
HALF_LAT = WIN_LAT // 2
HALF_LON = WIN_LON // 2
HEAD = 32
MAIN = 128
REST = WIN - MAIN
EPS = 1e-05
LOG2E = math.log2(math.e)
EXCLUDED = -1e30
PITCH = 32

F32 = jnp.float32
BF16 = jnp.bfloat16


def dot(a, b, contract=((1,), (0,))):
    return lax.dot_general(a, b, (contract, ((), ())), preferred_element_type=F32)


def layer_norm(values, gain):
    average = jnp.mean(values, axis=-1, keepdims=True)
    centred = values - average
    variance = jnp.mean(centred * centred, axis=-1, keepdims=True)
    return centred * lax.rsqrt(variance + EPS) * gain


def gelu(x):
    return 0.5 * x * (1.0 + lax.erf(x * (1.0 / math.sqrt(2.0))))


def token_index(shape, heads):
    key = lax.broadcasted_iota(jnp.int32, shape, 0)
    column = lax.broadcasted_iota(jnp.int32, shape, 1)
    rest = column - heads * MAIN
    query = jnp.where(rest < 0, jnp.bitwise_and(column, MAIN - 1), MAIN + jnp.bitwise_and(rest, REST - 1))
    return key, query


def level_mask(heads):
    key, query = token_index((WIN, heads * WIN), heads)
    half = WIN // 2
    return jnp.where((key >= half) != (query >= half), EXCLUDED, 0.0)


def lat_mask(heads):
    key, query = token_index((WIN, heads * WIN), heads)
    half, quarter = WIN // 2, WIN // 4

    def late(t):
        return jnp.where(t >= half, t - half, t) >= quarter

    return jnp.where(late(key) != late(query), EXCLUDED, 0.0)


def attend(q, k, vt, table, heads, step, near):
    width = heads * HEAD
    lane = lax.broadcasted_iota(jnp.int32, (1, MAIN), 1) // HEAD
    zero = jnp.zeros((), BF16)
    pieces = []
    rests = []
    for start in range(0, width, MAIN):
        stop = min(start + MAIN, width)
        span = stop - start
        qs = q[:, start:stop]
        here = span // HEAD
        masked = [jnp.where(lane[:, :span] == h, qs, zero) for h in range(here)]
        rest = jnp.concatenate([m[MAIN:] for m in masked], axis=0)
        ks = k[:, start:stop]
        for h in range(0, here, step):
            main = jnp.concatenate([m[:MAIN] for m in masked[h : h + step]], axis=0)
            pieces.append(dot(ks, main, ((1,), (1,))))
        rests.append(dot(ks, rest, ((1,), (1,))))
    outs = []
    base = 0
    for piece in pieces:
        span = piece.shape[1]
        s = piece + table[:, base : base + span]
        s = s - jnp.max(s, axis=0, keepdims=True)
        e = jnp.exp2(s)
        inv = 1.0 / jnp.sum(e, axis=0, keepdims=True)
        p = e.astype(BF16)
        for h in range(0, span // MAIN, near):
            row = base // MAIN + h
            both = dot(vt[row * HEAD : (row + near) * HEAD], p[:, h * MAIN : (h + near) * MAIN])
            for n in range(near):
                cut = slice(n * MAIN, (n + 1) * MAIN)
                outs.append(both[n * HEAD : (n + 1) * HEAD, cut] * inv[:, (h + n) * MAIN : (h + n + 1) * MAIN])
        base += span
    main_out = jnp.concatenate(outs, axis=0)
    s = jnp.concatenate(rests, axis=1) + table[:, base:]
    s = s - jnp.max(s, axis=0, keepdims=True)
    e = jnp.exp2(s)
    inv = 1.0 / jnp.sum(e, axis=0, keepdims=True)
    full = dot(vt, e.astype(BF16)) * inv
    row = lax.broadcasted_iota(jnp.int32, full.shape, 0) // HEAD
    column = lax.broadcasted_iota(jnp.int32, full.shape, 1) // REST
    full = jnp.where(row == column, full, 0.0).astype(BF16)
    fold_row = lax.broadcasted_iota(jnp.int32, (heads * REST, REST), 0)
    fold_column = lax.broadcasted_iota(jnp.int32, (heads * REST, REST), 1)
    fold = jnp.where(jnp.bitwise_and(fold_row, REST - 1) == fold_column, 1.0, 0.0).astype(BF16)
    rest_out = dot(full, fold)
    return jnp.concatenate([main_out.astype(BF16), rest_out.astype(BF16)], axis=1)


def block_rows(x_ref, count, table_ref, heads, gain_one, wq, wk, wvt, wo, gain_two, w1, w2, w2_dims, out_ref):
    x = x_ref[...]
    xn = layer_norm(x, gain_one[...][None, :]).astype(BF16)
    q = (dot(xn, wq) * (LOG2E / math.sqrt(HEAD))).astype(BF16)
    k = dot(xn, wk).astype(BF16)
    mixed = []
    for w in range(count):
        rows = slice(w * WIN, (w + 1) * WIN)
        vt = dot(wvt, xn[rows], ((1,), (1,))).astype(BF16)
        table = table_ref.at[1 if w == count - 1 else 0]
        attended = attend(q[rows], k[rows], vt, table, heads, *((4, 2) if heads == 6 else (2, 1)))
        mixed.append(dot(attended, wo[...], ((0,), (0,))))
    half = count // 2
    for first in range(0, count, half):
        rows = slice(first * WIN, (first + half) * WIN)
        after = x_ref[rows, :] + jnp.concatenate(mixed[first : first + half], axis=0)
        after = after.astype(BF16).astype(F32)
        normed = layer_norm(after, gain_two[...][None, :]).astype(BF16)
        hidden = gelu(dot(normed, w1[...])).astype(BF16)
        out_ref[rows, :] = (after + dot(hidden, w2[...], w2_dims)).astype(BF16).astype(F32)


class Packed:
    def __init__(self, low_ref, high_ref, rows):
        self.low, self.high, self.rows = low_ref, high_ref, rows
        self.pairs = low_ref.shape[0]

    def put(self, p, at, value):
        n = value.shape[0]
        self.low[p, at : at + n, :] = value[:, :MAIN]
        self.high[p, at : at + n, : value.shape[1] - MAIN] = value[:, MAIN:]

    def get(self, p, at, n):
        return jnp.concatenate([self.low[p, at : at + n, :], self.high[p, at : at + n, : MAIN // 2]], axis=1)

    def store(self, out_ref):
        half = self.pairs // 2
        rows = slice(0, self.rows)
        for p in range(self.pairs):
            out_ref[p] = self.low[p, rows, :].astype(BF16)
        for p in range(half):
            sides = [self.high[p + s * half, rows, : MAIN // 2] for s in range(2)]
            out_ref[self.pairs + p] = jnp.concatenate(sides, axis=1).astype(BF16)

    def load(self, in_ref):
        half = self.pairs // 2
        rows = slice(0, self.rows)
        for p in range(self.pairs):
            self.low[p, rows, :] = in_ref[p].astype(F32)
        for p in range(half):
            both = in_ref[self.pairs + p].astype(F32)
            for s in range(2):
                self.high[p + s * half, rows, : MAIN // 2] = both[:, s * MAIN // 2 : (s + 1) * MAIN // 2]
        return self


def packed_rows(tokens):
    return -(-tokens // 16) * 16


def pair_levels(p, levels):
    return [(WIN_P * p + WIN_P // 2 + lev) % levels for lev in range(WIN_P)]


def start_kernel(field, lat_ref, lon_ref, diag_ref, line_ref, low_ref, high_ref):
    levels, rows, columns, _ = field.shape
    packs = [Packed(low_ref.at[n], high_ref.at[n], ref.shape[1]) for n, ref in enumerate((lat_ref, lon_ref, diag_ref))]
    lat, lon, diag = packs
    for p in range(levels // WIN_P):
        for lev, level in enumerate(pair_levels(p, levels)):
            for r in range(rows):
                line = field[level, r].astype(F32)
                if r < HALF_LAT:
                    slot = level * HALF_LAT + r
                    line_ref[slot] = line
                    diag.put(p, (lev * HALF_LAT + r) * HALF_LON, line[:HALF_LON])
                    span = columns - HALF_LON
                    lat.put(p, (lev * HALF_LAT + r) * span, line_ref[slot, HALF_LON:, :])
                else:
                    lon.put(p, (lev * (rows - HALF_LAT) + r - HALF_LAT) * HALF_LON, line[:HALF_LON])
    for pack, ref in zip(packs, (lat_ref, lon_ref, diag_ref)):
        pack.store(ref)


def pack_second(w00, w10, lat_in, out_ref, low_ref, high_ref):
    rows, columns = 2 * WIN_LAT, 2 * WIN_LON
    lat = Packed(low_ref.at[0], high_ref.at[0], lat_in.shape[1]).load(lat_in)
    send = Packed(low_ref.at[1], high_ref.at[1], out_ref.shape[1])
    for p in range(w00.shape[0] // WIN):
        for lev in range(WIN_P):
            for r in range(rows):
                row = r + HALF_LAT
                if row < rows:
                    source = (w00, w10)[row // WIN_LAT]
                    here = ((p * WIN_P + lev) * WIN_LAT + row % WIN_LAT) * WIN_LON
                    value = source[here : here + HALF_LON, :]
                else:
                    value = lat.get(p, (lev * HALF_LAT + row - rows) * columns, HALF_LON)
                send.put(p, (lev * rows + r) * HALF_LON, value)
    send.store(out_ref)


def table_kernel(edge_ref, bias, *outs):
    heads = bias.shape[0]
    out = outs[0]
    for h in range(heads):
        turned = (bias[h] * LOG2E).T
        out[0, :, h * MAIN : (h + 1) * MAIN] = turned[:, :MAIN]
        out[0, :, heads * MAIN + h * REST : heads * MAIN + (h + 1) * REST] = turned[:, MAIN:]
    level = level_mask(heads)
    late = lat_mask(heads) * edge_ref[0].astype(F32)
    outs[-1][0] = out[0] + late
    for ref in outs:
        ref[1] = ref[0] + level


def fine_table_kernel(edge_ref, bias, project, plain_ref, late_ref, wq_ref, wk_ref, wvt_ref):
    table_kernel(edge_ref, bias, plain_ref, late_ref)
    width = wq_ref.shape[0]
    wq_ref[...] = project[:, :width]
    wk_ref[...] = project[:, width : 2 * width]
    wvt_ref[...] = project[:, 2 * width :].astype(F32).T.astype(BF16)


def fine_kernel(i, j, *refs):
    refs = list(refs)
    field = refs.pop(0)
    lat_in = refs.pop(0) if i else None
    lon_in = refs.pop(0) if j else None
    diag_in = refs.pop(0) if i and j else None
    sends = j and not i
    first = refs.pop(0) if sends else None
    table_ref, gain_one, wq, wk, wvt, wo, gain_two, w1, w2t, out_ref = refs[:10]
    refs = refs[10:]
    send_ref = refs.pop(0) if sends else None
    line_ref, x_ref, low_ref, high_ref = refs
    levels, rows, columns, _ = field.shape
    pairs = levels // WIN_P
    lat, lon, diag = [
        Packed(low_ref.at[n], high_ref.at[n], ref.shape[1]).load(ref) if ref is not None else None
        for n, ref in enumerate((lat_in, lon_in, diag_in))
    ]
    at = 0
    slot = 0
    start = HALF_LON + j * WIN_LON
    own = min(columns - start, WIN_LON)
    for p in range(pairs):
        for lev, level in enumerate(pair_levels(p, levels)):
            for row in range(i * WIN_LAT + HALF_LAT, (i + 1) * WIN_LAT + HALF_LAT):
                if row < rows:
                    line_ref[slot] = field[level, row].astype(F32)
                    x_ref[at : at + own, :] = line_ref[slot, start : start + own, :]
                    slot += 1
                    if own < WIN_LON:
                        late = lev * (rows - HALF_LAT) + row - HALF_LAT
                        x_ref[at + own : at + WIN_LON, :] = lon.get(p, late * HALF_LON, HALF_LON)
                else:
                    below = lev * HALF_LAT + row - rows
                    x_ref[at : at + own, :] = lat.get(p, below * (columns - HALF_LON) + j * WIN_LON, own)
                    if own < WIN_LON:
                        x_ref[at + own : at + WIN_LON, :] = diag.get(p, below * HALF_LON, HALF_LON)
                at += WIN_LON
    block_rows(
        x_ref, pairs, table_ref, 6, gain_one, wq[...], wk[...], wvt[...], wo, gain_two, w1, w2t, ((1,), (1,)), out_ref
    )
    if not sends:
        return
    send = Packed(low_ref.at[0], high_ref.at[0], send_ref.shape[1])
    for p in range(pairs):
        for lev in range(WIN_P):
            for row in range(HALF_LAT):
                at = (lev * HALF_LAT + row) * columns
                here = ((p * WIN_P + lev) * WIN_LAT + row) * WIN_LON
                send.put(p, at, first[here : here + WIN_LON, :])
                send.put(p, at + WIN_LON, out_ref[here : here + WIN_LON, :])
    send.store(send_ref)


def coarse_kernel(
    w00, w01, w10, w11, lat_in, lon_in, table_ref,
    merge_gain, merge_weight,
    gain_one, project, wo, gain_two, w1, w2,
    up_first, up_norm, up_second,
    stay_ref, to_lat_ref, to_lon_ref, to_diag_ref,
    low_ref, high_ref, grid_low, grid_high, quad_low, quad_high, parts_ref, x_ref, y_ref,
):
    heads = 12
    width = w00.shape[1]
    rows, columns = 2 * WIN_LAT, 2 * WIN_LON
    pairs = w00.shape[0] // WIN
    levels = pairs * WIN_P
    windows = ((w00, w01), (w10, w11))
    lat, lon = [Packed(low_ref.at[n], high_ref.at[n], ref.shape[1]).load(ref) for n, ref in enumerate((lat_in, lon_in))]

    def put(at, value):
        grid_low[at : at + value.shape[0], :] = value[:, :MAIN]
        grid_high[at : at + value.shape[0], : width - MAIN] = value[:, MAIN:]

    for p in range(pairs):
        for lev in range(WIN_P):
            for row in range(rows):
                at = ((p * WIN_P + lev) * rows + row) * PITCH
                if row + HALF_LAT < rows:
                    left, right = windows[(row + HALF_LAT) // WIN_LAT]
                    here = ((p * WIN_P + lev) * WIN_LAT + (row + HALF_LAT) % WIN_LAT) * WIN_LON
                    put(at + HALF_LON, left[here + HALF_LON : here + WIN_LON, :])
                    put(at + WIN_LON, right[here : here + WIN_LON, :])
                else:
                    below = lev * HALF_LAT + row + HALF_LAT - rows
                    put(at + HALF_LON, lat.get(p, below * columns + HALF_LON, columns - HALF_LON))
                put(at + columns, lon.get(p, (lev * rows + row) * HALF_LON, HALF_LON))
    for r in range(2):
        for t in range(2):
            n = 2 * r + t
            at = 0
            for level in range(levels):
                for a in range(rows // 2):
                    start = (level * rows + 2 * a + r) * PITCH + HALF_LON + t
                    parts_ref[n, at : at + WIN_LON, :MAIN] = grid_low[pl.ds(start, WIN_LON, stride=2), :]
                    parts_ref[n, at : at + WIN_LON, MAIN:] = grid_high[pl.ds(start, WIN_LON, stride=2), :]
                    at += WIN_LON
    parts = [parts_ref[n, :, :width] for n in range(4)]
    average = jnp.sum(parts[0] + parts[1] + parts[2] + parts[3], axis=-1, keepdims=True) * (1.0 / (4 * width))
    centred = [part - average for part in parts]
    squares = centred[0] * centred[0]
    for c in centred[1:]:
        squares += c * c
    scale = lax.rsqrt(jnp.sum(squares, axis=-1, keepdims=True) * (1.0 / (4 * width)) + EPS)
    total = None
    for n in range(4):
        gain = merge_gain[n * width : (n + 1) * width][None, :]
        normed = (centred[n] * scale * gain).astype(BF16)
        term = dot(normed, merge_weight[n * width : (n + 1) * width, :])
        total = term if total is None else total + term
    x_ref[...] = total.astype(BF16).astype(F32)
    double = 2 * width
    wvt = project[:, 2 * double :].astype(F32).T.astype(BF16)
    block_rows(
        x_ref, pairs, table_ref, heads, gain_one, project[:, :double], project[:, double : 2 * double], wvt,
        wo, gain_two, w1, w2, ((1,), (0,)), y_ref,
    )
    coarse = y_ref[...].astype(BF16)
    half = rows // 2
    for r in range(2):
        for t in range(2):
            n = 2 * r + t
            raised = dot(coarse, up_first[:, n * width : (n + 1) * width]).astype(BF16).astype(F32)
            normed = layer_norm(raised, up_norm[...][None, :]).astype(BF16)
            parts_ref[n, :, :width] = parts_ref[n, :, :width] + dot(normed, up_second[...])
            for level in range(levels):
                for a in range(half):
                    row = 2 * a + r
                    for side in range(2):
                        at = (level * half + a) * WIN_LON + side * HALF_LON
                        quad, p = 2 * (row // half) + side, level // WIN_P
                        start = (level % WIN_P * half + row % half) * WIN_LON + t
                        to = pl.ds(start, HALF_LON, stride=2)
                        quad_low[quad, p, to, :] = parts_ref[n, at : at + HALF_LON, :MAIN]
                        quad_high[quad, p, to, :] = parts_ref[n, at : at + HALF_LON, MAIN:]
    for quad, ref in enumerate((stay_ref, to_lon_ref, to_lat_ref, to_diag_ref)):
        Packed(quad_low.at[quad], quad_high.at[quad], WIN).store(ref)


def finish_kernel(upper_left, upper_right, lower_left, lower_right, out_ref, low_ref, high_ref, line_low, line_high):
    levels, rows, columns, width = out_ref.shape
    half = rows // 2
    for quad, ref in enumerate((upper_left, upper_right, lower_left, lower_right)):
        pack = Packed(low_ref.at[quad], high_ref.at[quad], WIN).load(ref)
        for p in range(levels // WIN_P):
            for lev, level in enumerate(pair_levels(p, levels)):
                for row in range(half):
                    at = (level * rows + (quad // 2) * half + row) * columns + quad % 2 * WIN_LON
                    here = (lev * half + row) * WIN_LON
                    line_low[at : at + WIN_LON, :] = pack.low[p, here : here + WIN_LON, :]
                    line_high[at : at + WIN_LON, :] = pack.high[p, here : here + WIN_LON, :]
    for level in range(levels):
        for row in range(rows):
            at = (level * rows + row) * columns
            out_ref[level, row, :, :MAIN] = line_low[at : at + columns, :].astype(BF16)
            out_ref[level, row, :, MAIN:] = line_high[at : at + columns, : width - MAIN].astype(BF16)


MIB = 1024 * 1024


def call(kernel, name, operands, outs, scratch, limit, scalars=0, us=1):
    vmem = pl.BlockSpec(memory_space=pltpu.VMEM)
    smem = pl.BlockSpec(memory_space=pltpu.SMEM)
    moved = sum(x.size * x.dtype.itemsize for x in operands) + sum(math.prod(s) * jnp.dtype(d).itemsize for s, d in outs)
    return pl.pallas_call(
        kernel,
        in_specs=[smem] * scalars + [vmem] * (len(operands) - scalars),
        out_specs=[vmem] * len(outs),
        out_shape=[jax.ShapeDtypeStruct(s, d) for s, d in outs],
        scratch_shapes=[pltpu.VMEM(s, F32) for s in scratch],
        compiler_params=pltpu.CompilerParams(vmem_limit_bytes=limit * MIB),
        cost_estimate=pl.CostEstimate(flops=us * 1000 * MIB, bytes_accessed=moved if us else 0, transcendentals=0),
        name=name,
    )(*operands)


def packed_shape(tokens, pairs):
    return (pairs * 3 // 2, packed_rows(tokens), MAIN)


def shift(array, lat_by, lon_by):
    lats, lons = lax.axis_size("lat"), lax.axis_size("lon")
    if lat_by and lon_by:
        pairs = [
            (((a + lat_by) % lats) * lons + (b + lon_by) % lons, a * lons + b)
            for a in range(lats)
            for b in range(lons)
        ]
        return lax.ppermute(array, ("lat", "lon"), pairs)
    if lat_by:
        return lax.ppermute(array, "lat", [((i + lat_by) % lats, i) for i in range(lats)])
    return lax.ppermute(array, "lon", [((i + lon_by) % lons, i) for i in range(lons)])


def body(
    field, a_norm_one, a_project, a_bias, a_output, a_norm_two, a_raise, a_lower,
    merge_norm_gain, merge_weight,
    b_norm_one, b_project, b_bias, b_output, b_norm_two, b_raise, b_lower,
    up_first, up_norm, up_second,
):
    levels, rows, columns, width = field.shape
    pairs = levels // WIN_P
    halo = packed_shape(WIN, pairs)
    staging = (pairs, WIN, MAIN)
    both = (2,) + staging
    tokens = pairs * WIN

    edge = (lax.axis_index("lat") == lax.axis_size("lat") - 1).astype(jnp.int32).reshape(1)
    lat_shape = packed_shape(WIN_P * HALF_LAT * (columns - HALF_LON), pairs)
    lon_shape = packed_shape(WIN_P * (rows - HALF_LAT) * HALF_LON, pairs)
    diag_shape = packed_shape(WIN_P * HALF_LAT * HALF_LON, pairs)
    lat, lon, diag = call(
        start_kernel, "start", [field], [(lat_shape, BF16), (lon_shape, BF16), (diag_shape, BF16)],
        [(levels * HALF_LAT, columns, width), (3,) + staging, (3,) + staging], 16, us=3,
    )
    lon = shift(lon, 0, 1)
    lat = shift(lat, 1, 0)
    diag = shift(diag, 1, 1)
    a_heads, b_heads = a_bias.shape[0], b_bias.shape[0]
    square = ((width, width), BF16)
    plain, late, wq, wk, wvt = call(
        fine_table_kernel, "fine_tables", [edge, a_bias, a_project],
        [((2, WIN, a_heads * WIN), F32)] * 2 + [square] * 3, [], 16, scalars=1, us=0,
    )
    weights = [a_norm_one, wq, wk, wvt, a_output, a_norm_two, a_raise, a_lower.T]
    scratch = [(levels * WIN_LAT, columns, width), (tokens, width), (3,) + staging, (3,) + staging]
    out = ((tokens, width), F32)

    def fine(i, j, halos, outs):
        def kernel(*refs):
            fine_kernel(i, j, *refs)

        operands = [field, *halos, late if i else plain, *weights]
        return call(kernel, f"fine_{i}{j}", operands, [out] + outs, scratch, 20, us=5)

    (w00,) = fine(0, 0, [], [])
    lon, lat, diag, w00 = lax.optimization_barrier((lon, lat, diag, w00))
    w01, lat_two = fine(0, 1, [lon, w00], [(halo, BF16)])
    lat_two = shift(lat_two, 1, 0)
    lat, w01 = lax.optimization_barrier((lat, w01))
    (w10,) = fine(1, 0, [lat], [])
    lat_two, w10 = lax.optimization_barrier((lat_two, w10))
    (lon_two,) = call(pack_second, "pack_second", [w00, w10, lat_two], [(halo, BF16)], [both, both], 16)
    lon_two, late_bias = lax.optimization_barrier((lon_two, b_bias))
    lon_two = shift(lon_two, 0, 1)
    (coarse_table,) = call(
        table_kernel, "coarse_table", [edge, late_bias], [((2, WIN, b_heads * WIN), F32)], [], 16, scalars=1, us=0
    )
    diag, coarse_table = lax.optimization_barrier((diag, coarse_table))
    (w11,) = fine(1, 1, [lat, lon, diag], [])

    quads = (4,) + staging
    lines = (levels * rows * PITCH, MAIN)
    stay, lat, lon, diag = call(
        coarse_kernel, "coarse",
        [
            w00, w01, w10, w11, lat_two, lon_two, coarse_table, merge_norm_gain, merge_weight,
            b_norm_one, b_project, b_output, b_norm_two, b_raise, b_lower, up_first, up_norm, up_second,
        ],
        [(halo, BF16)] * 4,
        [both, both, lines, lines, quads, quads, (4, tokens, 2 * MAIN), (tokens, 2 * width), (tokens, 2 * width)],
        32, us=12,
    )
    diag = shift(diag, -1, -1)
    lat = shift(lat, -1, 0)
    lon = shift(lon, 0, -1)
    lines = (levels * rows * columns, MAIN)
    (fine_out,) = call(
        finish_kernel, "finish", [diag, lat, lon, stay], [(field.shape, BF16)], [quads, quads, lines, lines], 24
    )
    return fine_out


def solution(mesh):
    in_specs = (P(None, "lat", "lon", None),) + (P(),) * 19
    out_specs = P(None, "lat", "lon", None)
    return jax.shard_map(body, mesh=mesh, in_specs=in_specs, out_specs=out_specs, check_vma=False)
```

```python
import math

import jax
import jax.numpy as jnp
from jax import lax
from jax.experimental import pallas as pl
from jax.experimental.pallas import tpu as pltpu
from jax.sharding import PartitionSpec as P

WIN_P = 2
WIN_LAT = 6
WIN_LON = 12
WIN = WIN_P * WIN_LAT * WIN_LON
HALF_LAT = WIN_LAT // 2
HALF_LON = WIN_LON // 2
HEAD = 32
MAIN = 128
REST = WIN - MAIN
EPS = 1e-05
LOG2E = math.log2(math.e)
EXCLUDED = -1e30
PITCH = 32

F32 = jnp.float32
BF16 = jnp.bfloat16


def dot(a, b, contract=((1,), (0,))):
    return lax.dot_general(a, b, (contract, ((), ())), preferred_element_type=F32)


def layer_norm(values, gain):
    average = jnp.mean(values, axis=-1, keepdims=True)
    centred = values - average
    variance = jnp.mean(centred * centred, axis=-1, keepdims=True)
    return centred * lax.rsqrt(variance + EPS) * gain


def gelu(x):
    return 0.5 * x * (1.0 + lax.erf(x * (1.0 / math.sqrt(2.0))))


def token_index(shape, heads):
    key = lax.broadcasted_iota(jnp.int32, shape, 0)
    column = lax.broadcasted_iota(jnp.int32, shape, 1)
    rest = column - heads * MAIN
    query = jnp.where(rest < 0, jnp.bitwise_and(column, MAIN - 1), MAIN + jnp.bitwise_and(rest, REST - 1))
    return key, query


def level_mask(heads):
    key, query = token_index((WIN, heads * WIN), heads)
    half = WIN // 2
    return jnp.where((key >= half) != (query >= half), EXCLUDED, 0.0)


def lat_mask(heads):
    key, query = token_index((WIN, heads * WIN), heads)
    half, quarter = WIN // 2, WIN // 4

    def late(t):
        return jnp.where(t >= half, t - half, t) >= quarter

    return jnp.where(late(key) != late(query), EXCLUDED, 0.0)


def attend(q, k, vt, table, heads, step, near):
    width = heads * HEAD
    lane = lax.broadcasted_iota(jnp.int32, (1, MAIN), 1) // HEAD
    zero = jnp.zeros((), BF16)
    pieces = []
    rests = []
    for start in range(0, width, MAIN):
        stop = min(start + MAIN, width)
        span = stop - start
        qs = q[:, start:stop]
        here = span // HEAD
        masked = [jnp.where(lane[:, :span] == h, qs, zero) for h in range(here)]
        rest = jnp.concatenate([m[MAIN:] for m in masked], axis=0)
        ks = k[:, start:stop]
        for h in range(0, here, step):
            main = jnp.concatenate([m[:MAIN] for m in masked[h : h + step]], axis=0)
            pieces.append(dot(ks, main, ((1,), (1,))))
        rests.append(dot(ks, rest, ((1,), (1,))))
    outs = []
    base = 0
    for piece in pieces:
        span = piece.shape[1]
        s = piece + table[:, base : base + span]
        s = s - jnp.max(s, axis=0, keepdims=True)
        e = jnp.exp2(s)
        inv = 1.0 / jnp.sum(e, axis=0, keepdims=True)
        p = e.astype(BF16)
        for h in range(0, span // MAIN, near):
            row = base // MAIN + h
            both = dot(vt[row * HEAD : (row + near) * HEAD], p[:, h * MAIN : (h + near) * MAIN])
            for n in range(near):
                cut = slice(n * MAIN, (n + 1) * MAIN)
                outs.append(both[n * HEAD : (n + 1) * HEAD, cut] * inv[:, (h + n) * MAIN : (h + n + 1) * MAIN])
        base += span
    main_out = jnp.concatenate(outs, axis=0)
    s = jnp.concatenate(rests, axis=1) + table[:, base:]
    s = s - jnp.max(s, axis=0, keepdims=True)
    e = jnp.exp2(s)
    inv = 1.0 / jnp.sum(e, axis=0, keepdims=True)
    full = dot(vt, e.astype(BF16)) * inv
    row = lax.broadcasted_iota(jnp.int32, full.shape, 0) // HEAD
    column = lax.broadcasted_iota(jnp.int32, full.shape, 1) // REST
    full = jnp.where(row == column, full, 0.0).astype(BF16)
    fold_row = lax.broadcasted_iota(jnp.int32, (heads * REST, REST), 0)
    fold_column = lax.broadcasted_iota(jnp.int32, (heads * REST, REST), 1)
    fold = jnp.where(jnp.bitwise_and(fold_row, REST - 1) == fold_column, 1.0, 0.0).astype(BF16)
    rest_out = dot(full, fold)
    return jnp.concatenate([main_out.astype(BF16), rest_out.astype(BF16)], axis=1)


def block_rows(x_ref, count, table_ref, heads, gain_one, wq, wk, wvt, wo, gain_two, w1, w2, w2_dims, out_ref):
    x = x_ref[...]
    xn = layer_norm(x, gain_one[...][None, :]).astype(BF16)
    q = (dot(xn, wq) * (LOG2E / math.sqrt(HEAD))).astype(BF16)
    k = dot(xn, wk).astype(BF16)
    mixed = []
    for w in range(count):
        rows = slice(w * WIN, (w + 1) * WIN)
        vt = dot(wvt, xn[rows], ((1,), (1,))).astype(BF16)
        table = table_ref.at[1 if w == count - 1 else 0]
        attended = attend(q[rows], k[rows], vt, table, heads, *((4, 2) if heads == 6 else (2, 1)))
        mixed.append(dot(attended, wo[...], ((0,), (0,))))
    half = count // 2
    for first in range(0, count, half):
        rows = slice(first * WIN, (first + half) * WIN)
        after = x_ref[rows, :] + jnp.concatenate(mixed[first : first + half], axis=0)
        after = after.astype(BF16).astype(F32)
        normed = layer_norm(after, gain_two[...][None, :]).astype(BF16)
        hidden = gelu(dot(normed, w1[...])).astype(BF16)
        out_ref[rows, :] = (after + dot(hidden, w2[...], w2_dims)).astype(BF16).astype(F32)


class Packed:
    def __init__(self, low_ref, high_ref, rows):
        self.low, self.high, self.rows = low_ref, high_ref, rows
        self.pairs = low_ref.shape[0]

    def put(self, p, at, value):
        n = value.shape[0]
        self.low[p, at : at + n, :] = value[:, :MAIN]
        self.high[p, at : at + n, : value.shape[1] - MAIN] = value[:, MAIN:]

    def get(self, p, at, n):
        return jnp.concatenate([self.low[p, at : at + n, :], self.high[p, at : at + n, : MAIN // 2]], axis=1)

    def store(self, out_ref):
        half = self.pairs // 2
        rows = slice(0, self.rows)
        for p in range(self.pairs):
            out_ref[p] = self.low[p, rows, :].astype(BF16)
        for p in range(half):
            sides = [self.high[p + s * half, rows, : MAIN // 2] for s in range(2)]
            out_ref[self.pairs + p] = jnp.concatenate(sides, axis=1).astype(BF16)

    def load(self, in_ref):
        half = self.pairs // 2
        rows = slice(0, self.rows)
        for p in range(self.pairs):
            self.low[p, rows, :] = in_ref[p].astype(F32)
        for p in range(half):
            both = in_ref[self.pairs + p].astype(F32)
            for s in range(2):
                self.high[p + s * half, rows, : MAIN // 2] = both[:, s * MAIN // 2 : (s + 1) * MAIN // 2]
        return self


def packed_rows(tokens):
    return -(-tokens // 16) * 16


def pair_levels(p, levels):
    return [(WIN_P * p + WIN_P // 2 + lev) % levels for lev in range(WIN_P)]


def start_kernel(field, lat_ref, lon_ref, diag_ref, line_ref, low_ref, high_ref):
    levels, rows, columns, _ = field.shape
    packs = [Packed(low_ref.at[n], high_ref.at[n], ref.shape[1]) for n, ref in enumerate((lat_ref, lon_ref, diag_ref))]
    lat, lon, diag = packs
    for p in range(levels // WIN_P):
        for lev, level in enumerate(pair_levels(p, levels)):
            for r in range(rows):
                line = field[level, r].astype(F32)
                if r < HALF_LAT:
                    slot = level * HALF_LAT + r
                    line_ref[slot] = line
                    diag.put(p, (lev * HALF_LAT + r) * HALF_LON, line[:HALF_LON])
                    span = columns - HALF_LON
                    lat.put(p, (lev * HALF_LAT + r) * span, line_ref[slot, HALF_LON:, :])
                else:
                    lon.put(p, (lev * (rows - HALF_LAT) + r - HALF_LAT) * HALF_LON, line[:HALF_LON])
    for pack, ref in zip(packs, (lat_ref, lon_ref, diag_ref)):
        pack.store(ref)


def pack_second(w00, w10, lat_in, out_ref, low_ref, high_ref):
    rows, columns = 2 * WIN_LAT, 2 * WIN_LON
    lat = Packed(low_ref.at[0], high_ref.at[0], lat_in.shape[1]).load(lat_in)
    send = Packed(low_ref.at[1], high_ref.at[1], out_ref.shape[1])
    for p in range(w00.shape[0] // WIN):
        for lev in range(WIN_P):
            for r in range(rows):
                row = r + HALF_LAT
                if row < rows:
                    source = (w00, w10)[row // WIN_LAT]
                    here = ((p * WIN_P + lev) * WIN_LAT + row % WIN_LAT) * WIN_LON
                    value = source[here : here + HALF_LON, :]
                else:
                    value = lat.get(p, (lev * HALF_LAT + row - rows) * columns, HALF_LON)
                send.put(p, (lev * rows + r) * HALF_LON, value)
    send.store(out_ref)


def table_kernel(edge_ref, bias, *outs):
    heads = bias.shape[0]
    out = outs[0]
    for h in range(heads):
        turned = (bias[h] * LOG2E).T
        out[0, :, h * MAIN : (h + 1) * MAIN] = turned[:, :MAIN]
        out[0, :, heads * MAIN + h * REST : heads * MAIN + (h + 1) * REST] = turned[:, MAIN:]
    level = level_mask(heads)
    late = lat_mask(heads) * edge_ref[0].astype(F32)
    outs[-1][0] = out[0] + late
    for ref in outs:
        ref[1] = ref[0] + level


def fine_table_kernel(edge_ref, bias, project, plain_ref, late_ref, wq_ref, wk_ref, wvt_ref):
    table_kernel(edge_ref, bias, plain_ref, late_ref)
    width = wq_ref.shape[0]
    wq_ref[...] = project[:, :width]
    wk_ref[...] = project[:, width : 2 * width]
    wvt_ref[...] = project[:, 2 * width :].astype(F32).T.astype(BF16)


def fine_kernel(i, j, *refs):
    refs = list(refs)
    field = refs.pop(0)
    lat_in = refs.pop(0) if i else None
    lon_in = refs.pop(0) if j else None
    diag_in = refs.pop(0) if i and j else None
    sends = j and not i
    first = refs.pop(0) if sends else None
    table_ref, gain_one, wq, wk, wvt, wo, gain_two, w1, w2t, out_ref = refs[:10]
    refs = refs[10:]
    send_ref = refs.pop(0) if sends else None
    line_ref, x_ref, low_ref, high_ref = refs
    levels, rows, columns, _ = field.shape
    pairs = levels // WIN_P
    lat, lon, diag = [
        Packed(low_ref.at[n], high_ref.at[n], ref.shape[1]).load(ref) if ref is not None else None
        for n, ref in enumerate((lat_in, lon_in, diag_in))
    ]
    at = 0
    slot = 0
    start = HALF_LON + j * WIN_LON
    own = min(columns - start, WIN_LON)
    for p in range(pairs):
        for lev, level in enumerate(pair_levels(p, levels)):
            for row in range(i * WIN_LAT + HALF_LAT, (i + 1) * WIN_LAT + HALF_LAT):
                if row < rows:
                    line_ref[slot] = field[level, row].astype(F32)
                    x_ref[at : at + own, :] = line_ref[slot, start : start + own, :]
                    slot += 1
                    if own < WIN_LON:
                        late = lev * (rows - HALF_LAT) + row - HALF_LAT
                        x_ref[at + own : at + WIN_LON, :] = lon.get(p, late * HALF_LON, HALF_LON)
                else:
                    below = lev * HALF_LAT + row - rows
                    x_ref[at : at + own, :] = lat.get(p, below * (columns - HALF_LON) + j * WIN_LON, own)
                    if own < WIN_LON:
                        x_ref[at + own : at + WIN_LON, :] = diag.get(p, below * HALF_LON, HALF_LON)
                at += WIN_LON
    block_rows(
        x_ref, pairs, table_ref, 6, gain_one, wq[...], wk[...], wvt[...], wo, gain_two, w1, w2t, ((1,), (1,)), out_ref
    )
    if not sends:
        return
    send = Packed(low_ref.at[0], high_ref.at[0], send_ref.shape[1])
    for p in range(pairs):
        for lev in range(WIN_P):
            for row in range(HALF_LAT):
                at = (lev * HALF_LAT + row) * columns
                here = ((p * WIN_P + lev) * WIN_LAT + row) * WIN_LON
                send.put(p, at, first[here : here + WIN_LON, :])
                send.put(p, at + WIN_LON, out_ref[here : here + WIN_LON, :])
    send.store(send_ref)


def coarse_kernel(
    w00, w01, w10, w11, lat_in, lon_in, table_ref,
    merge_gain, merge_weight,
    gain_one, project, wo, gain_two, w1, w2,
    up_first, up_norm, up_second,
    stay_ref, to_lat_ref, to_lon_ref, to_diag_ref,
    low_ref, high_ref, grid_low, grid_high, quad_low, quad_high, parts_ref, x_ref, y_ref,
):
    heads = 12
    width = w00.shape[1]
    rows, columns = 2 * WIN_LAT, 2 * WIN_LON
    pairs = w00.shape[0] // WIN
    levels = pairs * WIN_P
    windows = ((w00, w01), (w10, w11))
    lat, lon = [Packed(low_ref.at[n], high_ref.at[n], ref.shape[1]).load(ref) for n, ref in enumerate((lat_in, lon_in))]

    def put(at, value):
        grid_low[at : at + value.shape[0], :] = value[:, :MAIN]
        grid_high[at : at + value.shape[0], : width - MAIN] = value[:, MAIN:]

    for p in range(pairs):
        for lev in range(WIN_P):
            for row in range(rows):
                at = ((p * WIN_P + lev) * rows + row) * PITCH
                if row + HALF_LAT < rows:
                    left, right = windows[(row + HALF_LAT) // WIN_LAT]
                    here = ((p * WIN_P + lev) * WIN_LAT + (row + HALF_LAT) % WIN_LAT) * WIN_LON
                    put(at + HALF_LON, left[here + HALF_LON : here + WIN_LON, :])
                    put(at + WIN_LON, right[here : here + WIN_LON, :])
                else:
                    below = lev * HALF_LAT + row + HALF_LAT - rows
                    put(at + HALF_LON, lat.get(p, below * columns + HALF_LON, columns - HALF_LON))
                put(at + columns, lon.get(p, (lev * rows + row) * HALF_LON, HALF_LON))
    for r in range(2):
        for t in range(2):
            n = 2 * r + t
            at = 0
            for level in range(levels):
                for a in range(rows // 2):
                    start = (level * rows + 2 * a + r) * PITCH + HALF_LON + t
                    parts_ref[n, at : at + WIN_LON, :MAIN] = grid_low[pl.ds(start, WIN_LON, stride=2), :]
                    parts_ref[n, at : at + WIN_LON, MAIN:] = grid_high[pl.ds(start, WIN_LON, stride=2), :]
                    at += WIN_LON
    parts = [parts_ref[n, :, :width] for n in range(4)]
    average = jnp.sum(parts[0] + parts[1] + parts[2] + parts[3], axis=-1, keepdims=True) * (1.0 / (4 * width))
    centred = [part - average for part in parts]
    squares = centred[0] * centred[0]
    for c in centred[1:]:
        squares += c * c
    scale = lax.rsqrt(jnp.sum(squares, axis=-1, keepdims=True) * (1.0 / (4 * width)) + EPS)
    total = None
    for n in range(4):
        gain = merge_gain[n * width : (n + 1) * width][None, :]
        normed = (centred[n] * scale * gain).astype(BF16)
        term = dot(normed, merge_weight[n * width : (n + 1) * width, :])
        total = term if total is None else total + term
    x_ref[...] = total.astype(BF16).astype(F32)
    double = 2 * width
    wvt = project[:, 2 * double :].astype(F32).T.astype(BF16)
    block_rows(
        x_ref, pairs, table_ref, heads, gain_one, project[:, :double], project[:, double : 2 * double], wvt,
        wo, gain_two, w1, w2, ((1,), (0,)), y_ref,
    )
    coarse = y_ref[...].astype(BF16)
    half = rows // 2
    for r in range(2):
        for t in range(2):
            n = 2 * r + t
            raised = dot(coarse, up_first[:, n * width : (n + 1) * width]).astype(BF16).astype(F32)
            normed = layer_norm(raised, up_norm[...][None, :]).astype(BF16)
            parts_ref[n, :, :width] = parts_ref[n, :, :width] + dot(normed, up_second[...])
            for level in range(levels):
                for a in range(half):
                    row = 2 * a + r
                    for side in range(2):
                        at = (level * half + a) * WIN_LON + side * HALF_LON
                        quad, p = 2 * (row // half) + side, level // WIN_P
                        start = (level % WIN_P * half + row % half) * WIN_LON + t
                        to = pl.ds(start, HALF_LON, stride=2)
                        quad_low[quad, p, to, :] = parts_ref[n, at : at + HALF_LON, :MAIN]
                        quad_high[quad, p, to, :] = parts_ref[n, at : at + HALF_LON, MAIN:]
    for quad, ref in enumerate((stay_ref, to_lon_ref, to_lat_ref, to_diag_ref)):
        Packed(quad_low.at[quad], quad_high.at[quad], WIN).store(ref)


def finish_kernel(
    upper_left, upper_right, lower_left, lower_right, out_hbm, low_ref, high_ref, line_low, line_high, out_ref, sems
):
    levels, rows, columns, width = out_ref.shape
    half = rows // 2
    packs = [
        Packed(low_ref.at[quad], high_ref.at[quad], WIN).load(ref)
        for quad, ref in enumerate((upper_left, upper_right, lower_left, lower_right))
    ]
    copies = []
    for p in range(levels // WIN_P):
        for lev, level in enumerate(pair_levels(p, levels)):
            for quad, pack in enumerate(packs):
                for row in range(half):
                    at = (level * rows + (quad // 2) * half + row) * columns + quad % 2 * WIN_LON
                    here = (lev * half + row) * WIN_LON
                    line_low[at : at + WIN_LON, :] = pack.low[p, here : here + WIN_LON, :]
                    line_high[at : at + WIN_LON, :] = pack.high[p, here : here + WIN_LON, :]
            for row in range(rows):
                at = (level * rows + row) * columns
                out_ref[level, row, :, :MAIN] = line_low[at : at + columns, :].astype(BF16)
                out_ref[level, row, :, MAIN:] = line_high[at : at + columns, : width - MAIN].astype(BF16)
            copies.append(pltpu.make_async_copy(out_ref.at[level], out_hbm.at[level], sems.at[level]))
            copies[-1].start()
    for copy in copies:
        copy.wait()


MIB = 1024 * 1024


def call(kernel, name, operands, outs, scratch, limit, scalars=0, us=1, results=pltpu.VMEM):
    vmem = pl.BlockSpec(memory_space=pltpu.VMEM)
    smem = pl.BlockSpec(memory_space=pltpu.SMEM)
    moved = sum(x.size * x.dtype.itemsize for x in operands) + sum(math.prod(s) * jnp.dtype(d).itemsize for s, d in outs)
    return pl.pallas_call(
        kernel,
        in_specs=[smem] * scalars + [vmem] * (len(operands) - scalars),
        out_specs=[pl.BlockSpec(memory_space=results)] * len(outs),
        out_shape=[jax.ShapeDtypeStruct(s, d) for s, d in outs],
        scratch_shapes=[pltpu.VMEM(s, F32) if isinstance(s, tuple) else s for s in scratch],
        compiler_params=pltpu.CompilerParams(vmem_limit_bytes=limit * MIB),
        cost_estimate=pl.CostEstimate(flops=us * 1000 * MIB, bytes_accessed=moved if us else 0, transcendentals=0),
        name=name,
    )(*operands)


def packed_shape(tokens, pairs):
    return (pairs * 3 // 2, packed_rows(tokens), MAIN)


def shift(array, lat_by, lon_by):
    lats, lons = lax.axis_size("lat"), lax.axis_size("lon")
    if lat_by and lon_by:
        pairs = [
            (((a + lat_by) % lats) * lons + (b + lon_by) % lons, a * lons + b)
            for a in range(lats)
            for b in range(lons)
        ]
        return lax.ppermute(array, ("lat", "lon"), pairs)
    if lat_by:
        return lax.ppermute(array, "lat", [((i + lat_by) % lats, i) for i in range(lats)])
    return lax.ppermute(array, "lon", [((i + lon_by) % lons, i) for i in range(lons)])


def body(
    field, a_norm_one, a_project, a_bias, a_output, a_norm_two, a_raise, a_lower,
    merge_norm_gain, merge_weight,
    b_norm_one, b_project, b_bias, b_output, b_norm_two, b_raise, b_lower,
    up_first, up_norm, up_second,
):
    levels, rows, columns, width = field.shape
    pairs = levels // WIN_P
    halo = packed_shape(WIN, pairs)
    staging = (pairs, WIN, MAIN)
    both = (2,) + staging
    tokens = pairs * WIN

    edge = (lax.axis_index("lat") == lax.axis_size("lat") - 1).astype(jnp.int32).reshape(1)
    lat_shape = packed_shape(WIN_P * HALF_LAT * (columns - HALF_LON), pairs)
    lon_shape = packed_shape(WIN_P * (rows - HALF_LAT) * HALF_LON, pairs)
    diag_shape = packed_shape(WIN_P * HALF_LAT * HALF_LON, pairs)
    lat, lon, diag = call(
        start_kernel, "start", [field], [(lat_shape, BF16), (lon_shape, BF16), (diag_shape, BF16)],
        [(levels * HALF_LAT, columns, width), (3,) + staging, (3,) + staging], 16, us=3,
    )
    lon = shift(lon, 0, 1)
    lat = shift(lat, 1, 0)
    diag = shift(diag, 1, 1)
    a_heads, b_heads = a_bias.shape[0], b_bias.shape[0]
    square = ((width, width), BF16)
    plain, late, wq, wk, wvt = call(
        fine_table_kernel, "fine_tables", [edge, a_bias, a_project],
        [((2, WIN, a_heads * WIN), F32)] * 2 + [square] * 3, [], 16, scalars=1, us=3,
    )
    weights = [a_norm_one, wq, wk, wvt, a_output, a_norm_two, a_raise, a_lower.T]
    scratch = [(levels * WIN_LAT, columns, width), (tokens, width), (3,) + staging, (3,) + staging]
    out = ((tokens, width), F32)

    def fine(i, j, halos, outs):
        def kernel(*refs):
            fine_kernel(i, j, *refs)

        operands = [field, *halos, late if i else plain, *weights]
        return call(kernel, f"fine_{i}{j}", operands, [out] + outs, scratch, 20, us=5)

    (w00,) = fine(0, 0, [], [])
    lon, lat, diag, w00 = lax.optimization_barrier((lon, lat, diag, w00))
    w01, lat_two = fine(0, 1, [lon, w00], [(halo, BF16)])
    lat_two = shift(lat_two, 1, 0)
    lat, w01 = lax.optimization_barrier((lat, w01))
    (w10,) = fine(1, 0, [lat], [])
    lat_two, w10 = lax.optimization_barrier((lat_two, w10))
    (lon_two,) = call(pack_second, "pack_second", [w00, w10, lat_two], [(halo, BF16)], [both, both], 16)
    lon_two, late_bias = lax.optimization_barrier((lon_two, b_bias))
    lon_two = shift(lon_two, 0, 1)
    (coarse_table,) = call(
        table_kernel, "coarse_table", [edge, late_bias], [((2, WIN, b_heads * WIN), F32)], [], 16, scalars=1, us=0
    )
    diag, coarse_table = lax.optimization_barrier((diag, coarse_table))
    (w11,) = fine(1, 1, [lat, lon, diag], [])

    quads = (4,) + staging
    lines = (levels * rows * PITCH, MAIN)
    stay, lat, lon, diag = call(
        coarse_kernel, "coarse",
        [
            w00, w01, w10, w11, lat_two, lon_two, coarse_table, merge_norm_gain, merge_weight,
            b_norm_one, b_project, b_output, b_norm_two, b_raise, b_lower, up_first, up_norm, up_second,
        ],
        [(halo, BF16)] * 4,
        [both, both, lines, lines, quads, quads, (4, tokens, 2 * MAIN), (tokens, 2 * width), (tokens, 2 * width)],
        32, us=12,
    )
    diag = shift(diag, -1, -1)
    lat = shift(lat, -1, 0)
    lon = shift(lon, 0, -1)
    lines = (levels * rows * columns, MAIN)
    (fine_out,) = call(
        finish_kernel, "finish", [diag, lat, lon, stay], [(field.shape, BF16)],
        [quads, quads, lines, lines, pltpu.VMEM(field.shape, BF16), pltpu.SemaphoreType.DMA((levels,))],
        24, results=pl.ANY,
    )
    return fine_out


def solution(mesh):
    in_specs = (P(None, "lat", "lon", None),) + (P(),) * 19
    out_specs = P(None, "lat", "lon", None)
    return jax.shard_map(body, mesh=mesh, in_specs=in_specs, out_specs=out_specs, check_vma=False)
```

```python
import math

import jax
import jax.numpy as jnp
from jax import lax
from jax.experimental import pallas as pl
from jax.experimental.pallas import tpu as pltpu
from jax.sharding import PartitionSpec as P

WIN_P = 2
WIN_LAT = 6
WIN_LON = 12
WIN = WIN_P * WIN_LAT * WIN_LON
HALF_LAT = WIN_LAT // 2
HALF_LON = WIN_LON // 2
HEAD = 32
MAIN = 128
REST = WIN - MAIN
EPS = 1e-05
LOG2E = math.log2(math.e)
EXCLUDED = -1e30
PITCH = 32

F32 = jnp.float32
BF16 = jnp.bfloat16


def dot(a, b, contract=((1,), (0,))):
    return lax.dot_general(a, b, (contract, ((), ())), preferred_element_type=F32)


def layer_norm(values, gain):
    average = jnp.mean(values, axis=-1, keepdims=True)
    centred = values - average
    variance = jnp.mean(centred * centred, axis=-1, keepdims=True)
    return centred * lax.rsqrt(variance + EPS) * gain


def gelu(x):
    return 0.5 * x * (1.0 + lax.erf(x * (1.0 / math.sqrt(2.0))))


def token_index(shape, heads):
    key = lax.broadcasted_iota(jnp.int32, shape, 0)
    column = lax.broadcasted_iota(jnp.int32, shape, 1)
    rest = column - heads * MAIN
    query = jnp.where(rest < 0, jnp.bitwise_and(column, MAIN - 1), MAIN + jnp.bitwise_and(rest, REST - 1))
    return key, query


def level_mask(heads):
    key, query = token_index((WIN, heads * WIN), heads)
    half = WIN // 2
    return jnp.where((key >= half) != (query >= half), EXCLUDED, 0.0)


def lat_mask(heads):
    key, query = token_index((WIN, heads * WIN), heads)
    half, quarter = WIN // 2, WIN // 4

    def late(t):
        return jnp.where(t >= half, t - half, t) >= quarter

    return jnp.where(late(key) != late(query), EXCLUDED, 0.0)


def attend(q, k, vt, table, heads, step, near):
    width = heads * HEAD
    lane = lax.broadcasted_iota(jnp.int32, (1, MAIN), 1) // HEAD
    zero = jnp.zeros((), BF16)
    pieces = []
    rests = []
    for start in range(0, width, MAIN):
        stop = min(start + MAIN, width)
        span = stop - start
        qs = q[:, start:stop]
        here = span // HEAD
        masked = [jnp.where(lane[:, :span] == h, qs, zero) for h in range(here)]
        rest = jnp.concatenate([m[MAIN:] for m in masked], axis=0)
        ks = k[:, start:stop]
        for h in range(0, here, step):
            main = jnp.concatenate([m[:MAIN] for m in masked[h : h + step]], axis=0)
            pieces.append(dot(ks, main, ((1,), (1,))))
        rests.append(dot(ks, rest, ((1,), (1,))))
    outs = []
    base = 0
    for piece in pieces:
        span = piece.shape[1]
        s = piece + table[:, base : base + span]
        s = s - jnp.max(s, axis=0, keepdims=True)
        e = jnp.exp2(s)
        inv = 1.0 / jnp.sum(e, axis=0, keepdims=True)
        p = e.astype(BF16)
        for h in range(0, span // MAIN, near):
            row = base // MAIN + h
            both = dot(vt[row * HEAD : (row + near) * HEAD], p[:, h * MAIN : (h + near) * MAIN])
            for n in range(near):
                cut = slice(n * MAIN, (n + 1) * MAIN)
                outs.append(both[n * HEAD : (n + 1) * HEAD, cut] * inv[:, (h + n) * MAIN : (h + n + 1) * MAIN])
        base += span
    main_out = jnp.concatenate(outs, axis=0)
    s = jnp.concatenate(rests, axis=1) + table[:, base:]
    s = s - jnp.max(s, axis=0, keepdims=True)
    e = jnp.exp2(s)
    inv = 1.0 / jnp.sum(e, axis=0, keepdims=True)
    full = dot(vt, e.astype(BF16)) * inv
    row = lax.broadcasted_iota(jnp.int32, full.shape, 0) // HEAD
    column = lax.broadcasted_iota(jnp.int32, full.shape, 1) // REST
    full = jnp.where(row == column, full, 0.0).astype(BF16)
    fold_row = lax.broadcasted_iota(jnp.int32, (heads * REST, REST), 0)
    fold_column = lax.broadcasted_iota(jnp.int32, (heads * REST, REST), 1)
    fold = jnp.where(jnp.bitwise_and(fold_row, REST - 1) == fold_column, 1.0, 0.0).astype(BF16)
    rest_out = dot(full, fold)
    return jnp.concatenate([main_out.astype(BF16), rest_out.astype(BF16)], axis=1)


def block_rows(x_ref, count, table_ref, heads, gain_one, wq, wk, wvt, wo, gain_two, w1, w2, w2_dims, out_ref):
    x = x_ref[...]
    xn = layer_norm(x, gain_one[...][None, :]).astype(BF16)
    q = (dot(xn, wq) * (LOG2E / math.sqrt(HEAD))).astype(BF16)
    k = dot(xn, wk).astype(BF16)
    mixed = []
    for w in range(count):
        rows = slice(w * WIN, (w + 1) * WIN)
        vt = dot(wvt, xn[rows], ((1,), (1,))).astype(BF16)
        table = table_ref.at[1 if w == count - 1 else 0]
        attended = attend(q[rows], k[rows], vt, table, heads, *((4, 2) if heads == 6 else (2, 1)))
        mixed.append(dot(attended, wo[...], ((0,), (0,))))
    half = count // 2
    for first in range(0, count, half):
        rows = slice(first * WIN, (first + half) * WIN)
        after = x_ref[rows, :] + jnp.concatenate(mixed[first : first + half], axis=0)
        after = after.astype(BF16).astype(F32)
        normed = layer_norm(after, gain_two[...][None, :]).astype(BF16)
        hidden = gelu(dot(normed, w1[...])).astype(BF16)
        out_ref[rows, :] = (after + dot(hidden, w2[...], w2_dims)).astype(BF16).astype(F32)


class Packed:
    def __init__(self, low_ref, high_ref, rows):
        self.low, self.high, self.rows = low_ref, high_ref, rows
        self.pairs = low_ref.shape[0]

    def put(self, p, at, value):
        n = value.shape[0]
        self.low[p, at : at + n, :] = value[:, :MAIN]
        self.high[p, at : at + n, : value.shape[1] - MAIN] = value[:, MAIN:]

    def get(self, p, at, n):
        return jnp.concatenate([self.low[p, at : at + n, :], self.high[p, at : at + n, : MAIN // 2]], axis=1)

    def store(self, out_ref):
        half = self.pairs // 2
        rows = slice(0, self.rows)
        for p in range(self.pairs):
            out_ref[p] = self.low[p, rows, :].astype(BF16)
        for p in range(half):
            sides = [self.high[p + s * half, rows, : MAIN // 2] for s in range(2)]
            out_ref[self.pairs + p] = jnp.concatenate(sides, axis=1).astype(BF16)

    def load(self, in_ref):
        half = self.pairs // 2
        rows = slice(0, self.rows)
        for p in range(self.pairs):
            self.low[p, rows, :] = in_ref[p].astype(F32)
        for p in range(half):
            both = in_ref[self.pairs + p].astype(F32)
            for s in range(2):
                self.high[p + s * half, rows, : MAIN // 2] = both[:, s * MAIN // 2 : (s + 1) * MAIN // 2]
        return self


def packed_rows(tokens):
    return -(-tokens // 16) * 16


def pair_levels(p, levels):
    return [(WIN_P * p + WIN_P // 2 + lev) % levels for lev in range(WIN_P)]


def start_kernel(field, lat_ref, lon_ref, diag_ref, line_ref, low_ref, high_ref):
    levels, rows, columns, _ = field.shape
    packs = [Packed(low_ref.at[n], high_ref.at[n], ref.shape[1]) for n, ref in enumerate((lat_ref, lon_ref, diag_ref))]
    lat, lon, diag = packs
    for p in range(levels // WIN_P):
        for lev, level in enumerate(pair_levels(p, levels)):
            for r in range(rows):
                line = field[level, r].astype(F32)
                if r < HALF_LAT:
                    slot = level * HALF_LAT + r
                    line_ref[slot] = line
                    diag.put(p, (lev * HALF_LAT + r) * HALF_LON, line[:HALF_LON])
                    span = columns - HALF_LON
                    lat.put(p, (lev * HALF_LAT + r) * span, line_ref[slot, HALF_LON:, :])
                else:
                    lon.put(p, (lev * (rows - HALF_LAT) + r - HALF_LAT) * HALF_LON, line[:HALF_LON])
    for pack, ref in zip(packs, (lat_ref, lon_ref, diag_ref)):
        pack.store(ref)


def pack_second(w00, w10, lat_in, out_ref, low_ref, high_ref):
    rows, columns = 2 * WIN_LAT, 2 * WIN_LON
    lat = Packed(low_ref.at[0], high_ref.at[0], lat_in.shape[1]).load(lat_in)
    send = Packed(low_ref.at[1], high_ref.at[1], out_ref.shape[1])
    for p in range(w00.shape[0] // WIN):
        for lev in range(WIN_P):
            for r in range(rows):
                row = r + HALF_LAT
                if row < rows:
                    source = (w00, w10)[row // WIN_LAT]
                    here = ((p * WIN_P + lev) * WIN_LAT + row % WIN_LAT) * WIN_LON
                    value = source[here : here + HALF_LON, :]
                else:
                    value = lat.get(p, (lev * HALF_LAT + row - rows) * columns, HALF_LON)
                send.put(p, (lev * rows + r) * HALF_LON, value)
    send.store(out_ref)


def table_kernel(edge_ref, bias, *outs):
    heads = bias.shape[0]
    out = outs[0]
    for h in range(heads):
        turned = (bias[h] * LOG2E).T
        out[0, :, h * MAIN : (h + 1) * MAIN] = turned[:, :MAIN]
        out[0, :, heads * MAIN + h * REST : heads * MAIN + (h + 1) * REST] = turned[:, MAIN:]
    level = level_mask(heads)
    late = lat_mask(heads) * edge_ref[0].astype(F32)
    outs[-1][0] = out[0] + late
    for ref in outs:
        ref[1] = ref[0] + level


def fine_table_kernel(edge_ref, bias, project, plain_ref, late_ref, wq_ref, wk_ref, wvt_ref):
    table_kernel(edge_ref, bias, plain_ref, late_ref)
    width = wq_ref.shape[0]
    wq_ref[...] = project[:, :width]
    wk_ref[...] = project[:, width : 2 * width]
    wvt_ref[...] = project[:, 2 * width :].astype(F32).T.astype(BF16)


def fine_kernel(i, j, *refs):
    refs = list(refs)
    field = refs.pop(0)
    lat_in = refs.pop(0) if i else None
    lon_in = refs.pop(0) if j else None
    diag_in = refs.pop(0) if i and j else None
    sends = j and not i
    first = refs.pop(0) if sends else None
    table_ref, gain_one, wq, wk, wvt, wo, gain_two, w1, w2t, out_ref = refs[:10]
    refs = refs[10:]
    send_ref = refs.pop(0) if sends else None
    line_ref, x_ref, low_ref, high_ref = refs
    levels, rows, columns, _ = field.shape
    pairs = levels // WIN_P
    lat, lon, diag = [
        Packed(low_ref.at[n], high_ref.at[n], ref.shape[1]).load(ref) if ref is not None else None
        for n, ref in enumerate((lat_in, lon_in, diag_in))
    ]
    at = 0
    slot = 0
    start = HALF_LON + j * WIN_LON
    own = min(columns - start, WIN_LON)
    for p in range(pairs):
        for lev, level in enumerate(pair_levels(p, levels)):
            for row in range(i * WIN_LAT + HALF_LAT, (i + 1) * WIN_LAT + HALF_LAT):
                if row < rows:
                    line_ref[slot] = field[level, row].astype(F32)
                    x_ref[at : at + own, :] = line_ref[slot, start : start + own, :]
                    slot += 1
                    if own < WIN_LON:
                        late = lev * (rows - HALF_LAT) + row - HALF_LAT
                        x_ref[at + own : at + WIN_LON, :] = lon.get(p, late * HALF_LON, HALF_LON)
                else:
                    below = lev * HALF_LAT + row - rows
                    x_ref[at : at + own, :] = lat.get(p, below * (columns - HALF_LON) + j * WIN_LON, own)
                    if own < WIN_LON:
                        x_ref[at + own : at + WIN_LON, :] = diag.get(p, below * HALF_LON, HALF_LON)
                at += WIN_LON
    block_rows(
        x_ref, pairs, table_ref, 6, gain_one, wq[...], wk[...], wvt[...], wo, gain_two, w1, w2t, ((1,), (1,)), out_ref
    )
    if not sends:
        return
    send = Packed(low_ref.at[0], high_ref.at[0], send_ref.shape[1])
    for p in range(pairs):
        for lev in range(WIN_P):
            for row in range(HALF_LAT):
                at = (lev * HALF_LAT + row) * columns
                here = ((p * WIN_P + lev) * WIN_LAT + row) * WIN_LON
                send.put(p, at, first[here : here + WIN_LON, :])
                send.put(p, at + WIN_LON, out_ref[here : here + WIN_LON, :])
    send.store(send_ref)


def coarse_kernel(
    w00, w01, w10, w11, lat_in, lon_in, table_ref,
    merge_gain, merge_weight,
    gain_one, project, wo, gain_two, w1, w2,
    up_first, up_norm, up_second,
    stay_ref, to_lat_ref, to_lon_ref, to_diag_ref,
    low_ref, high_ref, grid_low, grid_high, quad_low, quad_high, parts_ref, x_ref, y_ref,
):
    heads = 12
    width = w00.shape[1]
    rows, columns = 2 * WIN_LAT, 2 * WIN_LON
    pairs = w00.shape[0] // WIN
    levels = pairs * WIN_P
    windows = ((w00, w01), (w10, w11))
    lat, lon = [Packed(low_ref.at[n], high_ref.at[n], ref.shape[1]).load(ref) for n, ref in enumerate((lat_in, lon_in))]

    def put(at, value):
        grid_low[at : at + value.shape[0], :] = value[:, :MAIN]
        grid_high[at : at + value.shape[0], : width - MAIN] = value[:, MAIN:]

    for p in range(pairs):
        for lev in range(WIN_P):
            for row in range(rows):
                at = ((p * WIN_P + lev) * rows + row) * PITCH
                if row + HALF_LAT < rows:
                    left, right = windows[(row + HALF_LAT) // WIN_LAT]
                    here = ((p * WIN_P + lev) * WIN_LAT + (row + HALF_LAT) % WIN_LAT) * WIN_LON
                    put(at + HALF_LON, left[here + HALF_LON : here + WIN_LON, :])
                    put(at + WIN_LON, right[here : here + WIN_LON, :])
                else:
                    below = lev * HALF_LAT + row + HALF_LAT - rows
                    put(at + HALF_LON, lat.get(p, below * columns + HALF_LON, columns - HALF_LON))
                put(at + columns, lon.get(p, (lev * rows + row) * HALF_LON, HALF_LON))
    for r in range(2):
        for t in range(2):
            n = 2 * r + t
            at = 0
            for level in range(levels):
                for a in range(rows // 2):
                    start = (level * rows + 2 * a + r) * PITCH + HALF_LON + t
                    parts_ref[n, at : at + WIN_LON, :MAIN] = grid_low[pl.ds(start, WIN_LON, stride=2), :]
                    parts_ref[n, at : at + WIN_LON, MAIN:] = grid_high[pl.ds(start, WIN_LON, stride=2), :]
                    at += WIN_LON
    parts = [parts_ref[n, :, :width] for n in range(4)]
    average = jnp.sum(parts[0] + parts[1] + parts[2] + parts[3], axis=-1, keepdims=True) * (1.0 / (4 * width))
    centred = [part - average for part in parts]
    squares = centred[0] * centred[0]
    for c in centred[1:]:
        squares += c * c
    scale = lax.rsqrt(jnp.sum(squares, axis=-1, keepdims=True) * (1.0 / (4 * width)) + EPS)
    total = None
    for n in range(4):
        gain = merge_gain[n * width : (n + 1) * width][None, :]
        normed = (centred[n] * scale * gain).astype(BF16)
        term = dot(normed, merge_weight[n * width : (n + 1) * width, :])
        total = term if total is None else total + term
    x_ref[...] = total.astype(BF16).astype(F32)
    double = 2 * width
    wvt = project[:, 2 * double :].astype(F32).T.astype(BF16)
    block_rows(
        x_ref, pairs, table_ref, heads, gain_one, project[:, :double], project[:, double : 2 * double], wvt,
        wo, gain_two, w1, w2, ((1,), (0,)), y_ref,
    )
    coarse = y_ref[...].astype(BF16)
    half = rows // 2
    for r in range(2):
        for t in range(2):
            n = 2 * r + t
            raised = dot(coarse, up_first[:, n * width : (n + 1) * width]).astype(BF16).astype(F32)
            normed = layer_norm(raised, up_norm[...][None, :]).astype(BF16)
            parts_ref[n, :, :width] = parts_ref[n, :, :width] + dot(normed, up_second[...])
            for level in range(levels):
                for a in range(half):
                    row = 2 * a + r
                    for side in range(2):
                        at = (level * half + a) * WIN_LON + side * HALF_LON
                        quad, p = 2 * (row // half) + side, level // WIN_P
                        start = (level % WIN_P * half + row % half) * WIN_LON + t
                        to = pl.ds(start, HALF_LON, stride=2)
                        quad_low[quad, p, to, :] = parts_ref[n, at : at + HALF_LON, :MAIN]
                        quad_high[quad, p, to, :] = parts_ref[n, at : at + HALF_LON, MAIN:]
    for quad, ref in enumerate((stay_ref, to_lon_ref, to_lat_ref, to_diag_ref)):
        Packed(quad_low.at[quad], quad_high.at[quad], WIN).store(ref)


def finish_kernel(
    upper_left, upper_right, lower_left, lower_right, out_hbm, low_ref, high_ref, line_low, line_high, out_ref, sems
):
    levels, rows, columns, width = out_ref.shape
    half = rows // 2
    packs = [
        Packed(low_ref.at[quad], high_ref.at[quad], WIN).load(ref)
        for quad, ref in enumerate((upper_left, upper_right, lower_left, lower_right))
    ]
    copies = []
    for p in range(levels // WIN_P):
        for lev, level in enumerate(pair_levels(p, levels)):
            for quad, pack in enumerate(packs):
                for row in range(half):
                    at = (level * rows + (quad // 2) * half + row) * columns + quad % 2 * WIN_LON
                    here = (lev * half + row) * WIN_LON
                    line_low[at : at + WIN_LON, :] = pack.low[p, here : here + WIN_LON, :]
                    line_high[at : at + WIN_LON, :] = pack.high[p, here : here + WIN_LON, :]
            for row in range(rows):
                at = (level * rows + row) * columns
                out_ref[level, row, :, :MAIN] = line_low[at : at + columns, :].astype(BF16)
                out_ref[level, row, :, MAIN:] = line_high[at : at + columns, : width - MAIN].astype(BF16)
            copies.append(pltpu.make_async_copy(out_ref.at[level], out_hbm.at[level], sems.at[level]))
            copies[-1].start()
    for copy in copies:
        copy.wait()


MIB = 1024 * 1024


def call(kernel, name, operands, outs, scratch, limit, scalars=0, us=1, results=pltpu.VMEM):
    vmem = pl.BlockSpec(memory_space=pltpu.VMEM)
    smem = pl.BlockSpec(memory_space=pltpu.SMEM)
    moved = sum(x.size * x.dtype.itemsize for x in operands) + sum(math.prod(s) * jnp.dtype(d).itemsize for s, d in outs)
    return pl.pallas_call(
        kernel,
        in_specs=[smem] * scalars + [vmem] * (len(operands) - scalars),
        out_specs=[pl.BlockSpec(memory_space=results)] * len(outs),
        out_shape=[jax.ShapeDtypeStruct(s, d) for s, d in outs],
        scratch_shapes=[pltpu.VMEM(s, F32) if isinstance(s, tuple) else s for s in scratch],
        compiler_params=pltpu.CompilerParams(vmem_limit_bytes=limit * MIB),
        cost_estimate=pl.CostEstimate(flops=us * 1000 * MIB, bytes_accessed=moved if us else 0, transcendentals=0),
        name=name,
    )(*operands)


def packed_shape(tokens, pairs):
    return (pairs * 3 // 2, packed_rows(tokens), MAIN)


def shift(array, lat_by, lon_by):
    lats, lons = lax.axis_size("lat"), lax.axis_size("lon")
    if lat_by and lon_by:
        pairs = [
            (((a + lat_by) % lats) * lons + (b + lon_by) % lons, a * lons + b)
            for a in range(lats)
            for b in range(lons)
        ]
        return lax.ppermute(array, ("lat", "lon"), pairs)
    if lat_by:
        return lax.ppermute(array, "lat", [((i + lat_by) % lats, i) for i in range(lats)])
    return lax.ppermute(array, "lon", [((i + lon_by) % lons, i) for i in range(lons)])


def body(
    field, a_norm_one, a_project, a_bias, a_output, a_norm_two, a_raise, a_lower,
    merge_norm_gain, merge_weight,
    b_norm_one, b_project, b_bias, b_output, b_norm_two, b_raise, b_lower,
    up_first, up_norm, up_second,
):
    levels, rows, columns, width = field.shape
    pairs = levels // WIN_P
    halo = packed_shape(WIN, pairs)
    staging = (pairs, WIN, MAIN)
    both = (2,) + staging
    tokens = pairs * WIN

    edge = (lax.axis_index("lat") == lax.axis_size("lat") - 1).astype(jnp.int32).reshape(1)
    lat_shape = packed_shape(WIN_P * HALF_LAT * (columns - HALF_LON), pairs)
    lon_shape = packed_shape(WIN_P * (rows - HALF_LAT) * HALF_LON, pairs)
    diag_shape = packed_shape(WIN_P * HALF_LAT * HALF_LON, pairs)
    lat, lon, diag = call(
        start_kernel, "start", [field], [(lat_shape, BF16), (lon_shape, BF16), (diag_shape, BF16)],
        [(levels * HALF_LAT, columns, width), (3,) + staging, (3,) + staging], 16, us=3,
    )
    lon = shift(lon, 0, 1)
    lat = shift(lat, 1, 0)
    diag = shift(diag, 1, 1)
    a_heads, b_heads = a_bias.shape[0], b_bias.shape[0]
    square = ((width, width), BF16)
    plain, late, wq, wk, wvt = call(
        fine_table_kernel, "fine_tables", [edge, a_bias, a_project],
        [((2, WIN, a_heads * WIN), F32)] * 2 + [square] * 3, [], 16, scalars=1, us=3,
    )
    weights = [a_norm_one, wq, wk, wvt, a_output, a_norm_two, a_raise, a_lower.T]
    scratch = [(levels * WIN_LAT, columns, width), (tokens, width), (3,) + staging, (3,) + staging]
    out = ((tokens, width), F32)

    def fine(i, j, halos, outs):
        def kernel(*refs):
            fine_kernel(i, j, *refs)

        operands = [field, *halos, late if i else plain, *weights]
        return call(kernel, f"fine_{i}{j}", operands, [out] + outs, scratch, 20, us=5)

    (w00,) = fine(0, 0, [], [])
    lon, diag, w00 = lax.optimization_barrier((lon, diag, w00))
    w01, lat_two = fine(0, 1, [lon, w00], [(halo, BF16)])
    lat_two = shift(lat_two, 1, 0)
    lat, w01 = lax.optimization_barrier((lat, w01))
    (w10,) = fine(1, 0, [lat], [])
    lat_two, w10 = lax.optimization_barrier((lat_two, w10))
    (lon_two,) = call(pack_second, "pack_second", [w00, w10, lat_two], [(halo, BF16)], [both, both], 16)
    lon_two, late_bias = lax.optimization_barrier((lon_two, b_bias))
    lon_two = shift(lon_two, 0, 1)
    (coarse_table,) = call(
        table_kernel, "coarse_table", [edge, late_bias], [((2, WIN, b_heads * WIN), F32)], [], 16, scalars=1, us=0
    )
    diag, coarse_table = lax.optimization_barrier((diag, coarse_table))
    (w11,) = fine(1, 1, [lat, lon, diag], [])

    quads = (4,) + staging
    lines = (levels * rows * PITCH, MAIN)
    stay, lat, lon, diag = call(
        coarse_kernel, "coarse",
        [
            w00, w01, w10, w11, lat_two, lon_two, coarse_table, merge_norm_gain, merge_weight,
            b_norm_one, b_project, b_output, b_norm_two, b_raise, b_lower, up_first, up_norm, up_second,
        ],
        [(halo, BF16)] * 4,
        [both, both, lines, lines, quads, quads, (4, tokens, 2 * MAIN), (tokens, 2 * width), (tokens, 2 * width)],
        32, us=12,
    )
    diag = shift(diag, -1, -1)
    lat = shift(lat, -1, 0)
    lon = shift(lon, 0, -1)
    lines = (levels * rows * columns, MAIN)
    (fine_out,) = call(
        finish_kernel, "finish", [diag, lat, lon, stay], [(field.shape, BF16)],
        [quads, quads, lines, lines, pltpu.VMEM(field.shape, BF16), pltpu.SemaphoreType.DMA((levels,))],
        24, results=pl.ANY,
    )
    return fine_out


def solution(mesh):
    in_specs = (P(None, "lat", "lon", None),) + (P(),) * 19
    out_specs = P(None, "lat", "lon", None)
    return jax.shard_map(body, mesh=mesh, in_specs=in_specs, out_specs=out_specs, check_vma=False)
```
